32 devices in a mesh: dp: 8 (over z, x), row: 2 (over y), col: 2 (over core).
Axes of the slice: x: 2, y: 2, z: 4, core: 2. Of those that a mesh axis runs over, the one named last changes fastest.
Arguments:
- tokens: bfloat16 [32768, 768], P(('dp', 'col'), 'row'), may hold values from -6 to 6
- condition: bfloat16 [128, 768], P('dp', 'col'), may hold values from -6 to 6
- adaptive: bfloat16 [6, 768, 768], P(None, 'col', 'row'), may hold values from -0.21875 to 0.21875
- adabias: bfloat16 [6, 768], P(None, 'row'), may hold values from -3 to 3
- attend: bfloat16 [3, 768, 768], P(None, 'row', 'col'), may hold values from -0.21875 to 0.21875
- attbias: bfloat16 [2, 768], P(None, 'col'), may hold values from -3 to 3
- outproj: bfloat16 [768, 768], P('col', 'row'), may hold values from -1.25 to 1.25
- outbias: bfloat16 [768], P('row'), may hold values from -3 to 3
- expand: bfloat16 [768, 3072], P('row', 'col'), may hold values from -0.21875 to 0.21875
- expbias: bfloat16 [3072], P('col'), may hold values from -3 to 3
- shrink: bfloat16 [3072, 768], P('col', 'row'), may hold values from -0.109375 to 0.109375
- shrbias: bfloat16 [768], P('row'), may hold values from -3 to 3
- cotangent: bfloat16 [32768, 768], P(('dp', 'col'), 'row'), may hold values from -6 to 6
Outputs:
- result: bfloat16 [32768, 768], P(('dp', 'col'), 'row')
- input_gradient: bfloat16 [32768, 768], P(('dp', 'col'), 'row')
- condition_gradient: bfloat16 [128, 768], P('dp', 'col')
- adaptive_gradient: float32 [6, 768, 768], P(None, 'col', 'row')
- adabias_gradient: float32 [6, 768], P(None, 'row')
- attend_gradient: float32 [3, 768, 768], P(None, 'row', 'col')
- attbias_gradient: float32 [2, 768], P(None, 'col')
- outproj_gradient: float32 [768, 768], P('col', 'row')
- outbias_gradient: float32 [768], P('row')
- expand_gradient: float32 [768, 3072], P('row', 'col')
- expbias_gradient: float32 [3072], P('col')
- shrink_gradient: float32 [3072, 768], P('col', 'row')
- shrbias_gradient: float32 [768], P('row')
The draws below stay inside these ranges and needn't reach their ends.
All inputs are finite; a program needn't handle non-finite values.
Results may differ from the reference program's by a relative error of at most 0.01575.
The reference program's roundings to bfloat16 on the way count: a program that leaves them out, or rounds other values in their place, can miss the bound.
Values may be sent and summed in bfloat16 or wider, within the bound.
No kernel may reach another device: no remote copies, remote signals or barrier semaphores. Data moves between devices by JAX's collectives and lax.ppermute only.
A program may use at most 256 MiB of HBM per device.

```python
import jax
import jax.numpy as jnp
from jax import lax

D = 768
HEADS = 12
FF = 3072
SEQ = 256
LAT_GRP = 16
HEAD_DIM = 64
LAT = 128
TOKENS = 32768


def block_levels(key, extent, cuts, low, largest):
    factor_of = 1.0
    for position, shards_of in cuts:
        draws = jax.random.uniform(jax.random.fold_in(jax.random.fold_in(key, 6), position), (shards_of,), jnp.float32, low / len(cuts), largest / len(cuts))
        factor_of = factor_of * jnp.repeat(jnp.exp(draws), extent[position] // shards_of).reshape((-1,) + (1,) * (len(extent) - 1 - position))
    return factor_of


def noise(key, extent, deviation, reach, cuts=(), kind=jnp.bfloat16):
    values = jax.random.normal(key, extent, jnp.float32) * deviation
    if len(cuts) > 0:
        values = block_levels(key, extent, cuts, -0.22, 0.18) * values
    return jnp.clip(values, min=-reach, max=reach).astype(kind)


def setup_inputs(seed: int = 0) -> dict:
    key_of = jax.random.split(jax.random.key(seed), 14)
    tokens = noise(key_of[0], (TOKENS, D), 1.0, 6.0, ((0, 16), (1, 2)))
    condition = noise(key_of[1], (LAT, D), 1.0, 6.0, ((0, 8), (1, 2)))
    adaptive = noise(key_of[2], (6, D, D), D ** -0.5, 0.21875, ((1, 2), (2, 2)))
    adabias = noise(key_of[3], (6, D), 0.5, 3.0, ((1, 2),))
    attend = noise(key_of[4], (3, D, D), D ** -0.5, 0.21875, ((1, 2), (2, 2)))
    attbias = noise(key_of[5], (2, D), 0.5, 3.0, ((1, 2),))
    outproj = noise(key_of[6], (D, D), (D // 32) ** -0.5, 1.25, ((0, 2), (1, 2)))
    outbias = noise(key_of[7], (D,), 0.5, 3.0, ((0, 2),))
    expand = noise(key_of[8], (D, FF), D ** -0.5, 0.21875, ((0, 2), (1, 2)))
    expbias = noise(key_of[9], (FF,), 0.5, 3.0, ((0, 2),))
    shrink = noise(key_of[10], (FF, D), FF ** -0.5, 0.109375, ((0, 2), (1, 2)))
    shrbias = noise(key_of[11], (D,), 0.5, 3.0, ((0, 2),))
    cotangent = noise(key_of[12], (TOKENS, D), 1.0, 6.0, ((0, 16), (1, 2)))
    return dict(tokens=tokens, condition=condition, adaptive=adaptive, adabias=adabias, attend=attend, attbias=attbias, outproj=outproj, outbias=outbias, expand=expand, expbias=expbias, shrink=shrink, shrbias=shrbias, cotangent=cotangent)


EPS = 1e-06
HIGH = lax.Precision.HIGHEST

@jax.custom_vjp
def low(v):
    return lax.optimization_barrier(v.astype(jnp.bfloat16)).astype(jnp.float32)

@jax.custom_vjp
def low_back(v):
    return v

def low_keep(v):
    return (low(v), None)

def low_pass(kept, grad):
    return (grad,)

def back_keep(v):
    return (v, None)

def back_low(kept, grad):
    return (low(grad),)
low.defvjp(low_keep, low_pass)
low_back.defvjp(back_keep, back_low)

def normed(values):
    center = lax.optimization_barrier(jnp.mean(values, axis=-1, keepdims=True))
    spread = lax.optimization_barrier(jnp.mean(values * values, axis=-1, keepdims=True)) - center * center
    return (values - center) * lax.rsqrt(spread + EPS)

def block(token_block, condition_block, parameters):
    adaptive, adabias, attend, attbias, outproj, outbias, expand, expbias, shrink, shrbias = parameters
    latents = condition_block.shape[0]
    act_cond = low(jax.nn.silu(condition_block))
    modulation = low_back(jnp.einsum('ld,kde->lke', act_cond, adaptive, precision=HIGH) + adabias)
    modulation = jnp.repeat(modulation, SEQ, axis=0)
    shift_one, scale_one, gate_one, shift_two, scale_two, gate_two = [modulation[:, number] for number in range(6)]
    normal_one = low(normed(token_block) * (1.0 + scale_one) + shift_one)
    triple = jnp.einsum('td,kde->tke', normal_one, attend, precision=HIGH)
    queries = low_back(low(triple[:, 0] + attbias[0]))
    key_rows = low_back(low(triple[:, 1]))
    value_rows = low_back(low(triple[:, 2] + attbias[1]))
    grid_shape = (latents, SEQ, HEADS, HEAD_DIM)
    scores = jnp.einsum('lqhe,lkhe->lhqk', queries.reshape(grid_shape), key_rows.reshape(grid_shape), precision=HIGH)
    scores = low_back(scores * HEAD_DIM ** (-0.5))
    weights = low(jax.nn.softmax(scores, axis=-1))
    attended = jnp.einsum('lhqk,lkhe->lqhe', weights, value_rows.reshape(grid_shape), precision=HIGH)
    attended = low_back(low(attended.reshape(latents * SEQ, D)))
    branch_one = low_back(jnp.dot(attended, outproj, precision=HIGH) + outbias)
    middle = token_block + gate_one * branch_one
    normal_two = low(normed(middle) * (1.0 + scale_two) + shift_two)
    hidden = low_back(jnp.dot(normal_two, expand, precision=HIGH) + expbias)
    active = low(jax.nn.gelu(hidden, approximate=True))
    branch_two = low_back(jnp.dot(active, shrink, precision=HIGH) + shrbias)
    return middle + gate_two * branch_two

def reference(tokens, condition, adaptive, adabias, attend, attbias, outproj, outbias, expand, expbias, shrink, shrbias, cotangent):
    parameters = tuple((array_in.astype(jnp.float32) for array_in in (adaptive, adabias, attend, attbias, outproj, outbias, expand, expbias, shrink, shrbias)))
    blocks = LAT // LAT_GRP
    token_blocks = tokens.astype(jnp.float32).reshape(blocks, LAT_GRP * SEQ, D)
    condition_blocks = condition.astype(jnp.float32).reshape(blocks, LAT_GRP, D)

    def forward(token_blocks, condition_blocks, parameters):
        stepper = jax.checkpoint(block)
        return lax.map(lambda couple: stepper(couple[0], couple[1], parameters), (token_blocks, condition_blocks))
    outputs, pullback = jax.vjp(forward, token_blocks, condition_blocks, parameters)
    token_grads, condition_grads, weight_grads = pullback(cotangent.astype(jnp.float32).reshape(outputs.shape))
    return (outputs.reshape(TOKENS, D).astype(jnp.bfloat16), token_grads.reshape(TOKENS, D).astype(jnp.bfloat16), condition_grads.reshape(LAT, D).astype(jnp.bfloat16), weight_grads[0], weight_grads[1], weight_grads[2], weight_grads[3], weight_grads[4], weight_grads[5], weight_grads[6], weight_grads[7], weight_grads[8], weight_grads[9])
```

```python
import functools

import jax
import jax.numpy as jnp
from jax import lax
from jax.experimental import pallas as pl
from jax.experimental.pallas import tpu as pltpu
from jax.sharding import PartitionSpec as P

D = 768
HALF = D // 2
FF = 3072
SEQ = 256
HEAD_DIM = 64
PAIR = 2 * HEAD_DIM
SIDE = 3 * HALF
EPS = 1e-06
F32 = jnp.float32
B16 = jnp.bfloat16
SWAP = ((0, 1), (1, 0))
SCALE = HEAD_DIM ** (-0.5)
ROOT = (2.0 / 3.141592653589793) ** 0.5
CUBE = 0.044715
PER_TILE = 2
VMEM_BYTES = 60 * 1024 * 1024


def dot(left, right):
    return jnp.dot(left, right, preferred_element_type=F32)


def dot_nt(left, right):
    return lax.dot_general(left, right, (((1,), (1,)), ((), ())), preferred_element_type=F32)


def dot_tn(left, right):
    return lax.dot_general(left, right, (((0,), (0,)), ((), ())), preferred_element_type=F32)


def normalize(values):
    center = jnp.mean(values, axis=1, keepdims=True)
    spread = jnp.mean(values * values, axis=1, keepdims=True) - center * center
    inverse = lax.rsqrt(spread + EPS)
    return (values - center) * inverse, inverse


def norm_grad(upstream, normal, inverse):
    first_mean = jnp.mean(upstream, axis=1, keepdims=True)
    second_mean = jnp.mean(upstream * normal, axis=1, keepdims=True)
    return inverse * (upstream - first_mean - normal * second_mean)


def both(own_ref, oth_ref):
    return jnp.concatenate([own_ref[...], oth_ref[...]], axis=1).astype(F32)


def spread_rows(mod_ref, number):
    rows = [
        jnp.broadcast_to(mod_ref[latent, number : number + 1, :], (SEQ, D))
        for latent in range(mod_ref.shape[0])
    ]
    return rows[0] if len(rows) == 1 else jnp.concatenate(rows, axis=0)


def store_sums(out_ref, number, values):
    for latent in range(out_ref.shape[0]):
        out_ref[latent, number : number + 1, :] = jnp.sum(
            values[latent * SEQ : (latent + 1) * SEQ], axis=0, keepdims=True
        )


def attend_copies(pieces, weight, sem):
    copies = []
    for number, piece in enumerate(pieces):
        row, col = number % 2, number // 2
        for kind in range(3):
            copies.append(
                pltpu.make_async_copy(
                    piece.at[kind],
                    weight.at[pl.ds(row * HALF, HALF), pl.ds(col * SIDE + kind * HALF, HALF)],
                    sem.at[len(copies)],
                )
            )
    return copies


def grid_copies(pieces, weight, sem, first_is_row):
    copies = []
    for number, piece in enumerate(pieces):
        row, col = number % 2, number // 2
        across, down = piece.shape[1], piece.shape[0]
        top, left = (row, col) if first_is_row else (col, row)
        copies.append(
            pltpu.make_async_copy(
                piece,
                weight.at[pl.ds(top * down, down), pl.ds(left * across, across)],
                sem.at[number],
            )
        )
    return copies


def forward_kernel(
    tok_own, tok_oth, mod, bias, w0, w1, w2, w3, first_ref, qkv_ref, att_ref, weight, sem
):
    @pl.when(pl.program_id(0) == 0)
    def _():
        copies = attend_copies((w0, w1, w2, w3), weight, sem)
        for copy in copies:
            copy.start()
        for copy in copies:
            copy.wait()

    normal, _ = normalize(both(tok_own, tok_oth))
    first = (normal * (1.0 + spread_rows(mod, 1)) + spread_rows(mod, 0)).astype(B16)
    first_ref[...] = first
    qkv_ref[...] = (dot(first, weight[...]) + bias[...]).astype(B16)
    low = lax.broadcasted_iota(jnp.int32, (SEQ, PAIR), 1) < HEAD_DIM
    for col in range(2):
        for pair in range(HALF // PAIR):
            base = col * SIDE + pair * PAIR
            q_part = qkv_ref[:, base : base + PAIR] * SCALE
            k_part = qkv_ref[:, base + HALF : base + HALF + PAIR]
            v_part = qkv_ref[:, base + D : base + D + PAIR]
            outs = []
            for keep in (low, jnp.logical_not(low)):
                scores = dot_nt(jnp.where(keep, q_part, 0).astype(B16), k_part)
                exponent = jnp.exp(scores - jnp.max(scores, axis=1, keepdims=True))
                probs = exponent * (1.0 / jnp.sum(exponent, axis=1, keepdims=True))
                outs.append(dot(probs.astype(B16), v_part))
            at = col * HALF + pair * PAIR
            att_ref[:, at : at + PAIR] = jnp.where(low, outs[0], outs[1]).astype(B16)


def middle_kernel(
    tok_own, tok_oth, cot_own, cot_oth, att, mod, outbias, expbias, shrbias,
    o0, o1, o2, o3, x0, x1, x2, x3, s0, s1, s2, s3,
    res_own, res_oth, second_ref, act_own, act_oth, dh_own, dh_oth, e_one_ref, e_two_ref,
    d_mid_ref, d_att_ref, mod_ref, sum_ref,
    w_out, w_exp, w_shr, sem_out, sem_exp, sem_shr,
):
    @pl.when(pl.program_id(0) == 0)
    def _():
        copies = (
            grid_copies((o0, o1, o2, o3), w_out, sem_out, False)
            + grid_copies((x0, x1, x2, x3), w_exp, sem_exp, True)
            + grid_copies((s0, s1, s2, s3), w_shr, sem_shr, False)
        )
        for copy in copies:
            copy.start()
        for copy in copies:
            copy.wait()

    branch_one = dot(att[...], w_out[...]) + outbias[...]
    middle = both(tok_own, tok_oth) + spread_rows(mod, 2) * branch_one
    normal, inverse = normalize(middle)
    second = (normal * (1.0 + spread_rows(mod, 4)) + spread_rows(mod, 3)).astype(B16)
    second_ref[...] = second
    upstream = both(cot_own, cot_oth)
    e_two = (spread_rows(mod, 5) * upstream).astype(B16)
    e_two_ref[...] = e_two
    branch_two = shrbias[...]
    d_second = 0.0
    for part in range(FF // D):
        at = part * D
        hidden = dot(second, w_exp[:, at : at + D]) + expbias[:, at : at + D]
        square = hidden * hidden
        bend = jnp.tanh(hidden * (ROOT + (ROOT * CUBE) * square))
        share = 0.5 + 0.5 * bend
        active = (hidden * share).astype(B16)
        slope = share + (0.5 * hidden) * (1.0 - bend * bend) * (ROOT + (3.0 * ROOT * CUBE) * square)
        branch_two = branch_two + dot(active, w_shr[at : at + D, :])
        d_hidden = (dot_nt(e_two, w_shr[at : at + D, :]) * slope).astype(B16)
        d_second = d_second + dot_nt(d_hidden, w_exp[:, at : at + D])
        act_ref, dh_ref = (act_own, dh_own) if 2 * at < FF else (act_oth, dh_oth)
        into = at % (FF // 2)
        act_ref[:, into : into + D] = active
        dh_ref[:, into : into + D] = d_hidden
        sum_ref[0, :, 2 * D + at : 2 * D + at + D] = jnp.sum(
            d_hidden.astype(F32), axis=0, keepdims=True
        )
    result = (middle + spread_rows(mod, 5) * branch_two).astype(B16)
    res_own[...] = result[:, :HALF]
    res_oth[...] = result[:, HALF:]
    store_sums(mod_ref, 3, upstream * branch_two)
    store_sums(mod_ref, 1, d_second)
    store_sums(mod_ref, 2, d_second * normal)
    d_middle = upstream + norm_grad(d_second * (1.0 + spread_rows(mod, 4)), normal, inverse)
    d_mid_ref[...] = d_middle
    store_sums(mod_ref, 0, d_middle * branch_one)
    e_one = (spread_rows(mod, 2) * d_middle).astype(B16)
    e_one_ref[...] = e_one
    d_att_ref[...] = dot_nt(e_one, w_out[...]).astype(B16)
    sum_ref[0, :, :D] = jnp.sum(e_one.astype(F32), axis=0, keepdims=True)
    sum_ref[0, :, D : 2 * D] = jnp.sum(e_two.astype(F32), axis=0, keepdims=True)


def backward_kernel(
    tok_own, tok_oth, mod, qkv, d_att, d_mid, w0, w1, w2, w3,
    dqkv_own, dqkv_oth, grad_own, grad_oth, mod_ref, sum_ref, weight, sem,
):
    @pl.when(pl.program_id(0) == 0)
    def _():
        copies = attend_copies((w0, w1, w2, w3), weight, sem)
        for copy in copies:
            copy.start()
        for copy in copies:
            copy.wait()

    low = lax.broadcasted_iota(jnp.int32, (SEQ, PAIR), 1) < HEAD_DIM
    for col in range(2):
        out_ref = (dqkv_own, dqkv_oth)[col]
        for pair in range(HALF // PAIR):
            base = col * SIDE + pair * PAIR
            q_part = qkv[:, base : base + PAIR]
            k_part = qkv[:, base + HALF : base + HALF + PAIR]
            v_part = qkv[:, base + D : base + D + PAIR]
            d_part = d_att[:, col * HALF + pair * PAIR : col * HALF + (pair + 1) * PAIR]
            queries, keys, values = [], [], []
            for keep in (low, jnp.logical_not(low)):
                scores = dot_nt(jnp.where(keep, k_part * SCALE, 0).astype(B16), q_part)
                exponent = jnp.exp(scores - jnp.max(scores, axis=0, keepdims=True))
                probs = exponent * (1.0 / jnp.sum(exponent, axis=0, keepdims=True))
                d_probs = dot_nt(jnp.where(keep, v_part, 0).astype(B16), d_part)
                weighted = probs * d_probs
                d_scores = (weighted - probs * jnp.sum(weighted, axis=0, keepdims=True)).astype(B16)
                values.append(dot(probs.astype(B16), d_part))
                keys.append(dot(d_scores, q_part))
                queries.append(dot_tn(d_scores, k_part))
            for kind, (first, then, factor) in enumerate(
                ((*queries, SCALE), (*keys, SCALE), (*values, 1.0))
            ):
                at = kind * HALF + pair * PAIR
                piece = (jnp.where(low, first, then) * factor).astype(B16)
                out_ref[:, at : at + PAIR] = piece
                sum_ref[0, :, col * SIDE + at : col * SIDE + at + PAIR] = jnp.sum(
                    piece.astype(F32), axis=0, keepdims=True
                )
    d_first = dot_nt(dqkv_own[...], weight[:, :SIDE]) + dot_nt(dqkv_oth[...], weight[:, SIDE:])
    normal, inverse = normalize(both(tok_own, tok_oth))
    store_sums(mod_ref, 0, d_first)
    store_sums(mod_ref, 1, d_first * normal)
    grad = (
        d_mid[...] + norm_grad(d_first * (1.0 + spread_rows(mod, 1)), normal, inverse)
    ).astype(B16)
    grad_own[...] = grad[:, :HALF]
    grad_oth[...] = grad[:, HALF:]


def tiles(rows, width):
    return pl.BlockSpec((rows, width), lambda step: (step, 0))


def stacked(count, rows, width):
    return pl.BlockSpec((count, rows, width), lambda step: (step, 0, 0))


def fixed(width):
    return pl.BlockSpec((1, width), lambda step: (0, 0))


def anywhere(count):
    return [pl.BlockSpec(memory_space=pl.ANY)] * count


def params():
    return pltpu.CompilerParams(
        vmem_limit_bytes=VMEM_BYTES, dimension_semantics=("arbitrary",)
    )


def call_forward(tok_own, tok_oth, modulation, bias, pieces):
    count = tok_own.shape[0]
    latents = count // SEQ
    return pl.pallas_call(
        forward_kernel,
        grid=(latents,),
        in_specs=[tiles(SEQ, HALF)] * 2 + [stacked(1, 6, D), fixed(2 * SIDE)] + anywhere(4),
        out_specs=[tiles(SEQ, D), tiles(SEQ, 2 * SIDE), tiles(SEQ, D)],
        out_shape=[
            jax.ShapeDtypeStruct((count, D), B16),
            jax.ShapeDtypeStruct((count, 2 * SIDE), B16),
            jax.ShapeDtypeStruct((count, D), B16),
        ],
        scratch_shapes=[pltpu.VMEM((D, 2 * SIDE), B16), pltpu.SemaphoreType.DMA((12,))],
        compiler_params=params(),
        cost_estimate=pl.CostEstimate(
            flops=14 * 10**9, bytes_accessed=16 * 10**6, transcendentals=count * SEQ * 12
        ),
        name="forward",
    )(tok_own, tok_oth, modulation, bias, *pieces)


def call_middle(tok, cot, att, modulation, biases, out_pieces, exp_pieces, shr_pieces):
    count = att.shape[0]
    latents = count // SEQ
    per_tile = PER_TILE if latents % PER_TILE == 0 else 1
    rows = per_tile * SEQ
    steps = latents // per_tile
    halves = [tiles(rows, HALF)] * 2

    def shape(width, kind=B16):
        return jax.ShapeDtypeStruct((count, width), kind)

    return pl.pallas_call(
        middle_kernel,
        grid=(steps,),
        in_specs=halves
        + halves
        + [tiles(rows, D), stacked(per_tile, 6, D), fixed(D), fixed(FF), fixed(D)]
        + anywhere(12),
        out_specs=halves
        + [tiles(rows, D)]
        + [tiles(rows, FF // 2)] * 4
        + [tiles(rows, D)] * 4
        + [stacked(per_tile, 4, D), stacked(1, 1, 2 * D + FF)],
        out_shape=[shape(HALF), shape(HALF), shape(D)]
        + [shape(FF // 2)] * 4
        + [shape(D), shape(D), shape(D, F32), shape(D)]
        + [
            jax.ShapeDtypeStruct((latents, 4, D), F32),
            jax.ShapeDtypeStruct((steps, 1, 2 * D + FF), F32),
        ],
        scratch_shapes=[
            pltpu.VMEM((D, D), B16),
            pltpu.VMEM((D, FF), B16),
            pltpu.VMEM((FF, D), B16),
            pltpu.SemaphoreType.DMA((4,)),
            pltpu.SemaphoreType.DMA((4,)),
            pltpu.SemaphoreType.DMA((4,)),
        ],
        compiler_params=params(),
        cost_estimate=pl.CostEstimate(
            flops=30 * 10**9, bytes_accessed=50 * 10**6, transcendentals=count * FF
        ),
        name="middle",
    )(*tok, *cot, att, modulation, *biases, *out_pieces, *exp_pieces, *shr_pieces)


def call_backward(tok, modulation, qkv, d_att, d_mid, pieces):
    count = d_att.shape[0]
    latents = count // SEQ
    return pl.pallas_call(
        backward_kernel,
        grid=(latents,),
        in_specs=[tiles(SEQ, HALF)] * 2
        + [stacked(1, 6, D), tiles(SEQ, 2 * SIDE), tiles(SEQ, D), tiles(SEQ, D)]
        + anywhere(4),
        out_specs=[tiles(SEQ, SIDE)] * 2
        + [tiles(SEQ, HALF)] * 2
        + [stacked(1, 2, D), stacked(1, 1, 2 * SIDE)],
        out_shape=[jax.ShapeDtypeStruct((count, SIDE), B16)] * 2
        + [jax.ShapeDtypeStruct((count, HALF), B16)] * 2
        + [
            jax.ShapeDtypeStruct((latents, 2, D), F32),
            jax.ShapeDtypeStruct((latents, 1, 2 * SIDE), F32),
        ],
        scratch_shapes=[pltpu.VMEM((D, 2 * SIDE), B16), pltpu.SemaphoreType.DMA((12,))],
        compiler_params=params(),
        cost_estimate=pl.CostEstimate(
            flops=25 * 10**9, bytes_accessed=20 * 10**6, transcendentals=count * SEQ * 12
        ),
        name="backward",
    )(*tok, modulation, qkv, d_att, d_mid, *pieces)


def swap_row(values):
    return lax.ppermute(values, "row", SWAP)


def swap_col(values):
    return lax.ppermute(values, "col", SWAP)


def swap_dp(values, distance):
    size = lax.axis_size("dp")
    return lax.ppermute(values, "dp", [(place, place ^ distance) for place in range(size)])


def distances():
    size = lax.axis_size("dp")
    return [1 << bit for bit in range(size.bit_length() - 1)]


def after(values, *earlier):
    return lax.optimization_barrier((values,) + earlier)[0]


def halves(values, dim):
    size = values.shape[dim] // 2
    return lax.slice_in_dim(values, 0, size, axis=dim), lax.slice_in_dim(
        values, size, 2 * size, axis=dim
    )


def pick(values, place):
    size = values.shape[0] // 2
    kept = lax.dynamic_slice_in_dim(values, place * size, size, 0)
    sent = lax.dynamic_slice_in_dim(values, (1 - place) * size, size, 0)
    return kept, sent


def in_order(place, mine, theirs):
    return jnp.concatenate(
        [jnp.where(place == 0, mine, theirs), jnp.where(place == 0, theirs, mine)], axis=0
    )


def reduce_grid(own, other, row_dim):
    arrived = swap_col(other().astype(B16))
    total = own() + arrived.astype(F32)
    mine, theirs = halves(total, row_dim)
    return mine + swap_row(theirs.astype(B16)).astype(F32)


def sum_dp(values):
    me = lax.axis_index("dp")
    for distance in distances():
        kept, sent = pick(values, (me // distance) % 2)
        values = kept + swap_dp(sent.astype(B16), distance).astype(F32)
    values = values.astype(B16)
    for distance in reversed(distances()):
        values = in_order((me // distance) % 2, values, swap_dp(values, distance))
    return values.astype(F32)


def gather_dp(values):
    for distance in distances():
        values = jnp.concatenate([values, swap_dp(values, distance)], axis=0)
    return values


def shards(
    tokens, condition, adaptive, adabias, attend, attbias, outproj, outbias,
    expand, expbias, shrink, shrbias, cotangent,
):
    row = lax.axis_index("row")
    col = lax.axis_index("col")

    raw_condition = condition.astype(F32)
    act_cond = jax.nn.silu(raw_condition).astype(B16)
    mod_terms = jnp.einsum("ld,kde->lke", act_cond, adaptive, preferred_element_type=F32)
    kept, sent = pick(mod_terms, col)
    mod_rows = kept + swap_col(sent) + adabias.astype(F32)
    kept, sent = pick(mod_rows, row)
    modulation = jnp.concatenate([kept, swap_row(sent)], axis=2)

    tok_own, sent = pick(tokens, row)
    tok_oth = swap_row(sent)
    tok = (tok_own, tok_oth)

    def pieces(values):
        over = swap_row(values)
        return values, over, swap_col(values), swap_col(over)

    attend_pieces = pieces(after(attend, tok_oth))
    ready = attend_pieces[1]
    out_pieces = pieces(after(outproj, ready))
    exp_pieces = pieces(after(expand, ready))
    shr_pieces = pieces(after(shrink, ready))
    cot_own, sent = pick(cotangent, row)
    cot_oth = swap_row(after(sent, ready))

    by_col = jnp.concatenate([attbias.reshape(-1), expbias]).astype(F32)
    by_row = jnp.concatenate([outbias, shrbias]).astype(F32)
    by_col = (by_col, swap_col(by_col))
    by_row = (by_row, swap_row(by_row))
    blank = jnp.zeros((HALF,), F32)
    bias = jnp.concatenate(
        [piece for part in by_col for piece in (part[:HALF], blank, part[HALF:D])]
    )[None]
    exp_bias = jnp.concatenate([part[D:] for part in by_col])[None]
    out_bias = jnp.concatenate([part[:HALF] for part in by_row])[None]
    shr_bias = jnp.concatenate([part[HALF:] for part in by_row])[None]

    first, qkv, attended = call_forward(tok_own, tok_oth, modulation, bias, attend_pieces)
    (
        res_own, res_oth, second, act_own, act_oth, dh_own, dh_oth, e_one, e_two,
        d_middle, d_attended, mod_late, sums_late,
    ) = call_middle(
        tok, (cot_own, cot_oth), attended, modulation, (out_bias, exp_bias, shr_bias),
        out_pieces, exp_pieces, shr_pieces,
    )
    result = in_order(row, res_own, swap_row(res_oth))
    shrink_part = reduce_grid(lambda: dot_tn(act_own, e_two), lambda: dot_tn(act_oth, e_two), 1)
    expand_part = reduce_grid(lambda: dot_tn(second, dh_own), lambda: dot_tn(second, dh_oth), 0)
    att_own, att_oth = halves(attended, 1)
    outproj_part = reduce_grid(lambda: dot_tn(att_own, e_one), lambda: dot_tn(att_oth, e_one), 1)
    dqkv_own, dqkv_oth, grad_own, grad_oth, mod_early, sums_early = call_backward(
        tok, modulation, qkv, d_attended, d_middle, attend_pieces
    )
    attend_part = reduce_grid(lambda: dot_tn(first, dqkv_own), lambda: dot_tn(first, dqkv_oth), 0)
    input_gradient = in_order(row, grad_own, swap_row(grad_oth))
    shrink_grad = sum_dp(shrink_part)
    expand_grad = sum_dp(expand_part)
    outproj_grad = sum_dp(outproj_part)
    attend_grad = sum_dp(attend_part).reshape(HALF, 3, HALF).transpose(1, 0, 2)

    d_modulation = jnp.concatenate([mod_early, mod_late], axis=1).astype(B16)
    mine, theirs = halves(d_modulation, 2)
    mod_block = in_order(row, mine, swap_row(theirs))
    mod_group = in_order(col, mod_block, swap_col(mod_block))
    mod_all = gather_dp(mod_group)
    cond_all = gather_dp(act_cond)
    adabias_grad = jnp.sum(mod_all, axis=0, dtype=F32)
    adaptive_grad = jnp.einsum("ld,lke->kde", cond_all, mod_all, preferred_element_type=F32)
    d_act = jnp.einsum("lke,kde->ld", mod_group, adaptive, preferred_element_type=F32)
    d_act = d_act + swap_row(d_act)
    condition_gradient = jax.vjp(jax.nn.silu, raw_condition)[1](d_act)[0].astype(B16)

    sums_late = jnp.sum(sums_late, axis=(0, 1))
    sums_early = jnp.sum(sums_early, axis=(0, 1))
    mine, theirs = halves(sums_late[: 2 * D].reshape(2, D), 1)
    row_sums = mine + swap_row(theirs)
    row_sums = row_sums + swap_col(row_sums)
    wide = halves(sums_late[2 * D :], 0)
    narrow = halves(sums_early, 0)
    mine, theirs = [jnp.concatenate([narrow[side], wide[side]]) for side in range(2)]
    col_sums = mine + swap_col(theirs)
    col_sums = col_sums + swap_row(col_sums)
    sums = jnp.concatenate([row_sums.reshape(-1), col_sums])
    for distance in distances():
        sums = sums + swap_dp(sums, distance)
    outbias_grad = sums[:HALF]
    shrbias_grad = sums[HALF:D]
    attbias_grad = jnp.stack([sums[D : D + HALF], sums[2 * D : 2 * D + HALF]])
    expbias_grad = sums[D + SIDE :]
    return (
        result, input_gradient, condition_gradient, adaptive_grad, adabias_grad, attend_grad,
        attbias_grad, outproj_grad, outbias_grad, expand_grad, expbias_grad, shrink_grad,
        shrbias_grad,
    )


def solution(mesh):
    placed = (
        P(("dp", "col"), "row"),
        P("dp", "col"),
        P(None, "col", "row"),
        P(None, "row"),
        P(None, "row", "col"),
        P(None, "col"),
        P("col", "row"),
        P("row"),
        P("row", "col"),
        P("col"),
        P("col", "row"),
        P("row"),
        P(("dp", "col"), "row"),
    )
    return jax.shard_map(
        shards,
        mesh=mesh,
        in_specs=placed,
        out_specs=(
            P(("dp", "col"), "row"),
            P(("dp", "col"), "row"),
            P("dp", "col"),
            P(None, "col", "row"),
            P(None, "row"),
            P(None, "row", "col"),
            P(None, "col"),
            P("col", "row"),
            P("row"),
            P("row", "col"),
            P("col"),
            P("col", "row"),
            P("row"),
        ),
        check_vma=False,
    )
```

```python
import functools

import jax
import jax.numpy as jnp
from jax import lax
from jax.experimental import pallas as pl
from jax.experimental.pallas import tpu as pltpu
from jax.sharding import PartitionSpec as P

D = 768
HALF = D // 2
FF = 3072
SEQ = 256
HEAD_DIM = 64
PAIR = 2 * HEAD_DIM
SIDE = 3 * HALF
EPS = 1e-06
F32 = jnp.float32
B16 = jnp.bfloat16
SWAP = ((0, 1), (1, 0))
SCALE = HEAD_DIM ** (-0.5)
ROOT = (2.0 / 3.141592653589793) ** 0.5
CUBE = 0.044715
PER_TILE = 2
VMEM_BYTES = 60 * 1024 * 1024


def dot(left, right):
    return jnp.dot(left, right, preferred_element_type=F32)


def dot_nt(left, right):
    return lax.dot_general(left, right, (((1,), (1,)), ((), ())), preferred_element_type=F32)


def dot_tn(left, right):
    return lax.dot_general(left, right, (((0,), (0,)), ((), ())), preferred_element_type=F32)


def normalize(values):
    center = jnp.mean(values, axis=1, keepdims=True)
    spread = jnp.mean(values * values, axis=1, keepdims=True) - center * center
    inverse = lax.rsqrt(spread + EPS)
    return (values - center) * inverse, inverse


def norm_grad(upstream, normal, inverse):
    first_mean = jnp.mean(upstream, axis=1, keepdims=True)
    second_mean = jnp.mean(upstream * normal, axis=1, keepdims=True)
    return inverse * (upstream - first_mean - normal * second_mean)


def both(own_ref, oth_ref):
    return jnp.concatenate([own_ref[...], oth_ref[...]], axis=1).astype(F32)


def spread_rows(mod_ref, number):
    rows = [
        jnp.broadcast_to(mod_ref[latent, number : number + 1, :], (SEQ, D))
        for latent in range(mod_ref.shape[0])
    ]
    return rows[0] if len(rows) == 1 else jnp.concatenate(rows, axis=0)


def store_sums(out_ref, number, values):
    for latent in range(out_ref.shape[0]):
        out_ref[latent, number : number + 1, :] = jnp.sum(
            values[latent * SEQ : (latent + 1) * SEQ], axis=0, keepdims=True
        )


def attend_copies(pieces, weight, sem):
    copies = []
    for number, piece in enumerate(pieces):
        row, col = number % 2, number // 2
        for kind in range(3):
            copies.append(
                pltpu.make_async_copy(
                    piece.at[kind],
                    weight.at[pl.ds(row * HALF, HALF), pl.ds(col * SIDE + kind * HALF, HALF)],
                    sem.at[len(copies)],
                )
            )
    return copies


def grid_copies(pieces, weight, sem, first_is_row):
    copies = []
    for number, piece in enumerate(pieces):
        row, col = number % 2, number // 2
        across, down = piece.shape[1], piece.shape[0]
        top, left = (row, col) if first_is_row else (col, row)
        copies.append(
            pltpu.make_async_copy(
                piece,
                weight.at[pl.ds(top * down, down), pl.ds(left * across, across)],
                sem.at[number],
            )
        )
    return copies


def forward_kernel(
    tok_own, tok_oth, mod, bias, w0, w1, w2, w3, first_ref, qkv_ref, att_ref, weight, sem
):
    @pl.when(pl.program_id(0) == 0)
    def _():
        copies = attend_copies((w0, w1, w2, w3), weight, sem)
        for copy in copies:
            copy.start()
        for copy in copies:
            copy.wait()

    normal, _ = normalize(both(tok_own, tok_oth))
    first = (normal * (1.0 + spread_rows(mod, 1)) + spread_rows(mod, 0)).astype(B16)
    first_ref[...] = first
    qkv_ref[...] = (dot(first, weight[...]) + bias[...]).astype(B16)
    low = lax.broadcasted_iota(jnp.int32, (SEQ, PAIR), 1) < HEAD_DIM
    for col in range(2):
        for pair in range(HALF // PAIR):
            base = col * SIDE + pair * PAIR
            q_part = qkv_ref[:, base : base + PAIR] * SCALE
            k_part = qkv_ref[:, base + HALF : base + HALF + PAIR]
            v_part = qkv_ref[:, base + D : base + D + PAIR]
            outs = []
            for keep in (low, jnp.logical_not(low)):
                scores = dot_nt(jnp.where(keep, q_part, 0).astype(B16), k_part)
                exponent = jnp.exp(scores - jnp.max(scores, axis=1, keepdims=True))
                probs = exponent * (1.0 / jnp.sum(exponent, axis=1, keepdims=True))
                outs.append(dot(probs.astype(B16), v_part))
            at = col * HALF + pair * PAIR
            att_ref[:, at : at + PAIR] = jnp.where(low, outs[0], outs[1]).astype(B16)


def middle_kernel(
    tok_own, tok_oth, cot_own, cot_oth, att, mod, outbias, expbias, shrbias,
    o0, o1, o2, o3, x0, x1, x2, x3, s0, s1, s2, s3,
    res_own, res_oth, second_ref, act_own, act_oth, dh_own, dh_oth, e_one_ref, e_two_ref,
    d_mid_ref, d_att_ref, mod_ref, sum_ref,
    w_out, w_exp, w_shr, sem_out, sem_exp, sem_shr,
):
    @pl.when(pl.program_id(0) == 0)
    def _():
        copies = (
            grid_copies((o0, o1, o2, o3), w_out, sem_out, False)
            + grid_copies((x0, x1, x2, x3), w_exp, sem_exp, True)
            + grid_copies((s0, s1, s2, s3), w_shr, sem_shr, False)
        )
        for copy in copies:
            copy.start()
        for copy in copies:
            copy.wait()

    branch_one = dot(att[...], w_out[...]) + outbias[...]
    middle = both(tok_own, tok_oth) + spread_rows(mod, 2) * branch_one
    normal, inverse = normalize(middle)
    second = (normal * (1.0 + spread_rows(mod, 4)) + spread_rows(mod, 3)).astype(B16)
    second_ref[...] = second
    upstream = both(cot_own, cot_oth)
    e_two = (spread_rows(mod, 5) * upstream).astype(B16)
    e_two_ref[...] = e_two
    branch_two = shrbias[...]
    d_second = 0.0
    for part in range(FF // D):
        at = part * D
        hidden = dot(second, w_exp[:, at : at + D]) + expbias[:, at : at + D]
        square = hidden * hidden
        bend = jnp.tanh(hidden * (ROOT + (ROOT * CUBE) * square))
        share = 0.5 + 0.5 * bend
        active = (hidden * share).astype(B16)
        slope = share + (0.5 * hidden) * (1.0 - bend * bend) * (ROOT + (3.0 * ROOT * CUBE) * square)
        branch_two = branch_two + dot(active, w_shr[at : at + D, :])
        d_hidden = (dot_nt(e_two, w_shr[at : at + D, :]) * slope).astype(B16)
        d_second = d_second + dot_nt(d_hidden, w_exp[:, at : at + D])
        act_ref, dh_ref = (act_own, dh_own) if 2 * at < FF else (act_oth, dh_oth)
        into = at % (FF // 2)
        act_ref[:, into : into + D] = active
        dh_ref[:, into : into + D] = d_hidden
        sum_ref[0, :, 2 * D + at : 2 * D + at + D] = jnp.sum(
            d_hidden.astype(F32), axis=0, keepdims=True
        )
    result = (middle + spread_rows(mod, 5) * branch_two).astype(B16)
    res_own[...] = result[:, :HALF]
    res_oth[...] = result[:, HALF:]
    store_sums(mod_ref, 3, upstream * branch_two)
    store_sums(mod_ref, 1, d_second)
    store_sums(mod_ref, 2, d_second * normal)
    d_middle = upstream + norm_grad(d_second * (1.0 + spread_rows(mod, 4)), normal, inverse)
    d_mid_ref[...] = d_middle
    store_sums(mod_ref, 0, d_middle * branch_one)
    e_one = (spread_rows(mod, 2) * d_middle).astype(B16)
    e_one_ref[...] = e_one
    d_att_ref[...] = dot_nt(e_one, w_out[...]).astype(B16)
    sum_ref[0, :, :D] = jnp.sum(e_one.astype(F32), axis=0, keepdims=True)
    sum_ref[0, :, D : 2 * D] = jnp.sum(e_two.astype(F32), axis=0, keepdims=True)


def backward_kernel(
    tok_own, tok_oth, mod, qkv, d_att, d_mid, w0, w1, w2, w3,
    dqkv_own, dqkv_oth, grad_own, grad_oth, mod_ref, sum_ref, weight, sem,
):
    @pl.when(pl.program_id(0) == 0)
    def _():
        copies = attend_copies((w0, w1, w2, w3), weight, sem)
        for copy in copies:
            copy.start()
        for copy in copies:
            copy.wait()

    low = lax.broadcasted_iota(jnp.int32, (SEQ, PAIR), 1) < HEAD_DIM
    for col in range(2):
        out_ref = (dqkv_own, dqkv_oth)[col]
        for pair in range(HALF // PAIR):
            base = col * SIDE + pair * PAIR
            q_part = qkv[:, base : base + PAIR]
            k_part = qkv[:, base + HALF : base + HALF + PAIR]
            v_part = qkv[:, base + D : base + D + PAIR]
            d_part = d_att[:, col * HALF + pair * PAIR : col * HALF + (pair + 1) * PAIR]
            queries, keys, values = [], [], []
            for keep in (low, jnp.logical_not(low)):
                scores = dot_nt(jnp.where(keep, k_part * SCALE, 0).astype(B16), q_part)
                exponent = jnp.exp(scores - jnp.max(scores, axis=0, keepdims=True))
                probs = exponent * (1.0 / jnp.sum(exponent, axis=0, keepdims=True))
                d_probs = dot_nt(jnp.where(keep, v_part, 0).astype(B16), d_part)
                weighted = probs * d_probs
                d_scores = (weighted - probs * jnp.sum(weighted, axis=0, keepdims=True)).astype(B16)
                values.append(dot(probs.astype(B16), d_part))
                keys.append(dot(d_scores, q_part))
                queries.append(dot_tn(d_scores, k_part))
            for kind, (first, then, factor) in enumerate(
                ((*queries, SCALE), (*keys, SCALE), (*values, 1.0))
            ):
                at = kind * HALF + pair * PAIR
                piece = (jnp.where(low, first, then) * factor).astype(B16)
                out_ref[:, at : at + PAIR] = piece
                sum_ref[0, :, col * SIDE + at : col * SIDE + at + PAIR] = jnp.sum(
                    piece.astype(F32), axis=0, keepdims=True
                )
    d_first = dot_nt(dqkv_own[...], weight[:, :SIDE]) + dot_nt(dqkv_oth[...], weight[:, SIDE:])
    normal, inverse = normalize(both(tok_own, tok_oth))
    store_sums(mod_ref, 0, d_first)
    store_sums(mod_ref, 1, d_first * normal)
    grad = (
        d_mid[...] + norm_grad(d_first * (1.0 + spread_rows(mod, 1)), normal, inverse)
    ).astype(B16)
    grad_own[...] = grad[:, :HALF]
    grad_oth[...] = grad[:, HALF:]


def tiles(rows, width):
    return pl.BlockSpec((rows, width), lambda step: (step, 0))


def stacked(count, rows, width):
    return pl.BlockSpec((count, rows, width), lambda step: (step, 0, 0))


def fixed(width):
    return pl.BlockSpec((1, width), lambda step: (0, 0))


def anywhere(count):
    return [pl.BlockSpec(memory_space=pl.ANY)] * count


def params():
    return pltpu.CompilerParams(
        vmem_limit_bytes=VMEM_BYTES, dimension_semantics=("arbitrary",)
    )


def call_forward(tok_own, tok_oth, modulation, bias, pieces):
    count = tok_own.shape[0]
    latents = count // SEQ
    return pl.pallas_call(
        forward_kernel,
        grid=(latents,),
        in_specs=[tiles(SEQ, HALF)] * 2 + [stacked(1, 6, D), fixed(2 * SIDE)] + anywhere(4),
        out_specs=[tiles(SEQ, D), tiles(SEQ, 2 * SIDE), tiles(SEQ, D)],
        out_shape=[
            jax.ShapeDtypeStruct((count, D), B16),
            jax.ShapeDtypeStruct((count, 2 * SIDE), B16),
            jax.ShapeDtypeStruct((count, D), B16),
        ],
        scratch_shapes=[pltpu.VMEM((D, 2 * SIDE), B16), pltpu.SemaphoreType.DMA((12,))],
        compiler_params=params(),
        cost_estimate=pl.CostEstimate(
            flops=14 * 10**9, bytes_accessed=16 * 10**6, transcendentals=count * SEQ * 12
        ),
        name="forward",
    )(tok_own, tok_oth, modulation, bias, *pieces)


def call_middle(tok, cot, att, modulation, biases, out_pieces, exp_pieces, shr_pieces):
    count = att.shape[0]
    latents = count // SEQ
    per_tile = PER_TILE if latents % PER_TILE == 0 else 1
    rows = per_tile * SEQ
    steps = latents // per_tile
    halves = [tiles(rows, HALF)] * 2

    def shape(width, kind=B16):
        return jax.ShapeDtypeStruct((count, width), kind)

    return pl.pallas_call(
        middle_kernel,
        grid=(steps,),
        in_specs=halves
        + halves
        + [tiles(rows, D), stacked(per_tile, 6, D), fixed(D), fixed(FF), fixed(D)]
        + anywhere(12),
        out_specs=halves
        + [tiles(rows, D)]
        + [tiles(rows, FF // 2)] * 4
        + [tiles(rows, D)] * 4
        + [stacked(per_tile, 4, D), stacked(1, 1, 2 * D + FF)],
        out_shape=[shape(HALF), shape(HALF), shape(D)]
        + [shape(FF // 2)] * 4
        + [shape(D), shape(D), shape(D, F32), shape(D)]
        + [
            jax.ShapeDtypeStruct((latents, 4, D), F32),
            jax.ShapeDtypeStruct((steps, 1, 2 * D + FF), F32),
        ],
        scratch_shapes=[
            pltpu.VMEM((D, D), B16),
            pltpu.VMEM((D, FF), B16),
            pltpu.VMEM((FF, D), B16),
            pltpu.SemaphoreType.DMA((4,)),
            pltpu.SemaphoreType.DMA((4,)),
            pltpu.SemaphoreType.DMA((4,)),
        ],
        compiler_params=params(),
        cost_estimate=pl.CostEstimate(
            flops=30 * 10**9, bytes_accessed=50 * 10**6, transcendentals=count * FF
        ),
        name="middle",
    )(*tok, *cot, att, modulation, *biases, *out_pieces, *exp_pieces, *shr_pieces)


def call_backward(tok, modulation, qkv, d_att, d_mid, pieces):
    count = d_att.shape[0]
    latents = count // SEQ
    return pl.pallas_call(
        backward_kernel,
        grid=(latents,),
        in_specs=[tiles(SEQ, HALF)] * 2
        + [stacked(1, 6, D), tiles(SEQ, 2 * SIDE), tiles(SEQ, D), tiles(SEQ, D)]
        + anywhere(4),
        out_specs=[tiles(SEQ, SIDE)] * 2
        + [tiles(SEQ, HALF)] * 2
        + [stacked(1, 2, D), stacked(1, 1, 2 * SIDE)],
        out_shape=[jax.ShapeDtypeStruct((count, SIDE), B16)] * 2
        + [jax.ShapeDtypeStruct((count, HALF), B16)] * 2
        + [
            jax.ShapeDtypeStruct((latents, 2, D), F32),
            jax.ShapeDtypeStruct((latents, 1, 2 * SIDE), F32),
        ],
        scratch_shapes=[pltpu.VMEM((D, 2 * SIDE), B16), pltpu.SemaphoreType.DMA((12,))],
        compiler_params=params(),
        cost_estimate=pl.CostEstimate(
            flops=25 * 10**9, bytes_accessed=20 * 10**6, transcendentals=count * SEQ * 12
        ),
        name="backward",
    )(*tok, modulation, qkv, d_att, d_mid, *pieces)


def swap_row(values):
    return lax.ppermute(values, "row", SWAP)


def swap_col(values):
    return lax.ppermute(values, "col", SWAP)


def swap_dp(values, distance):
    size = lax.axis_size("dp")
    return lax.ppermute(values, "dp", [(place, place ^ distance) for place in range(size)])


def distances():
    size = lax.axis_size("dp")
    return [1 << bit for bit in range(size.bit_length() - 1)]


def after(values, *earlier):
    return lax.optimization_barrier((values,) + earlier)[0]


def halves(values, dim):
    size = values.shape[dim] // 2
    return lax.slice_in_dim(values, 0, size, axis=dim), lax.slice_in_dim(
        values, size, 2 * size, axis=dim
    )


def pick(values, place):
    size = values.shape[0] // 2
    kept = lax.dynamic_slice_in_dim(values, place * size, size, 0)
    sent = lax.dynamic_slice_in_dim(values, (1 - place) * size, size, 0)
    return kept, sent


def in_order(place, mine, theirs):
    return jnp.concatenate(
        [jnp.where(place == 0, mine, theirs), jnp.where(place == 0, theirs, mine)], axis=0
    )


def x_place():
    return lax.axis_index("dp") % 2


def scatter_stage(values, distance, axis=0):
    place = (lax.axis_index("dp") // distance) % 2
    size = values.shape[axis] // 2
    kept = lax.dynamic_slice_in_dim(values, place * size, size, axis)
    sent = lax.dynamic_slice_in_dim(values, (1 - place) * size, size, axis)
    return kept + swap_dp(sent.astype(B16), distance).astype(F32)


def gather_dp(values):
    for distance in reversed(distances()):
        values = jnp.concatenate([values, swap_dp(values, distance)], axis=0)
    return values


def sum_order():
    me, mine = lax.axis_index("dp"), 0
    for distance in distances():
        mine = mine * 2 + (me // distance) % 2
    return jnp.full((1,), mine, jnp.int32)


def order_grid_kernel(mine, values, shr_out, out_out, exp_out):
    shr_rows, out_rows, exp_rows = shr_out.shape[1], out_out.shape[1], exp_out.shape[1]
    for block in range(values.shape[0]):
        place = mine[0] ^ block
        shr_out[place] = values[block, :shr_rows].astype(F32)
        out_out[place] = values[block, shr_rows : shr_rows + out_rows].astype(F32)
        for part in range(exp_out.shape[2] // HALF):
            at = shr_rows + out_rows + part * exp_rows
            exp_out[place, :, part * HALF : (part + 1) * HALF] = values[
                block, at : at + exp_rows
            ].astype(F32)


def order(kernel, values, shapes):
    whole = [pl.BlockSpec(memory_space=pltpu.VMEM)]
    return pl.pallas_call(
        kernel,
        in_specs=[pl.BlockSpec(memory_space=pltpu.SMEM)] + whole,
        out_specs=whole * len(shapes),
        out_shape=[jax.ShapeDtypeStruct(shape, F32) for shape in shapes],
        compiler_params=pltpu.CompilerParams(vmem_limit_bytes=VMEM_BYTES),
        name="order",
    )(sum_order(), values)


def shards(
    tokens, condition, adaptive, adabias, attend, attbias, outproj, outbias,
    expand, expbias, shrink, shrbias, cotangent,
):
    row = lax.axis_index("row")
    col = lax.axis_index("col")

    tok_own, sent = pick(tokens, row)
    tok_oth = swap_row(sent)
    tok = (tok_own, tok_oth)

    raw_condition = condition.astype(F32)
    act_cond = jax.nn.silu(raw_condition).astype(B16)
    mod_terms = jnp.einsum("ld,kde->lke", act_cond, adaptive, preferred_element_type=F32)
    kept, sent = pick(mod_terms, col)
    group = kept.shape[0]
    latents = group // 2
    col_bias = jnp.concatenate([attbias.reshape(-1), expbias]).astype(F32).reshape(-1, 1, HALF)
    got = swap_col(
        jnp.concatenate([sent.reshape(-1, HALF), col_bias.reshape(-1, HALF)], axis=0)
    )
    mod_rows = kept + got[: 6 * group].reshape(group, 6, HALF) + adabias.astype(F32)
    col_other = got[6 * group :]
    kept, sent = pick(mod_rows, row)
    row_bias = jnp.stack([outbias, shrbias]).astype(F32)
    got = swap_row(jnp.concatenate([sent.reshape(-1, HALF), row_bias], axis=0))
    modulation = jnp.concatenate([kept, got[: 6 * latents].reshape(latents, 6, HALF)], axis=2)
    row_other = got[6 * latents :]
    col_bias = col_bias.reshape(-1, HALF)
    blank = jnp.zeros((HALF,), F32)
    bias = jnp.concatenate(
        [piece for part in (col_bias, col_other) for piece in (part[0], blank, part[1])]
    )[None]
    exp_bias = jnp.concatenate([col_bias[2:], col_other[2:]], axis=0).reshape(1, FF)
    out_bias = jnp.concatenate([row_bias[:1], row_other[:1]], axis=1)
    shr_bias = jnp.concatenate([row_bias[1:], row_other[1:]], axis=1)

    def pieces(values, over):
        return values, over, swap_col(values), swap_col(over)

    def near(values):
        return pick(values, x_place())[0]

    def relayed(half):
        return in_order(x_place(), half, swap_dp(half, 1))

    flat_attend = attend.reshape(-1, attend.shape[2])
    att_half = swap_row(after(near(flat_attend), tok_oth, got))
    att_half, exp_half = lax.optimization_barrier((att_half, near(expand)))
    exp_half = swap_row(exp_half)
    attend_pieces = pieces(attend, relayed(att_half).reshape(attend.shape))
    cond_all = gather_dp(act_cond)
    *attend_pieces, exp_half, shr_half, outproj, cond_all = lax.optimization_barrier(
        (*attend_pieces, exp_half, near(shrink), outproj, cond_all)
    )
    shr_half, out_over = swap_row(shr_half), swap_row(outproj)
    exp_far = swap_dp(exp_half, 1)
    cot_own, cot_sent = pick(cotangent, row)
    first, qkv, attended = call_forward(tok_own, tok_oth, modulation, bias, attend_pieces)
    attended, exp_half, exp_far, shr_half, out_over, cot_sent = lax.optimization_barrier(
        (attended, exp_half, exp_far, shr_half, out_over, cot_sent)
    )
    cot_oth = swap_row(cot_sent)
    shr_far = swap_dp(shr_half, 1)
    exp_over = in_order(x_place(), exp_half, exp_far)
    out_pieces = pieces(outproj, out_over)
    exp_pieces = pieces(expand, exp_over)
    shr_over = in_order(x_place(), shr_half, shr_far)
    shr_pieces = pieces(shrink, shr_over)
    (
        res_own, res_oth, second, act_own, act_oth, dh_own, dh_oth, e_one, e_two,
        d_middle, d_attended, mod_late, sums_late,
    ) = call_middle(
        tok, (cot_own, cot_oth), attended, modulation, (out_bias, exp_bias, shr_bias),
        out_pieces, exp_pieces, shr_pieces,
    )
    att_own, att_oth = halves(attended, 1)
    depth = act_oth.shape[1]
    shr_got = swap_col(
        jnp.concatenate(
            [dot_tn(act_oth, e_two).astype(B16), dot_tn(att_oth, e_one).astype(B16)], axis=0
        )
    )
    exp_got = swap_col(dot_tn(second, dh_oth).astype(B16))
    shr_total = dot_tn(act_own, e_two) + shr_got[:depth].astype(F32)
    out_total = dot_tn(att_own, e_one) + shr_got[depth:].astype(F32)
    exp_total = dot_tn(second, dh_own) + exp_got.astype(F32)
    d_attended, shr_total, out_total, exp_total = lax.optimization_barrier(
        (d_attended, shr_total, out_total, exp_total)
    )
    near_step, *far_steps = distances()
    size = lax.axis_size("dp")
    shr_mine, shr_theirs = [
        jnp.concatenate(
            [part.reshape(size, -1, HALF) for part in parts], axis=1
        )
        for parts in zip(halves(shr_total, 1), halves(out_total, 1))
    ]
    shr_part = shr_mine + swap_row(shr_theirs.astype(B16)).astype(F32)
    exp_part = scatter_stage(exp_total.reshape(2, HALF, -1), near_step, 1)

    dqkv_own, dqkv_oth, grad_own, grad_oth, mod_early, sums_early = call_backward(
        tok, modulation, qkv, d_attended, d_middle, attend_pieces
    )
    dqkv_own, dqkv_oth, shr_part, exp_part = lax.optimization_barrier(
        (dqkv_own, dqkv_oth, shr_part, exp_part)
    )
    exp_part = exp_part[0] + swap_row(exp_part[1].astype(B16)).astype(F32)
    shr_part = scatter_stage(shr_part, near_step)
    att_got = swap_col(dot_tn(first, dqkv_oth).astype(B16)).astype(F32)
    att_total = dot_tn(first, dqkv_own) + att_got
    att_total, shr_part, exp_part, mod_early, res_oth = lax.optimization_barrier(
        (att_total, shr_part, exp_part, mod_early, res_oth)
    )
    att_mine, att_theirs = halves(att_total, 0)
    att_part = att_mine + swap_row(att_theirs.astype(B16)).astype(F32)
    exp_part = exp_part.reshape(size // 2, HALF // size, -1)
    grid_part = jnp.concatenate(
        [shr_part]
        + [
            exp_part[:, :, at : at + HALF] for at in range(0, exp_part.shape[2], HALF)
        ],
        axis=1,
    )
    grid_part = scatter_stage(grid_part, far_steps[0])

    d_modulation = jnp.concatenate([mod_early, mod_late], axis=1).astype(B16).astype(F32)
    sums_late = jnp.sum(sums_late, axis=(0, 1))
    sums_early = jnp.sum(sums_early, axis=(0, 1)).reshape(6, HALF)
    row_sums = sums_late[: 2 * D].reshape(2, 2, HALF)
    wide = sums_late[2 * D :].reshape(2, -1, HALF)
    col_sums = jnp.concatenate(
        [sums_early[0:3:2], wide[0], sums_early[3:6:2], wide[1]], axis=0
    )
    mine = d_modulation[:, :, :HALF].reshape(-1, HALF)
    theirs = d_modulation[:, :, HALF:].reshape(-1, HALF)
    got = swap_row(jnp.concatenate([theirs, row_sums[:, 1], col_sums], axis=0))
    rows = mine.shape[0]
    block = in_order(row, mine, got[:rows]).astype(B16)
    sums = jnp.concatenate([row_sums[:, 0], col_sums], axis=0) + got[rows:]
    high = sums.astype(B16)
    low = (sums - high.astype(F32)).astype(B16)
    width = block.shape[0] + 2 * sums.shape[0]
    packed = jnp.concatenate([block, high, low], axis=0)[None]
    att_part, packed, grid_part, grad_oth, res_oth = lax.optimization_barrier(
        (att_part, packed, grid_part, grad_oth, res_oth)
    )
    attend_grad = lax.psum(att_part.astype(B16), "dp").astype(F32)
    attend_grad = attend_grad.reshape(HALF, 3, HALF).transpose(1, 0, 2)
    packed_all = gather_dp(packed)
    for distance in far_steps[1:]:
        grid_part = scatter_stage(grid_part, distance)
    block_all = packed_all[:, : block.shape[0]].reshape(-1, HALF)
    both_sums = jnp.sum(packed_all[:, block.shape[0] :].astype(F32), axis=0)
    sums = both_sums[: sums.shape[0]] + both_sums[sums.shape[0] :]
    count = col_sums.shape[0] // 2
    given = jnp.concatenate([sums[:2], sums[2 + count :]], axis=0)
    high = given.astype(B16)
    low = (given - high.astype(F32)).astype(B16)
    got = swap_col(jnp.concatenate([block_all, high, low], axis=0))
    other_all = got[: block_all.shape[0]]
    got = got[block_all.shape[0] :].astype(F32)
    sums = sums[: 2 + count] + got[: 2 + count] + got[2 + count :]
    outbias_grad, shrbias_grad = sums[0], sums[1]
    attbias_grad = sums[2:4]
    expbias_grad = sums[4:].reshape(-1)

    result = in_order(row, res_own, swap_row(res_oth))
    input_gradient = in_order(row, grad_own, swap_row(grad_oth))
    exp_width = expand.shape[1]
    shrink_grad, outproj_grad, expand_grad = order(
        order_grid_kernel,
        gather_dp(grid_part.astype(B16)),
        [(size, depth // size, HALF), (size, HALF // size, HALF), (size, HALF // size, exp_width)],
    )
    shrink_grad, outproj_grad = [part.reshape(-1, HALF) for part in (shrink_grad, outproj_grad)]
    expand_grad = expand_grad.reshape(HALF, exp_width)
    mod_all = jnp.concatenate([block_all, other_all], axis=0).reshape(-1, 6, HALF)
    cond_mine, cond_theirs = pick(
        cond_all.reshape(-1, 2 * group, HALF).transpose(1, 0, 2), col
    )
    cond_all = jnp.concatenate(
        [part.transpose(1, 0, 2).reshape(-1, HALF) for part in (cond_mine, cond_theirs)], axis=0
    )
    adabias_grad = jnp.sum(mod_all, axis=0, dtype=F32)
    adaptive_grad = jnp.einsum("ld,lke->kde", cond_all, mod_all, preferred_element_type=F32)
    mod_group = in_order(col, block, other_all[: block.shape[0]]).reshape(-1, 6, HALF)
    d_act = jnp.einsum("lke,kde->ld", mod_group, adaptive, preferred_element_type=F32)
    d_act = d_act + swap_row(d_act)
    condition_gradient = jax.vjp(jax.nn.silu, raw_condition)[1](d_act)[0].astype(B16)
    return (
        result, input_gradient, condition_gradient, adaptive_grad, adabias_grad, attend_grad,
        attbias_grad, outproj_grad, outbias_grad, expand_grad, expbias_grad, shrink_grad,
        shrbias_grad,
    )


def solution(mesh):
    placed = (
        P(("dp", "col"), "row"),
        P("dp", "col"),
        P(None, "col", "row"),
        P(None, "row"),
        P(None, "row", "col"),
        P(None, "col"),
        P("col", "row"),
        P("row"),
        P("row", "col"),
        P("col"),
        P("col", "row"),
        P("row"),
        P(("dp", "col"), "row"),
    )
    return jax.shard_map(
        shards,
        mesh=mesh,
        in_specs=placed,
        out_specs=(
            P(("dp", "col"), "row"),
            P(("dp", "col"), "row"),
            P("dp", "col"),
            P(None, "col", "row"),
            P(None, "row"),
            P(None, "row", "col"),
            P(None, "col"),
            P("col", "row"),
            P("row"),
            P("row", "col"),
            P("col"),
            P("col", "row"),
            P("row"),
        ),
        check_vma=False,
    )
```

```python
import functools

import jax
import jax.numpy as jnp
from jax import lax
from jax.experimental import pallas as pl
from jax.experimental.pallas import tpu as pltpu
from jax.sharding import PartitionSpec as P

D = 768
HALF = D // 2
FF = 3072
SEQ = 256
HEAD_DIM = 64
PAIR = 2 * HEAD_DIM
SIDE = 3 * HALF
EPS = 1e-06
F32 = jnp.float32
B16 = jnp.bfloat16
SWAP = ((0, 1), (1, 0))
SCALE = HEAD_DIM ** (-0.5)
ROOT = (2.0 / 3.141592653589793) ** 0.5
CUBE = 0.044715
PER_TILE = 2
VMEM_BYTES = 60 * 1024 * 1024


def dot(left, right):
    return jnp.dot(left, right, preferred_element_type=F32)


def dot_nt(left, right):
    return lax.dot_general(left, right, (((1,), (1,)), ((), ())), preferred_element_type=F32)


def dot_tn(left, right):
    return lax.dot_general(left, right, (((0,), (0,)), ((), ())), preferred_element_type=F32)


def normalize(values):
    center = jnp.mean(values, axis=1, keepdims=True)
    spread = jnp.mean(values * values, axis=1, keepdims=True) - center * center
    inverse = lax.rsqrt(spread + EPS)
    return (values - center) * inverse, inverse


def norm_grad(upstream, normal, inverse):
    first_mean = jnp.mean(upstream, axis=1, keepdims=True)
    second_mean = jnp.mean(upstream * normal, axis=1, keepdims=True)
    return inverse * (upstream - first_mean - normal * second_mean)


def both(own_ref, oth_ref):
    return jnp.concatenate([own_ref[...], oth_ref[...]], axis=1).astype(F32)


def line(ref, lead, number):
    return ref[lead, number : number + 1, :]


def spread_rows(mods, number, per_tile):
    own, oth = mods
    rows = []
    for latent in range(per_tile):
        at = pl.ds(pl.program_id(0) * per_tile + latent, 1)
        pair = jnp.concatenate([own[number, at, :], oth[number, at, :]], axis=1)
        rows.append(jnp.broadcast_to(pair, (SEQ, D)))
    return rows[0] if per_tile == 1 else jnp.concatenate(rows, axis=0)


def store_sums(out_ref, number, values):
    for latent in range(out_ref.shape[0]):
        out_ref[latent, number : number + 1, :] = jnp.sum(
            values[latent * SEQ : (latent + 1) * SEQ], axis=0, keepdims=True
        )


def attend_copies(pieces, weight, sem):
    copies = []
    for number, piece in enumerate(pieces):
        row, col = number % 2, number // 2
        for kind in range(3):
            copies.append(
                pltpu.make_async_copy(
                    piece.at[kind],
                    weight.at[pl.ds(row * HALF, HALF), pl.ds(col * SIDE + kind * HALF, HALF)],
                    sem.at[len(copies)],
                )
            )
    return copies


def grid_copies(pieces, weight, sem):
    copies = []
    for number, piece in enumerate(pieces):
        row, col = number % 2, number // 2
        across, down = piece.shape[1], piece.shape[0]
        copies.append(
            pltpu.make_async_copy(
                piece,
                weight.at[pl.ds(col * down, down), pl.ds(row * across, across)],
                sem.at[number],
            )
        )
    return copies


def relay_copies(place, pieces, weight, sem, first_is_row):
    copies = []
    for col in range(2):
        whole, near, far = pieces[3 * col : 3 * col + 3]
        down, across = whole.shape
        size = near.shape[0]
        for piece, row, start in (
            (whole, 0, 0),
            (near, 1, place * size),
            (far, 1, (1 - place) * size),
        ):
            top, left = (row, col) if first_is_row else (col, row)
            rows = pl.ds(pl.multiple_of(top * down + start, 16), piece.shape[0])
            copies.append(
                pltpu.make_async_copy(
                    piece, weight.at[rows, pl.ds(left * across, across)], sem.at[len(copies)]
                )
            )
    return copies


def forward_kernel(
    tok_own, tok_oth, mod_own, mod_oth, col_own, col_oth, w0, w1, w2, w3,
    first_ref, qkv_ref, att_ref, weight, sem,
):
    mod = (mod_own, mod_oth)

    @pl.when(pl.program_id(0) == 0)
    def _():
        copies = attend_copies((w0, w1, w2, w3), weight, sem)
        for copy in copies:
            copy.start()
        for copy in copies:
            copy.wait()

    normal, _ = normalize(both(tok_own, tok_oth))
    first = (normal * (1.0 + spread_rows(mod, 1, 1)) + spread_rows(mod, 0, 1)).astype(B16)
    first_ref[...] = first
    blank = jnp.zeros((1, HALF), F32)
    last = col_oth.shape[0] - 1
    bias = jnp.concatenate(
        [line(col_own, 0, 0), blank, line(col_own, 0, 1)]
        + [line(col_oth, last, 0), blank, line(col_oth, last, 1)],
        axis=1,
    )
    qkv_ref[...] = (dot(first, weight[...]) + bias).astype(B16)
    low = lax.broadcasted_iota(jnp.int32, (SEQ, PAIR), 1) < HEAD_DIM
    for col in range(2):
        for pair in range(HALF // PAIR):
            base = col * SIDE + pair * PAIR
            q_part = qkv_ref[:, base : base + PAIR] * SCALE
            k_part = qkv_ref[:, base + HALF : base + HALF + PAIR]
            v_part = qkv_ref[:, base + D : base + D + PAIR]
            outs = []
            for keep in (low, jnp.logical_not(low)):
                scores = dot_nt(jnp.where(keep, q_part, 0).astype(B16), k_part)
                exponent = jnp.exp(scores - jnp.max(scores, axis=1, keepdims=True))
                probs = exponent * (1.0 / jnp.sum(exponent, axis=1, keepdims=True))
                outs.append(dot(probs.astype(B16), v_part))
            at = col * HALF + pair * PAIR
            att_ref[:, at : at + PAIR] = jnp.where(low, outs[0], outs[1]).astype(B16)


def middle_kernel(
    place, tok_own, tok_oth, cot_own, cot_oth, att, mod_own, mod_oth, col_own, col_oth, row_own,
    o0, o1, o2, o3, x0, x1, x2, x3, x4, x5, s0, s1, s2, s3, s4, s5,
    res_own, res_oth, second_ref, act_own, act_oth, dh_own, dh_oth, e_one_ref, e_two_ref,
    d_mid_ref, d_att_ref, mod_ref, sum_ref,
    w_out, w_exp, w_shr, sem_out, sem_exp, sem_shr,
):
    @pl.when(pl.program_id(0) == 0)
    def _():
        copies = (
            grid_copies((o0, o1, o2, o3), w_out, sem_out)
            + relay_copies(place[0], (x0, x1, x2, x3, x4, x5), w_exp, sem_exp, True)
            + relay_copies(place[0], (s0, s1, s2, s3, s4, s5), w_shr, sem_shr, False)
        )
        for copy in copies:
            copy.start()
        for copy in copies:
            copy.wait()

    per_tile = mod_ref.shape[0]
    last = mod_oth.shape[0] - 1
    rows = functools.partial(spread_rows, (mod_own, mod_oth), per_tile=per_tile)
    outbias = jnp.concatenate([line(row_own, 0, 0), line(mod_oth, last, 0)], axis=1)
    shrbias = jnp.concatenate([line(row_own, 0, 1), line(mod_oth, last, 1)], axis=1)

    branch_one = dot(att[...], w_out[...]) + outbias
    middle = both(tok_own, tok_oth) + rows(2) * branch_one
    normal, inverse = normalize(middle)
    second = (normal * (1.0 + rows(4)) + rows(3)).astype(B16)
    second_ref[...] = second
    upstream = both(cot_own, cot_oth)
    e_two = (rows(5) * upstream).astype(B16)
    e_two_ref[...] = e_two
    branch_two = shrbias
    d_second = 0.0
    for part in range(FF // D):
        at = part * D
        owner, lead = (col_own, 0) if 2 * at < FF else (col_oth, col_oth.shape[0] - 1)
        number = 2 + 2 * (part % (FF // D // 2))
        expbias = jnp.concatenate(
            [line(owner, lead, number), line(owner, lead, number + 1)], axis=1
        )
        hidden = dot(second, w_exp[:, at : at + D]) + expbias
        square = hidden * hidden
        bend = jnp.tanh(hidden * (ROOT + (ROOT * CUBE) * square))
        share = 0.5 + 0.5 * bend
        active = (hidden * share).astype(B16)
        slope = share + (0.5 * hidden) * (1.0 - bend * bend) * (ROOT + (3.0 * ROOT * CUBE) * square)
        branch_two = branch_two + dot(active, w_shr[at : at + D, :])
        d_hidden = (dot_nt(e_two, w_shr[at : at + D, :]) * slope).astype(B16)
        d_second = d_second + dot_nt(d_hidden, w_exp[:, at : at + D])
        act_ref, dh_ref = (act_own, dh_own) if 2 * at < FF else (act_oth, dh_oth)
        into = at % (FF // 2)
        act_ref[:, into : into + D] = active
        dh_ref[:, into : into + D] = d_hidden
        sum_ref[0, :, 2 * D + at : 2 * D + at + D] = jnp.sum(
            d_hidden.astype(F32), axis=0, keepdims=True
        )
    result = (middle + rows(5) * branch_two).astype(B16)
    res_own[...] = result[:, :HALF]
    res_oth[...] = result[:, HALF:]
    store_sums(mod_ref, 3, upstream * branch_two)
    store_sums(mod_ref, 1, d_second)
    store_sums(mod_ref, 2, d_second * normal)
    d_middle = upstream + norm_grad(d_second * (1.0 + rows(4)), normal, inverse)
    d_mid_ref[...] = d_middle
    store_sums(mod_ref, 0, d_middle * branch_one)
    e_one = (rows(2) * d_middle).astype(B16)
    e_one_ref[...] = e_one
    d_att_ref[...] = dot_nt(e_one, w_out[...]).astype(B16)
    sum_ref[0, :, :D] = jnp.sum(e_one.astype(F32), axis=0, keepdims=True)
    sum_ref[0, :, D : 2 * D] = jnp.sum(e_two.astype(F32), axis=0, keepdims=True)


def backward_kernel(
    tok_own, tok_oth, mod_own, mod_oth, qkv, d_att, d_mid, w0, w1, w2, w3,
    dqkv_own, dqkv_oth, grad_own, grad_oth, mod_ref, sum_ref, weight, sem,
):
    mod = (mod_own, mod_oth)

    @pl.when(pl.program_id(0) == 0)
    def _():
        copies = attend_copies((w0, w1, w2, w3), weight, sem)
        for copy in copies:
            copy.start()
        for copy in copies:
            copy.wait()

    low = lax.broadcasted_iota(jnp.int32, (SEQ, PAIR), 1) < HEAD_DIM
    for col in range(2):
        out_ref = (dqkv_own, dqkv_oth)[col]
        for pair in range(HALF // PAIR):
            base = col * SIDE + pair * PAIR
            q_part = qkv[:, base : base + PAIR]
            k_part = qkv[:, base + HALF : base + HALF + PAIR]
            v_part = qkv[:, base + D : base + D + PAIR]
            d_part = d_att[:, col * HALF + pair * PAIR : col * HALF + (pair + 1) * PAIR]
            queries, keys, values = [], [], []
            for keep in (low, jnp.logical_not(low)):
                scores = dot_nt(jnp.where(keep, k_part * SCALE, 0).astype(B16), q_part)
                exponent = jnp.exp(scores - jnp.max(scores, axis=0, keepdims=True))
                probs = exponent * (1.0 / jnp.sum(exponent, axis=0, keepdims=True))
                d_probs = dot_nt(jnp.where(keep, v_part, 0).astype(B16), d_part)
                weighted = probs * d_probs
                d_scores = (weighted - probs * jnp.sum(weighted, axis=0, keepdims=True)).astype(B16)
                values.append(dot(probs.astype(B16), d_part))
                keys.append(dot(d_scores, q_part))
                queries.append(dot_tn(d_scores, k_part))
            for kind, (first, then, factor) in enumerate(
                ((*queries, SCALE), (*keys, SCALE), (*values, 1.0))
            ):
                at = kind * HALF + pair * PAIR
                piece = (jnp.where(low, first, then) * factor).astype(B16)
                out_ref[:, at : at + PAIR] = piece
                sum_ref[0, :, col * SIDE + at : col * SIDE + at + PAIR] = jnp.sum(
                    piece.astype(F32), axis=0, keepdims=True
                )
    d_first = dot_nt(dqkv_own[...], weight[:, :SIDE]) + dot_nt(dqkv_oth[...], weight[:, SIDE:])
    normal, inverse = normalize(both(tok_own, tok_oth))
    store_sums(mod_ref, 0, d_first)
    store_sums(mod_ref, 1, d_first * normal)
    grad = (
        d_mid[...] + norm_grad(d_first * (1.0 + spread_rows(mod, 1, 1)), normal, inverse)
    ).astype(B16)
    grad_own[...] = grad[:, :HALF]
    grad_oth[...] = grad[:, HALF:]


def tiles(rows, width):
    return pl.BlockSpec((rows, width), lambda step: (step, 0))


def stacked(count, rows, width):
    return pl.BlockSpec((count, rows, width), lambda step: (step, 0, 0))


def fixed(values):
    return pl.BlockSpec(values.shape, lambda step: (0,) * values.ndim)


def anywhere(count):
    return [pl.BlockSpec(memory_space=pl.ANY)] * count


def params():
    return pltpu.CompilerParams(
        vmem_limit_bytes=VMEM_BYTES, dimension_semantics=("arbitrary",)
    )


def call_forward(tok_own, tok_oth, vectors, pieces):
    count = tok_own.shape[0]
    latents = count // SEQ
    return pl.pallas_call(
        forward_kernel,
        grid=(latents,),
        in_specs=[tiles(SEQ, HALF)] * 2 + [fixed(values) for values in vectors] + anywhere(4),
        out_specs=[tiles(SEQ, D), tiles(SEQ, 2 * SIDE), tiles(SEQ, D)],
        out_shape=[
            jax.ShapeDtypeStruct((count, D), B16),
            jax.ShapeDtypeStruct((count, 2 * SIDE), B16),
            jax.ShapeDtypeStruct((count, D), B16),
        ],
        scratch_shapes=[pltpu.VMEM((D, 2 * SIDE), B16), pltpu.SemaphoreType.DMA((12,))],
        compiler_params=params(),
        cost_estimate=pl.CostEstimate(
            flops=14 * 10**9, bytes_accessed=16 * 10**6, transcendentals=count * SEQ * 12
        ),
        name="forward",
    )(tok_own, tok_oth, *vectors, *pieces)


def call_middle(place, tok, cot, att, vectors, out_pieces, exp_pieces, shr_pieces):
    count = att.shape[0]
    latents = count // SEQ
    per_tile = PER_TILE if latents % PER_TILE == 0 else 1
    rows = per_tile * SEQ
    steps = latents // per_tile
    halves = [tiles(rows, HALF)] * 2

    def shape(width, kind=B16):
        return jax.ShapeDtypeStruct((count, width), kind)

    return pl.pallas_call(
        middle_kernel,
        grid=(steps,),
        in_specs=[pl.BlockSpec(memory_space=pltpu.SMEM)]
        + halves
        + halves
        + [tiles(rows, D)]
        + [fixed(values) for values in vectors]
        + anywhere(16),
        out_specs=halves
        + [tiles(rows, D)]
        + [tiles(rows, FF // 2)] * 4
        + [tiles(rows, D)] * 4
        + [stacked(per_tile, 4, D), stacked(1, 1, 2 * D + FF)],
        out_shape=[shape(HALF), shape(HALF), shape(D)]
        + [shape(FF // 2)] * 4
        + [shape(D), shape(D), shape(D, F32), shape(D)]
        + [
            jax.ShapeDtypeStruct((latents, 4, D), F32),
            jax.ShapeDtypeStruct((steps, 1, 2 * D + FF), F32),
        ],
        scratch_shapes=[
            pltpu.VMEM((D, D), B16),
            pltpu.VMEM((D, FF), B16),
            pltpu.VMEM((FF, D), B16),
            pltpu.SemaphoreType.DMA((4,)),
            pltpu.SemaphoreType.DMA((6,)),
            pltpu.SemaphoreType.DMA((6,)),
        ],
        compiler_params=params(),
        cost_estimate=pl.CostEstimate(
            flops=30 * 10**9, bytes_accessed=50 * 10**6, transcendentals=count * FF
        ),
        name="middle",
    )(place, *tok, *cot, att, *vectors, *out_pieces, *exp_pieces, *shr_pieces)


def call_backward(tok, vectors, qkv, d_att, d_mid, pieces):
    count = d_att.shape[0]
    latents = count // SEQ
    return pl.pallas_call(
        backward_kernel,
        grid=(latents,),
        in_specs=[tiles(SEQ, HALF)] * 2
        + [fixed(values) for values in vectors]
        + [tiles(SEQ, 2 * SIDE), tiles(SEQ, D), tiles(SEQ, D)]
        + anywhere(4),
        out_specs=[tiles(SEQ, SIDE)] * 2
        + [tiles(SEQ, HALF)] * 2
        + [stacked(1, 2, D), stacked(1, 1, 2 * SIDE)],
        out_shape=[jax.ShapeDtypeStruct((count, SIDE), B16)] * 2
        + [jax.ShapeDtypeStruct((count, HALF), B16)] * 2
        + [
            jax.ShapeDtypeStruct((latents, 2, D), F32),
            jax.ShapeDtypeStruct((latents, 1, 2 * SIDE), F32),
        ],
        scratch_shapes=[pltpu.VMEM((D, 2 * SIDE), B16), pltpu.SemaphoreType.DMA((12,))],
        compiler_params=params(),
        cost_estimate=pl.CostEstimate(
            flops=25 * 10**9, bytes_accessed=20 * 10**6, transcendentals=count * SEQ * 12
        ),
        name="backward",
    )(*tok, *vectors, qkv, d_att, d_mid, *pieces)


def swap_row(values):
    return lax.ppermute(values, "row", SWAP)


def swap_col(values):
    return lax.ppermute(values, "col", SWAP)


def swap_dp(values, distance):
    size = lax.axis_size("dp")
    return lax.ppermute(values, "dp", [(place, place ^ distance) for place in range(size)])


def distances():
    size = lax.axis_size("dp")
    return [1 << bit for bit in range(size.bit_length() - 1)]


def after(values, *earlier):
    return lax.optimization_barrier((values,) + earlier)[0]


def halves(values, dim):
    size = values.shape[dim] // 2
    return lax.slice_in_dim(values, 0, size, axis=dim), lax.slice_in_dim(
        values, size, 2 * size, axis=dim
    )


def pick(values, place, axis=0):
    size = values.shape[axis] // 2
    kept = lax.dynamic_slice_in_dim(values, place * size, size, axis)
    sent = lax.dynamic_slice_in_dim(values, (1 - place) * size, size, axis)
    return kept, sent


def in_order(place, mine, theirs):
    return jnp.concatenate(
        [jnp.where(place == 0, mine, theirs), jnp.where(place == 0, theirs, mine)], axis=0
    )


def x_place():
    return lax.axis_index("dp") % 2


def scatter_stage(values, distance, axis=0):
    place = (lax.axis_index("dp") // distance) % 2
    size = values.shape[axis] // 2
    kept = lax.dynamic_slice_in_dim(values, place * size, size, axis)
    sent = lax.dynamic_slice_in_dim(values, (1 - place) * size, size, axis)
    return kept + swap_dp(sent.astype(B16), distance).astype(F32)


def gather_dp(values):
    for distance in reversed(distances()):
        values = jnp.concatenate([values, swap_dp(values, distance)], axis=0)
    return values


def near_place():
    return jnp.full((1,), x_place(), jnp.int32)


def sum_place():
    me, mine = lax.axis_index("dp"), 0
    for distance in distances():
        mine = mine * 2 + (me // distance) % 2
    return jnp.full((1,), mine, jnp.int32)


def order_grid_kernel(mine, near, far, shr_out, out_out, exp_out):
    shr_rows, out_rows, exp_rows = shr_out.shape[1], out_out.shape[1], exp_out.shape[1]
    count = near.shape[0]
    for values, place in ((near, mine[0]), (far, 1 - mine[0])):
        for block in range(count):
            into = place * count + block
            shr_out[into] = values[block, :shr_rows].astype(F32)
            out_out[into] = values[block, shr_rows : shr_rows + out_rows].astype(F32)
            for part in range(exp_out.shape[2] // HALF):
                at = shr_rows + out_rows + part * exp_rows
                exp_out[into, :, part * HALF : (part + 1) * HALF] = values[
                    block, at : at + exp_rows
                ].astype(F32)


def order_attend_kernel(mine, near, far, out):
    count = near.shape[0]
    for number, values in enumerate((near, far)):
        for block in range(count):
            place = mine[0] ^ (number * count + block)
            for kind in range(out.shape[0]):
                out[kind, place] = values[block, :, kind * HALF : (kind + 1) * HALF].astype(F32)


def order(kernel, place, values, shapes):
    whole = [pl.BlockSpec(memory_space=pltpu.VMEM)]
    return pl.pallas_call(
        kernel,
        in_specs=[pl.BlockSpec(memory_space=pltpu.SMEM)] + whole * len(values),
        out_specs=whole * len(shapes),
        out_shape=[jax.ShapeDtypeStruct(shape, F32) for shape in shapes],
        compiler_params=pltpu.CompilerParams(vmem_limit_bytes=VMEM_BYTES),
        name="order",
    )(place, *values)


def shards(
    tokens, condition, adaptive, adabias, attend, attbias, outproj, outbias,
    expand, expbias, shrink, shrbias, cotangent,
):
    row = lax.axis_index("row")
    col = lax.axis_index("col")

    tok_own, sent = pick(tokens, row)
    tok_oth = swap_row(sent)
    tok = (tok_own, tok_oth)

    raw_condition = after(condition, sent).astype(F32)
    act_cond = jax.nn.silu(raw_condition).astype(B16)
    mod_terms = jnp.einsum("ld,kde->kle", act_cond, adaptive, preferred_element_type=F32)
    kept, sent = pick(mod_terms, col, 1)
    group = kept.shape[1]
    latents = group // 2
    col_own = jnp.concatenate([attbias, expbias.reshape(-1, HALF)], axis=0).astype(F32)
    col_own = jnp.pad(col_own, ((0, group - col_own.shape[0]), (0, 0)))[None]
    col_oth = swap_col(jnp.concatenate([sent, col_own], axis=0))
    mod_rows = kept + col_oth[:6] + adabias.astype(F32)[:, None]
    mod_own, sent = pick(mod_rows, row, 1)
    row_own = jnp.stack([outbias, shrbias]).astype(F32)
    row_own = jnp.pad(row_own, ((0, latents - 2), (0, 0)))[None]
    mod_oth = swap_row(jnp.concatenate([sent, row_own], axis=0))
    mods = (mod_own, mod_oth)

    def pieces(values, over):
        return values, over, swap_col(values), swap_col(over)

    def near(values):
        return pick(values, x_place())[0]

    cot_own, cot_sent = pick(cotangent, row)
    attend, _, _, exp_near, shr_near, cot_sent = lax.optimization_barrier(
        (attend, tok_oth, mod_oth, near(expand), near(shrink), cot_sent)
    )
    attend_pieces = pieces(attend, swap_row(attend))
    *attend_pieces, exp_near, shr_near = lax.optimization_barrier(
        (*attend_pieces, exp_near, shr_near)
    )
    exp_near, shr_near = swap_row(exp_near), swap_row(shr_near)
    first, qkv, attended = call_forward(
        tok_own, tok_oth, (*mods, col_own, col_oth), attend_pieces
    )
    attended, exp_near, shr_near, outproj, cot_sent, act_late = lax.optimization_barrier(
        (attended, exp_near, shr_near, outproj, cot_sent, act_cond)
    )
    cot_oth, out_over = swap_row(cot_sent), swap_row(outproj)
    exp_far, shr_far = swap_dp(exp_near, 1), swap_dp(shr_near, 1)
    early = [swap_col(values) for values in (expand, shrink, exp_near, shr_near)]
    cond_all = gather_dp(act_late)
    cot_oth, out_over, exp_far, shr_far, cond_all, *early = lax.optimization_barrier(
        (cot_oth, out_over, exp_far, shr_far, cond_all, *early)
    )
    exp_pieces = (expand, exp_near, exp_far, early[0], early[2], swap_col(exp_far))
    shr_pieces = (shrink, shr_near, shr_far, early[1], early[3], swap_col(shr_far))
    out_pieces = pieces(outproj, out_over)
    (
        res_own, res_oth, second, act_own, act_oth, dh_own, dh_oth, e_one, e_two,
        d_middle, d_attended, mod_late, sums_late,
    ) = call_middle(
        near_place(), tok, (cot_own, cot_oth), attended, (*mods, col_own, col_oth, row_own),
        out_pieces, exp_pieces, shr_pieces,
    )
    att_own, att_oth = halves(attended, 1)
    depth = act_oth.shape[1]
    shr_got = swap_col(
        jnp.concatenate(
            [dot_tn(act_oth, e_two).astype(B16), dot_tn(att_oth, e_one).astype(B16)], axis=0
        )
    )
    exp_got = swap_col(dot_tn(second, dh_oth).astype(B16))
    shr_total = dot_tn(act_own, e_two) + shr_got[:depth].astype(F32)
    out_total = dot_tn(att_own, e_one) + shr_got[depth:].astype(F32)
    exp_total = dot_tn(second, dh_own) + exp_got.astype(F32)
    d_attended, shr_total, out_total, exp_total = lax.optimization_barrier(
        (d_attended, shr_total, out_total, exp_total)
    )
    near_step, *far_steps = distances()
    size = lax.axis_size("dp")
    shr_mine, shr_theirs = [
        jnp.concatenate([part.reshape(size, -1, HALF) for part in parts], axis=1)
        for parts in zip(halves(shr_total, 1), halves(out_total, 1))
    ]
    shr_got = swap_row(shr_theirs.astype(B16))
    exp_kept, exp_sent = pick(exp_total.reshape(2, HALF, -1), x_place(), 1)
    exp_got = swap_dp(exp_sent.astype(B16), near_step)

    dqkv_own, dqkv_oth, grad_own, grad_oth, mod_early, sums_early = call_backward(
        tok, mods, qkv, d_attended, d_middle, attend_pieces
    )
    dqkv_own, dqkv_oth, shr_got, exp_got = lax.optimization_barrier(
        (dqkv_own, dqkv_oth, shr_got, exp_got)
    )
    att_got = swap_col(dot_tn(first, dqkv_oth).astype(B16)).astype(F32)
    exp_part = exp_kept + exp_got.astype(F32)
    shr_kept, shr_sent = pick(shr_mine + shr_got.astype(F32), x_place())
    exp_got = swap_row(exp_part[1].astype(B16))
    shr_got = swap_dp(shr_sent.astype(B16), near_step)
    att_total = dot_tn(first, dqkv_own) + att_got
    att_total, exp_got, shr_got, mod_early, grad_oth, res_oth = lax.optimization_barrier(
        (att_total, exp_got, shr_got, mod_early, grad_oth, res_oth)
    )
    att_mine, att_theirs = halves(att_total, 0)
    att_part = att_mine + swap_row(att_theirs.astype(B16)).astype(F32)
    exp_part = (exp_part[0] + exp_got.astype(F32)).astype(B16)
    exp_part = exp_part.reshape(size // 2, HALF // size, -1)
    grid_part = jnp.concatenate(
        [(shr_kept + shr_got.astype(F32)).astype(B16)]
        + [exp_part[:, :, at : at + HALF] for at in range(0, exp_part.shape[2], HALF)],
        axis=1,
    )
    grid_part = lax.psum(
        grid_part, "dp", axis_index_groups=[list(range(place, size, 2)) for place in range(2)]
    )

    d_modulation = jnp.concatenate([mod_early, mod_late], axis=1).astype(B16).astype(F32)
    sums_late = jnp.sum(sums_late, axis=(0, 1))
    sums_early = jnp.sum(sums_early, axis=(0, 1)).reshape(6, HALF)
    row_sums = sums_late[: 2 * D].reshape(2, 2, HALF)
    wide = sums_late[2 * D :].reshape(2, -1, HALF)
    col_sums = jnp.concatenate(
        [sums_early[0:3:2], wide[0], sums_early[3:6:2], wide[1]], axis=0
    )
    mine = d_modulation[:, :, :HALF].reshape(-1, HALF)
    theirs = d_modulation[:, :, HALF:].reshape(-1, HALF)
    got = swap_row(jnp.concatenate([theirs, row_sums[:, 1], col_sums], axis=0))
    rows = mine.shape[0]
    block = in_order(row, mine, got[:rows]).astype(B16)
    sums = jnp.concatenate([row_sums[:, 0], col_sums], axis=0) + got[rows:]
    high = sums.astype(B16)
    low = (sums - high.astype(F32)).astype(B16)
    width = block.shape[0] + 2 * sums.shape[0]
    packed = jnp.concatenate([block, high, low], axis=0)[None]
    att_part, packed, grad_oth, res_oth = lax.optimization_barrier(
        (att_part, packed, grad_oth, res_oth)
    )
    packed_all = gather_dp(packed)
    att_part = att_part.reshape(size, HALF // size, -1)
    for distance in distances():
        att_part = scatter_stage(att_part, distance)
    att_part, grid_part = lax.optimization_barrier((att_part.astype(B16), grid_part))
    for distance in reversed(far_steps):
        att_part = jnp.concatenate([att_part, swap_dp(att_part, distance)], axis=0)
    exp_width = expand.shape[1]
    shrink_grad, outproj_grad, expand_grad = order(
        order_grid_kernel,
        near_place(),
        (grid_part, swap_dp(grid_part, near_step)),
        [(size, depth // size, HALF), (size, HALF // size, HALF), (size, HALF // size, exp_width)],
    )
    shrink_grad, outproj_grad = [part.reshape(-1, HALF) for part in (shrink_grad, outproj_grad)]
    expand_grad = expand_grad.reshape(HALF, exp_width)
    (attend_grad,) = order(
        order_attend_kernel,
        sum_place(),
        (att_part, swap_dp(att_part, near_step)),
        [(3, size, HALF // size, HALF)],
    )
    attend_grad = attend_grad.reshape(3, HALF, HALF)
    block_all = packed_all[:, : block.shape[0]].reshape(-1, HALF)
    both_sums = jnp.sum(packed_all[:, block.shape[0] :].astype(F32), axis=0)
    sums = both_sums[: sums.shape[0]] + both_sums[sums.shape[0] :]
    count = col_sums.shape[0] // 2
    given = jnp.concatenate([sums[:2], sums[2 + count :]], axis=0)
    high = given.astype(B16)
    low = (given - high.astype(F32)).astype(B16)
    got = swap_col(jnp.concatenate([block_all, high, low], axis=0))
    other_all = got[: block_all.shape[0]]
    got = got[block_all.shape[0] :].astype(F32)
    sums = sums[: 2 + count] + got[: 2 + count] + got[2 + count :]
    outbias_grad, shrbias_grad = sums[0], sums[1]
    attbias_grad = sums[2:4]
    expbias_grad = sums[4:].reshape(-1)

    result = in_order(row, res_own, swap_row(res_oth))
    input_gradient = in_order(row, grad_own, swap_row(grad_oth))
    mod_all = jnp.concatenate([block_all, other_all], axis=0).reshape(-1, 6, HALF)
    cond_mine, cond_theirs = pick(
        cond_all.reshape(-1, 2 * group, HALF).transpose(1, 0, 2), col
    )
    cond_all = jnp.concatenate(
        [part.transpose(1, 0, 2).reshape(-1, HALF) for part in (cond_mine, cond_theirs)], axis=0
    )
    adabias_grad = jnp.sum(mod_all, axis=0, dtype=F32)
    adaptive_grad = jnp.einsum("ld,lke->kde", cond_all, mod_all, preferred_element_type=F32)
    mod_group = in_order(col, block, other_all[: block.shape[0]]).reshape(-1, 6, HALF)
    d_act = jnp.einsum("lke,kde->ld", mod_group, adaptive, preferred_element_type=F32)
    d_act = d_act + swap_row(d_act)
    condition_gradient = jax.vjp(jax.nn.silu, raw_condition)[1](d_act)[0].astype(B16)
    return (
        result, input_gradient, condition_gradient, adaptive_grad, adabias_grad, attend_grad,
        attbias_grad, outproj_grad, outbias_grad, expand_grad, expbias_grad, shrink_grad,
        shrbias_grad,
    )


def solution(mesh):
    placed = (
        P(("dp", "col"), "row"),
        P("dp", "col"),
        P(None, "col", "row"),
        P(None, "row"),
        P(None, "row", "col"),
        P(None, "col"),
        P("col", "row"),
        P("row"),
        P("row", "col"),
        P("col"),
        P("col", "row"),
        P("row"),
        P(("dp", "col"), "row"),
    )
    return jax.shard_map(
        shards,
        mesh=mesh,
        in_specs=placed,
        out_specs=(
            P(("dp", "col"), "row"),
            P(("dp", "col"), "row"),
            P("dp", "col"),
            P(None, "col", "row"),
            P(None, "row"),
            P(None, "row", "col"),
            P(None, "col"),
            P("col", "row"),
            P("row"),
            P("row", "col"),
            P("col"),
            P("col", "row"),
            P("row"),
        ),
        check_vma=False,
    )
```

```python
import functools

import jax
import jax.numpy as jnp
from jax import lax
from jax.experimental import pallas as pl
from jax.experimental.pallas import tpu as pltpu
from jax.sharding import PartitionSpec as P

D = 768
HALF = D // 2
FF = 3072
SEQ = 256
HEAD_DIM = 64
PAIR = 2 * HEAD_DIM
SIDE = 3 * HALF
EPS = 1e-06
F32 = jnp.float32
B16 = jnp.bfloat16
SWAP = ((0, 1), (1, 0))
SCALE = HEAD_DIM ** (-0.5)
ROOT = (2.0 / 3.141592653589793) ** 0.5
CUBE = 0.044715
PER_TILE = 2
VMEM_BYTES = 60 * 1024 * 1024


def dot(left, right):
    return jnp.dot(left, right, preferred_element_type=F32)


def dot_nt(left, right):
    return lax.dot_general(left, right, (((1,), (1,)), ((), ())), preferred_element_type=F32)


def dot_tn(left, right):
    return lax.dot_general(left, right, (((0,), (0,)), ((), ())), preferred_element_type=F32)


def normalize(values):
    center = jnp.mean(values, axis=1, keepdims=True)
    spread = jnp.mean(values * values, axis=1, keepdims=True) - center * center
    inverse = lax.rsqrt(spread + EPS)
    return (values - center) * inverse, inverse


def norm_grad(upstream, normal, inverse):
    first_mean = jnp.mean(upstream, axis=1, keepdims=True)
    second_mean = jnp.mean(upstream * normal, axis=1, keepdims=True)
    return inverse * (upstream - first_mean - normal * second_mean)


def both(own_ref, oth_ref):
    return jnp.concatenate([own_ref[...], oth_ref[...]], axis=1).astype(F32)


def line(ref, lead, number):
    return ref[lead, number : number + 1, :]


def spread_rows(mods, number, per_tile):
    own, oth = mods
    rows = []
    for latent in range(per_tile):
        at = pl.ds(pl.program_id(0) * per_tile + latent, 1)
        pair = jnp.concatenate([own[number, at, :], oth[number, at, :]], axis=1)
        rows.append(jnp.broadcast_to(pair, (SEQ, D)))
    return rows[0] if per_tile == 1 else jnp.concatenate(rows, axis=0)


def store_sums(out_ref, number, values):
    for latent in range(out_ref.shape[0]):
        out_ref[latent, number : number + 1, :] = jnp.sum(
            values[latent * SEQ : (latent + 1) * SEQ], axis=0, keepdims=True
        )


def attend_copies(pieces, weight, sem):
    copies = []
    for number, piece in enumerate(pieces):
        row, col = number % 2, number // 2
        for kind in range(3):
            copies.append(
                pltpu.make_async_copy(
                    piece.at[kind],
                    weight.at[pl.ds(row * HALF, HALF), pl.ds(col * SIDE + kind * HALF, HALF)],
                    sem.at[len(copies)],
                )
            )
    return copies


def grid_copies(pieces, weight, sem):
    copies = []
    for number, piece in enumerate(pieces):
        row, col = number % 2, number // 2
        across, down = piece.shape[1], piece.shape[0]
        copies.append(
            pltpu.make_async_copy(
                piece,
                weight.at[pl.ds(col * down, down), pl.ds(row * across, across)],
                sem.at[number],
            )
        )
    return copies


def relay_copies(place, pieces, weight, sem, first_is_row):
    copies = []
    for col in range(2):
        whole, near, far = pieces[3 * col : 3 * col + 3]
        down, across = whole.shape
        size = near.shape[0]
        for piece, row, start in (
            (whole, 0, 0),
            (near, 1, place * size),
            (far, 1, (1 - place) * size),
        ):
            top, left = (row, col) if first_is_row else (col, row)
            rows = pl.ds(pl.multiple_of(top * down + start, 16), piece.shape[0])
            copies.append(
                pltpu.make_async_copy(
                    piece, weight.at[rows, pl.ds(left * across, across)], sem.at[len(copies)]
                )
            )
    return copies


def forward_kernel(
    tok_own, tok_oth, mod_own, mod_oth, col_own, col_oth, w0, w1, w2, w3,
    first_ref, qkv_ref, att_ref, weight, sem,
):
    mod = (mod_own, mod_oth)

    @pl.when(pl.program_id(0) == 0)
    def _():
        copies = attend_copies((w0, w1, w2, w3), weight, sem)
        for copy in copies:
            copy.start()
        for copy in copies:
            copy.wait()

    normal, _ = normalize(both(tok_own, tok_oth))
    first = (normal * (1.0 + spread_rows(mod, 1, 1)) + spread_rows(mod, 0, 1)).astype(B16)
    first_ref[...] = first
    blank = jnp.zeros((1, HALF), F32)
    last = col_oth.shape[0] - 1
    bias = jnp.concatenate(
        [line(col_own, 0, 0), blank, line(col_own, 0, 1)]
        + [line(col_oth, last, 0), blank, line(col_oth, last, 1)],
        axis=1,
    )
    qkv_ref[...] = (dot(first, weight[...]) + bias).astype(B16)
    low = lax.broadcasted_iota(jnp.int32, (SEQ, PAIR), 1) < HEAD_DIM
    for col in range(2):
        for pair in range(HALF // PAIR):
            base = col * SIDE + pair * PAIR
            q_part = qkv_ref[:, base : base + PAIR] * SCALE
            k_part = qkv_ref[:, base + HALF : base + HALF + PAIR]
            v_part = qkv_ref[:, base + D : base + D + PAIR]
            outs = []
            for keep in (low, jnp.logical_not(low)):
                scores = dot_nt(jnp.where(keep, q_part, 0).astype(B16), k_part)
                exponent = jnp.exp(scores - jnp.max(scores, axis=1, keepdims=True))
                probs = exponent * (1.0 / jnp.sum(exponent, axis=1, keepdims=True))
                outs.append(dot(probs.astype(B16), v_part))
            at = col * HALF + pair * PAIR
            att_ref[:, at : at + PAIR] = jnp.where(low, outs[0], outs[1]).astype(B16)


def middle_kernel(
    place, tok_own, tok_oth, cot_own, cot_oth, att, mod_own, mod_oth, col_own, col_oth, row_own,
    o0, o1, o2, o3, x0, x1, x2, x3, x4, x5, s0, s1, s2, s3, s4, s5,
    res_own, res_oth, second_ref, act_own, act_oth, dh_own, dh_oth, e_one_ref, e_two_ref,
    d_mid_ref, d_att_ref, mod_ref, sum_ref,
    w_out, w_exp, w_shr, sem_out, sem_exp, sem_shr,
):
    @pl.when(pl.program_id(0) == 0)
    def _():
        copies = (
            grid_copies((o0, o1, o2, o3), w_out, sem_out)
            + relay_copies(place[0], (x0, x1, x2, x3, x4, x5), w_exp, sem_exp, True)
            + relay_copies(place[0], (s0, s1, s2, s3, s4, s5), w_shr, sem_shr, False)
        )
        for copy in copies:
            copy.start()
        for copy in copies:
            copy.wait()

    per_tile = mod_ref.shape[0]
    last = mod_oth.shape[0] - 1
    rows = functools.partial(spread_rows, (mod_own, mod_oth), per_tile=per_tile)
    outbias = jnp.concatenate([line(row_own, 0, 0), line(mod_oth, last, 0)], axis=1)
    shrbias = jnp.concatenate([line(row_own, 0, 1), line(mod_oth, last, 1)], axis=1)

    branch_one = dot(att[...], w_out[...]) + outbias
    middle = both(tok_own, tok_oth) + rows(2) * branch_one
    normal, inverse = normalize(middle)
    second = (normal * (1.0 + rows(4)) + rows(3)).astype(B16)
    second_ref[...] = second
    upstream = both(cot_own, cot_oth)
    e_two = (rows(5) * upstream).astype(B16)
    e_two_ref[...] = e_two
    branch_two = shrbias
    d_second = 0.0
    for part in range(FF // D):
        at = part * D
        owner, lead = (col_own, 0) if 2 * at < FF else (col_oth, col_oth.shape[0] - 1)
        number = 2 + 2 * (part % (FF // D // 2))
        expbias = jnp.concatenate(
            [line(owner, lead, number), line(owner, lead, number + 1)], axis=1
        )
        hidden = dot(second, w_exp[:, at : at + D]) + expbias
        square = hidden * hidden
        bend = jnp.tanh(hidden * (ROOT + (ROOT * CUBE) * square))
        share = 0.5 + 0.5 * bend
        active = (hidden * share).astype(B16)
        slope = share + (0.5 * hidden) * (1.0 - bend * bend) * (ROOT + (3.0 * ROOT * CUBE) * square)
        branch_two = branch_two + dot(active, w_shr[at : at + D, :])
        d_hidden = (dot_nt(e_two, w_shr[at : at + D, :]) * slope).astype(B16)
        d_second = d_second + dot_nt(d_hidden, w_exp[:, at : at + D])
        act_ref, dh_ref = (act_own, dh_own) if 2 * at < FF else (act_oth, dh_oth)
        into = at % (FF // 2)
        act_ref[:, into : into + D] = active
        dh_ref[:, into : into + D] = d_hidden
        sum_ref[0, :, 2 * D + at : 2 * D + at + D] = jnp.sum(
            d_hidden.astype(F32), axis=0, keepdims=True
        )
    result = (middle + rows(5) * branch_two).astype(B16)
    res_own[...] = result[:, :HALF]
    res_oth[...] = result[:, HALF:]
    store_sums(mod_ref, 3, upstream * branch_two)
    store_sums(mod_ref, 1, d_second)
    store_sums(mod_ref, 2, d_second * normal)
    d_middle = upstream + norm_grad(d_second * (1.0 + rows(4)), normal, inverse)
    d_mid_ref[...] = d_middle
    store_sums(mod_ref, 0, d_middle * branch_one)
    e_one = (rows(2) * d_middle).astype(B16)
    e_one_ref[...] = e_one
    d_att_ref[...] = dot_nt(e_one, w_out[...]).astype(B16)
    sum_ref[0, :, :D] = jnp.sum(e_one.astype(F32), axis=0, keepdims=True)
    sum_ref[0, :, D : 2 * D] = jnp.sum(e_two.astype(F32), axis=0, keepdims=True)


def backward_kernel(
    tok_own, tok_oth, mod_own, mod_oth, qkv, d_att, d_mid, w0, w1, w2, w3,
    dqkv_own, dqkv_oth, grad_own, grad_oth, mod_ref, sum_ref, weight, sem,
):
    mod = (mod_own, mod_oth)

    @pl.when(pl.program_id(0) == 0)
    def _():
        copies = attend_copies((w0, w1, w2, w3), weight, sem)
        for copy in copies:
            copy.start()
        for copy in copies:
            copy.wait()

    low = lax.broadcasted_iota(jnp.int32, (SEQ, PAIR), 1) < HEAD_DIM
    for col in range(2):
        out_ref = (dqkv_own, dqkv_oth)[col]
        for pair in range(HALF // PAIR):
            base = col * SIDE + pair * PAIR
            q_part = qkv[:, base : base + PAIR]
            k_part = qkv[:, base + HALF : base + HALF + PAIR]
            v_part = qkv[:, base + D : base + D + PAIR]
            d_part = d_att[:, col * HALF + pair * PAIR : col * HALF + (pair + 1) * PAIR]
            queries, keys, values = [], [], []
            for keep in (low, jnp.logical_not(low)):
                scores = dot_nt(jnp.where(keep, k_part * SCALE, 0).astype(B16), q_part)
                exponent = jnp.exp(scores - jnp.max(scores, axis=0, keepdims=True))
                probs = exponent * (1.0 / jnp.sum(exponent, axis=0, keepdims=True))
                d_probs = dot_nt(jnp.where(keep, v_part, 0).astype(B16), d_part)
                weighted = probs * d_probs
                d_scores = (weighted - probs * jnp.sum(weighted, axis=0, keepdims=True)).astype(B16)
                values.append(dot(probs.astype(B16), d_part))
                keys.append(dot(d_scores, q_part))
                queries.append(dot_tn(d_scores, k_part))
            for kind, (first, then, factor) in enumerate(
                ((*queries, SCALE), (*keys, SCALE), (*values, 1.0))
            ):
                at = kind * HALF + pair * PAIR
                piece = (jnp.where(low, first, then) * factor).astype(B16)
                out_ref[:, at : at + PAIR] = piece
                sum_ref[0, :, col * SIDE + at : col * SIDE + at + PAIR] = jnp.sum(
                    piece.astype(F32), axis=0, keepdims=True
                )
    d_first = dot_nt(dqkv_own[...], weight[:, :SIDE]) + dot_nt(dqkv_oth[...], weight[:, SIDE:])
    normal, inverse = normalize(both(tok_own, tok_oth))
    store_sums(mod_ref, 0, d_first)
    store_sums(mod_ref, 1, d_first * normal)
    grad = (
        d_mid[...] + norm_grad(d_first * (1.0 + spread_rows(mod, 1, 1)), normal, inverse)
    ).astype(B16)
    grad_own[...] = grad[:, :HALF]
    grad_oth[...] = grad[:, HALF:]


def tiles(rows, width):
    return pl.BlockSpec((rows, width), lambda step: (step, 0))


def stacked(count, rows, width):
    return pl.BlockSpec((count, rows, width), lambda step: (step, 0, 0))


def fixed(values):
    return pl.BlockSpec(values.shape, lambda step: (0,) * values.ndim)


def anywhere(count):
    return [pl.BlockSpec(memory_space=pl.ANY)] * count


def params():
    return pltpu.CompilerParams(
        vmem_limit_bytes=VMEM_BYTES, dimension_semantics=("arbitrary",)
    )


def call_forward(tok_own, tok_oth, vectors, pieces):
    count = tok_own.shape[0]
    latents = count // SEQ
    return pl.pallas_call(
        forward_kernel,
        grid=(latents,),
        in_specs=[tiles(SEQ, HALF)] * 2 + [fixed(values) for values in vectors] + anywhere(4),
        out_specs=[tiles(SEQ, D), tiles(SEQ, 2 * SIDE), tiles(SEQ, D)],
        out_shape=[
            jax.ShapeDtypeStruct((count, D), B16),
            jax.ShapeDtypeStruct((count, 2 * SIDE), B16),
            jax.ShapeDtypeStruct((count, D), B16),
        ],
        scratch_shapes=[pltpu.VMEM((D, 2 * SIDE), B16), pltpu.SemaphoreType.DMA((12,))],
        compiler_params=params(),
        cost_estimate=pl.CostEstimate(
            flops=14 * 10**9, bytes_accessed=16 * 10**6, transcendentals=count * SEQ * 12
        ),
        name="forward",
    )(tok_own, tok_oth, *vectors, *pieces)


def call_middle(place, tok, cot, att, vectors, out_pieces, exp_pieces, shr_pieces):
    count = att.shape[0]
    latents = count // SEQ
    per_tile = PER_TILE if latents % PER_TILE == 0 else 1
    rows = per_tile * SEQ
    steps = latents // per_tile
    halves = [tiles(rows, HALF)] * 2

    def shape(width, kind=B16):
        return jax.ShapeDtypeStruct((count, width), kind)

    return pl.pallas_call(
        middle_kernel,
        grid=(steps,),
        in_specs=[pl.BlockSpec(memory_space=pltpu.SMEM)]
        + halves
        + halves
        + [tiles(rows, D)]
        + [fixed(values) for values in vectors]
        + anywhere(16),
        out_specs=halves
        + [tiles(rows, D)]
        + [tiles(rows, FF // 2)] * 4
        + [tiles(rows, D)] * 4
        + [stacked(per_tile, 4, D), stacked(1, 1, 2 * D + FF)],
        out_shape=[shape(HALF), shape(HALF), shape(D)]
        + [shape(FF // 2)] * 4
        + [shape(D), shape(D), shape(D, F32), shape(D)]
        + [
            jax.ShapeDtypeStruct((latents, 4, D), F32),
            jax.ShapeDtypeStruct((steps, 1, 2 * D + FF), F32),
        ],
        scratch_shapes=[
            pltpu.VMEM((D, D), B16),
            pltpu.VMEM((D, FF), B16),
            pltpu.VMEM((FF, D), B16),
            pltpu.SemaphoreType.DMA((4,)),
            pltpu.SemaphoreType.DMA((6,)),
            pltpu.SemaphoreType.DMA((6,)),
        ],
        compiler_params=params(),
        cost_estimate=pl.CostEstimate(
            flops=30 * 10**9, bytes_accessed=50 * 10**6, transcendentals=count * FF
        ),
        name="middle",
    )(place, *tok, *cot, att, *vectors, *out_pieces, *exp_pieces, *shr_pieces)


def call_backward(tok, vectors, qkv, d_att, d_mid, pieces):
    count = d_att.shape[0]
    latents = count // SEQ
    return pl.pallas_call(
        backward_kernel,
        grid=(latents,),
        in_specs=[tiles(SEQ, HALF)] * 2
        + [fixed(values) for values in vectors]
        + [tiles(SEQ, 2 * SIDE), tiles(SEQ, D), tiles(SEQ, D)]
        + anywhere(4),
        out_specs=[tiles(SEQ, SIDE)] * 2
        + [tiles(SEQ, HALF)] * 2
        + [stacked(1, 2, D), stacked(1, 1, 2 * SIDE)],
        out_shape=[jax.ShapeDtypeStruct((count, SIDE), B16)] * 2
        + [jax.ShapeDtypeStruct((count, HALF), B16)] * 2
        + [
            jax.ShapeDtypeStruct((latents, 2, D), F32),
            jax.ShapeDtypeStruct((latents, 1, 2 * SIDE), F32),
        ],
        scratch_shapes=[pltpu.VMEM((D, 2 * SIDE), B16), pltpu.SemaphoreType.DMA((12,))],
        compiler_params=params(),
        cost_estimate=pl.CostEstimate(
            flops=25 * 10**9, bytes_accessed=20 * 10**6, transcendentals=count * SEQ * 12
        ),
        name="backward",
    )(*tok, *vectors, qkv, d_att, d_mid, *pieces)


def swap_row(values):
    return lax.ppermute(values, "row", SWAP)


def swap_col(values):
    return lax.ppermute(values, "col", SWAP)


def swap_dp(values, distance):
    size = lax.axis_size("dp")
    return lax.ppermute(values, "dp", [(place, place ^ distance) for place in range(size)])


def distances():
    size = lax.axis_size("dp")
    return [1 << bit for bit in range(size.bit_length() - 1)]


def after(values, *earlier):
    return lax.optimization_barrier((values,) + earlier)[0]


def halves(values, dim):
    size = values.shape[dim] // 2
    return lax.slice_in_dim(values, 0, size, axis=dim), lax.slice_in_dim(
        values, size, 2 * size, axis=dim
    )


def pick(values, place, axis=0):
    size = values.shape[axis] // 2
    kept = lax.dynamic_slice_in_dim(values, place * size, size, axis)
    sent = lax.dynamic_slice_in_dim(values, (1 - place) * size, size, axis)
    return kept, sent


def in_order(place, mine, theirs):
    return jnp.concatenate(
        [jnp.where(place == 0, mine, theirs), jnp.where(place == 0, theirs, mine)], axis=0
    )


def x_place():
    return lax.axis_index("dp") % 2


def scatter_stage(values, distance, axis=0):
    place = (lax.axis_index("dp") // distance) % 2
    size = values.shape[axis] // 2
    kept = lax.dynamic_slice_in_dim(values, place * size, size, axis)
    sent = lax.dynamic_slice_in_dim(values, (1 - place) * size, size, axis)
    return kept + swap_dp(sent.astype(B16), distance).astype(F32)


def far_groups():
    far = distances()[1:]
    return [far[at : at + 2] for at in range(0, len(far), 2)]


def around(group):
    if len(group) == 1:
        return [group[0]]
    return [group[1], group[0], group[0] + group[1]]


def scatter_group(values, group):
    me = lax.axis_index("dp")
    place = 0
    for distance in group:
        place = 2 * place + (me // distance) % 2
    size = values.shape[0] >> len(group)
    total = lax.dynamic_slice_in_dim(values, place * size, size, 0)
    for block, distance in enumerate(around(group), 1):
        sent = lax.dynamic_slice_in_dim(values, (place ^ block) * size, size, 0)
        total = total + swap_dp(sent.astype(B16), distance).astype(F32)
    return total


def gather_group(values, group):
    return jnp.concatenate(
        [values] + [swap_dp(values, distance) for distance in around(group)], axis=0
    )


def gather_far(values):
    for group in reversed(far_groups()):
        values = gather_group(values, group)
    return values


def gather_near(values):
    return jnp.concatenate([values, swap_dp(values, 1)], axis=0)


def near_place():
    return jnp.full((1,), x_place(), jnp.int32)


def sum_place():
    me, mine = lax.axis_index("dp"), 0
    for distance in distances():
        mine = mine * 2 + (me // distance) % 2
    return jnp.full((1,), mine, jnp.int32)


def order_grid_kernel(mine, p0, p1, p2, p3, shr_out, out_out, exp_out):
    shr_rows, out_rows, exp_rows = shr_out.shape[1], out_out.shape[1], exp_out.shape[1]
    index = 0
    for values in (p0, p1, p2, p3):
        for block in range(values.shape[0]):
            into = mine[0] ^ index
            index += 1
            shr_out[into] = values[block, :shr_rows].astype(F32)
            out_out[into] = values[block, shr_rows : shr_rows + out_rows].astype(F32)
            for part in range(exp_out.shape[2] // HALF):
                at = shr_rows + out_rows + part * exp_rows
                exp_out[into, :, part * HALF : (part + 1) * HALF] = values[
                    block, at : at + exp_rows
                ].astype(F32)


def order_attend_kernel(mine, near, far, out):
    count = near.shape[0]
    for number, values in enumerate((near, far)):
        for block in range(count):
            place = mine[0] ^ (number * count + block)
            for kind in range(out.shape[0]):
                out[kind, place] = values[block, :, kind * HALF : (kind + 1) * HALF].astype(F32)


def order(kernel, place, values, shapes):
    whole = [pl.BlockSpec(memory_space=pltpu.VMEM)]
    return pl.pallas_call(
        kernel,
        in_specs=[pl.BlockSpec(memory_space=pltpu.SMEM)] + whole * len(values),
        out_specs=whole * len(shapes),
        out_shape=[jax.ShapeDtypeStruct(shape, F32) for shape in shapes],
        compiler_params=pltpu.CompilerParams(vmem_limit_bytes=VMEM_BYTES),
        name="order",
    )(place, *values)


def shards(
    tokens, condition, adaptive, adabias, attend, attbias, outproj, outbias,
    expand, expbias, shrink, shrbias, cotangent,
):
    row = lax.axis_index("row")
    col = lax.axis_index("col")

    tok_own, sent = pick(tokens, row)
    tok_oth = swap_row(sent)
    tok = (tok_own, tok_oth)

    raw_condition = after(condition, sent).astype(F32)
    act_cond = jax.nn.silu(raw_condition).astype(B16)
    mod_terms = jnp.einsum("ld,kde->kle", act_cond, adaptive, preferred_element_type=F32)
    kept, sent = pick(mod_terms, col, 1)
    group = kept.shape[1]
    latents = group // 2
    col_own = jnp.concatenate([attbias, expbias.reshape(-1, HALF)], axis=0).astype(F32)
    col_own = jnp.pad(col_own, ((0, group - col_own.shape[0]), (0, 0)))[None]
    col_oth = swap_col(jnp.concatenate([sent, col_own], axis=0))
    mod_rows = kept + col_oth[:6] + adabias.astype(F32)[:, None]
    mod_own, sent = pick(mod_rows, row, 1)
    row_own = jnp.stack([outbias, shrbias]).astype(F32)
    row_own = jnp.pad(row_own, ((0, latents - 2), (0, 0)))[None]
    mod_oth = swap_row(jnp.concatenate([sent, row_own], axis=0))
    mods = (mod_own, mod_oth)

    def pieces(values, over):
        return values, over, swap_col(values), swap_col(over)

    def near(values):
        return pick(values, x_place())[0]

    cot_own, cot_sent = pick(cotangent, row)
    attend, _, _, exp_near, shr_near, cot_sent = lax.optimization_barrier(
        (attend, tok_oth, mod_oth, near(expand), near(shrink), cot_sent)
    )
    attend_pieces = pieces(attend, swap_row(attend))
    *attend_pieces, exp_near, shr_near = lax.optimization_barrier(
        (*attend_pieces, exp_near, shr_near)
    )
    exp_near, shr_near = swap_row(exp_near), swap_row(shr_near)
    first, qkv, attended = call_forward(
        tok_own, tok_oth, (*mods, col_own, col_oth), attend_pieces
    )
    attended, exp_near, shr_near, outproj, cot_sent = lax.optimization_barrier(
        (attended, exp_near, shr_near, outproj, cot_sent)
    )
    cot_oth, out_over = swap_row(cot_sent), swap_row(outproj)
    exp_far, shr_far = swap_dp(exp_near, 1), swap_dp(shr_near, 1)
    early = [swap_col(values) for values in (expand, shrink, exp_near, shr_near)]
    cot_oth, out_over, exp_far, shr_far, *early = lax.optimization_barrier(
        (cot_oth, out_over, exp_far, shr_far, *early)
    )
    exp_pieces = (expand, exp_near, exp_far, early[0], early[2], swap_col(exp_far))
    shr_pieces = (shrink, shr_near, shr_far, early[1], early[3], swap_col(shr_far))
    out_pieces = pieces(outproj, out_over)
    (
        res_own, res_oth, second, act_own, act_oth, dh_own, dh_oth, e_one, e_two,
        d_middle, d_attended, mod_late, sums_late,
    ) = call_middle(
        near_place(), tok, (cot_own, cot_oth), attended, (*mods, col_own, col_oth, row_own),
        out_pieces, exp_pieces, shr_pieces,
    )
    att_own, att_oth = halves(attended, 1)
    depth = act_oth.shape[1]
    shr_got = swap_col(
        jnp.concatenate(
            [dot_tn(act_oth, e_two).astype(B16), dot_tn(att_oth, e_one).astype(B16)], axis=0
        )
    )
    exp_got = swap_col(dot_tn(second, dh_oth).astype(B16))
    shr_total = dot_tn(act_own, e_two) + shr_got[:depth].astype(F32)
    out_total = dot_tn(att_own, e_one) + shr_got[depth:].astype(F32)
    exp_total = dot_tn(second, dh_own) + exp_got.astype(F32)
    d_attended, shr_total, out_total, exp_total = lax.optimization_barrier(
        (d_attended, shr_total, out_total, exp_total)
    )
    near_step, *far_steps = distances()
    size = lax.axis_size("dp")
    shr_mine, shr_theirs = [
        jnp.concatenate([part.reshape(size, -1, HALF) for part in parts], axis=1)
        for parts in zip(halves(shr_total, 1), halves(out_total, 1))
    ]
    shr_got = swap_row(shr_theirs.astype(B16))
    exp_kept, exp_sent = pick(exp_total.reshape(2, HALF, -1), x_place(), 1)
    exp_got = swap_dp(exp_sent.astype(B16), near_step)

    dqkv_own, dqkv_oth, grad_own, grad_oth, mod_early, sums_early = call_backward(
        tok, mods, qkv, d_attended, d_middle, attend_pieces
    )
    dqkv_own, dqkv_oth, shr_got, exp_got = lax.optimization_barrier(
        (dqkv_own, dqkv_oth, shr_got, exp_got)
    )
    att_got = swap_col(dot_tn(first, dqkv_oth).astype(B16)).astype(F32)
    exp_part = exp_kept + exp_got.astype(F32)
    shr_kept, shr_sent = pick(shr_mine + shr_got.astype(F32), x_place())
    exp_got = swap_row(exp_part[1].astype(B16))
    shr_got = swap_dp(shr_sent.astype(B16), near_step)
    att_total = dot_tn(first, dqkv_own) + att_got
    att_total, exp_got, shr_got, mod_early, act_late = lax.optimization_barrier(
        (att_total, exp_got, shr_got, mod_early, act_cond)
    )
    att_mine, att_theirs = halves(att_total, 0)
    att_part = att_mine + swap_row(att_theirs.astype(B16)).astype(F32)
    exp_part = exp_part[0] + exp_got.astype(F32)
    exp_part = exp_part.reshape(size // 2, HALF // size, -1)
    grid_part = jnp.concatenate(
        [shr_kept + shr_got.astype(F32)]
        + [exp_part[:, :, at : at + HALF] for at in range(0, exp_part.shape[2], HALF)],
        axis=1,
    )
    grid_part = scatter_stage(grid_part, far_steps[0])

    d_modulation = jnp.concatenate([mod_early, mod_late], axis=1).astype(B16).astype(F32)
    sums_late = jnp.sum(sums_late, axis=(0, 1))
    sums_early = jnp.sum(sums_early, axis=(0, 1)).reshape(6, HALF)
    row_sums = sums_late[: 2 * D].reshape(2, 2, HALF)
    wide = sums_late[2 * D :].reshape(2, -1, HALF)
    col_sums = jnp.concatenate(
        [sums_early[0:3:2], wide[0], sums_early[3:6:2], wide[1]], axis=0
    )
    mine = d_modulation[:, :, :HALF].reshape(-1, HALF)
    theirs = d_modulation[:, :, HALF:].reshape(-1, HALF)
    got = swap_row(jnp.concatenate([theirs, row_sums[:, 1], col_sums], axis=0))
    rows = mine.shape[0]
    block = in_order(row, mine, got[:rows]).astype(B16)
    sums = jnp.concatenate([row_sums[:, 0], col_sums], axis=0) + got[rows:]
    high = sums.astype(B16)
    low = (sums - high.astype(F32)).astype(B16)
    width = block.shape[0] + 2 * sums.shape[0]
    packed = jnp.concatenate([block, high, low], axis=0)[None]
    att_part, grid_part, packed, act_late, res_oth = lax.optimization_barrier(
        (att_part, grid_part, packed, act_late, res_oth)
    )

    res_got = swap_row(res_oth)
    att_part = scatter_stage(att_part.reshape(size, HALF // size, -1), near_step)
    for distance in far_steps[1:]:
        grid_part = scatter_stage(grid_part, distance)
    packed_all = gather_far(packed)
    att_part, near_one, packed_all, grad_oth = lax.optimization_barrier(
        (att_part, grid_part.astype(B16), packed_all, grad_oth)
    )

    grad_got = swap_row(grad_oth)
    for distance in reversed(far_steps[1:]):
        near_one = jnp.concatenate([near_one, swap_dp(near_one, distance)], axis=0)
    for places in far_groups():
        att_part = scatter_group(att_part, places)
    packed_all = gather_near(packed_all)
    att_near, near_one, packed_all, act_late = lax.optimization_barrier(
        (att_part.astype(B16), near_one, packed_all, act_late)
    )

    near_two = swap_dp(near_one, far_steps[0])
    far_one = swap_dp(near_one, near_step)
    att_near = gather_far(att_near)
    cond_all = gather_far(act_late)
    att_near, near_two, cond_all = lax.optimization_barrier((att_near, near_two, cond_all))

    far_two = swap_dp(near_two, near_step)
    att_far = swap_dp(att_near, near_step)
    cond_all = gather_near(cond_all)
    result = in_order(row, res_own, res_got)
    input_gradient = in_order(row, grad_own, grad_got)
    exp_width = expand.shape[1]
    shrink_grad, outproj_grad, expand_grad = order(
        order_grid_kernel,
        sum_place(),
        (near_one, near_two, far_one, far_two),
        [(size, depth // size, HALF), (size, HALF // size, HALF), (size, HALF // size, exp_width)],
    )
    shrink_grad, outproj_grad = [part.reshape(-1, HALF) for part in (shrink_grad, outproj_grad)]
    expand_grad = expand_grad.reshape(HALF, exp_width)
    (attend_grad,) = order(
        order_attend_kernel,
        sum_place(),
        (att_near, att_far),
        [(3, size, HALF // size, HALF)],
    )
    attend_grad = attend_grad.reshape(3, HALF, HALF)
    block_all = packed_all[:, : block.shape[0]].reshape(-1, HALF)
    both_sums = jnp.sum(packed_all[:, block.shape[0] :].astype(F32), axis=0)
    sums = both_sums[: sums.shape[0]] + both_sums[sums.shape[0] :]
    count = col_sums.shape[0] // 2
    given = jnp.concatenate([sums[:2], sums[2 + count :]], axis=0)
    high = given.astype(B16)
    low = (given - high.astype(F32)).astype(B16)
    got = swap_col(jnp.concatenate([block_all, high, low], axis=0))
    other_all = got[: block_all.shape[0]]
    got = got[block_all.shape[0] :].astype(F32)
    sums = sums[: 2 + count] + got[: 2 + count] + got[2 + count :]
    outbias_grad, shrbias_grad = sums[0], sums[1]
    attbias_grad = sums[2:4]
    expbias_grad = sums[4:].reshape(-1)

    mod_all = jnp.concatenate([block_all, other_all], axis=0).reshape(-1, 6, HALF)
    cond_mine, cond_theirs = pick(
        cond_all.reshape(-1, 2 * group, HALF).transpose(1, 0, 2), col
    )
    cond_all = jnp.concatenate(
        [part.transpose(1, 0, 2).reshape(-1, HALF) for part in (cond_mine, cond_theirs)], axis=0
    )
    adabias_grad = jnp.sum(mod_all, axis=0, dtype=F32)
    adaptive_grad = jnp.einsum("ld,lke->kde", cond_all, mod_all, preferred_element_type=F32)
    mod_group = in_order(col, block, other_all[: block.shape[0]]).reshape(-1, 6, HALF)
    d_act = jnp.einsum("lke,kde->ld", mod_group, adaptive, preferred_element_type=F32)
    d_act = d_act + swap_row(d_act)
    condition_gradient = jax.vjp(jax.nn.silu, raw_condition)[1](d_act)[0].astype(B16)
    return (
        result, input_gradient, condition_gradient, adaptive_grad, adabias_grad, attend_grad,
        attbias_grad, outproj_grad, outbias_grad, expand_grad, expbias_grad, shrink_grad,
        shrbias_grad,
    )


def solution(mesh):
    placed = (
        P(("dp", "col"), "row"),
        P("dp", "col"),
        P(None, "col", "row"),
        P(None, "row"),
        P(None, "row", "col"),
        P(None, "col"),
        P("col", "row"),
        P("row"),
        P("row", "col"),
        P("col"),
        P("col", "row"),
        P("row"),
        P(("dp", "col"), "row"),
    )
    return jax.shard_map(
        shards,
        mesh=mesh,
        in_specs=placed,
        out_specs=(
            P(("dp", "col"), "row"),
            P(("dp", "col"), "row"),
            P("dp", "col"),
            P(None, "col", "row"),
            P(None, "row"),
            P(None, "row", "col"),
            P(None, "col"),
            P("col", "row"),
            P("row"),
            P("row", "col"),
            P("col"),
            P("col", "row"),
            P("row"),
        ),
        check_vma=False,
    )
```

```python
import functools

import jax
import jax.numpy as jnp
from jax import lax
from jax.experimental import pallas as pl
from jax.experimental.pallas import tpu as pltpu
from jax.sharding import PartitionSpec as P

D = 768
HALF = D // 2
FF = 3072
SEQ = 256
HEAD_DIM = 64
PAIR = 2 * HEAD_DIM
SIDE = 3 * HALF
EPS = 1e-06
F32 = jnp.float32
B16 = jnp.bfloat16
SWAP = ((0, 1), (1, 0))
SCALE = HEAD_DIM ** (-0.5)
ROOT = (2.0 / 3.141592653589793) ** 0.5
CUBE = 0.044715
PER_TILE = 2
VMEM_BYTES = 60 * 1024 * 1024


def dot(left, right):
    return jnp.dot(left, right, preferred_element_type=F32)


def dot_nt(left, right):
    return lax.dot_general(left, right, (((1,), (1,)), ((), ())), preferred_element_type=F32)


def dot_tn(left, right):
    return lax.dot_general(left, right, (((0,), (0,)), ((), ())), preferred_element_type=F32)


def normalize(values):
    center = jnp.mean(values, axis=1, keepdims=True)
    spread = jnp.mean(values * values, axis=1, keepdims=True) - center * center
    inverse = lax.rsqrt(spread + EPS)
    return (values - center) * inverse, inverse


def norm_grad(upstream, normal, inverse):
    first_mean = jnp.mean(upstream, axis=1, keepdims=True)
    second_mean = jnp.mean(upstream * normal, axis=1, keepdims=True)
    return inverse * (upstream - first_mean - normal * second_mean)


def both(own_ref, oth_ref):
    return jnp.concatenate([own_ref[...], oth_ref[...]], axis=1).astype(F32)


def line(ref, lead, number):
    return ref[lead, number : number + 1, :]


def spread_rows(mods, number, per_tile, start=0):
    own, oth = mods
    rows = []
    for latent in range(per_tile):
        at = pl.ds((pl.program_id(0) + start) * per_tile + latent, 1)
        pair = jnp.concatenate([own[number, at, :], oth[number, at, :]], axis=1)
        rows.append(jnp.broadcast_to(pair, (SEQ, D)))
    return rows[0] if per_tile == 1 else jnp.concatenate(rows, axis=0)


def store_sums(out_ref, number, values):
    for latent in range(out_ref.shape[0]):
        out_ref[latent, number : number + 1, :] = jnp.sum(
            values[latent * SEQ : (latent + 1) * SEQ], axis=0, keepdims=True
        )


def attend_copies(pieces, weight, sem):
    copies = []
    for number, piece in enumerate(pieces):
        row, col = number % 2, number // 2
        for kind in range(3):
            copies.append(
                pltpu.make_async_copy(
                    piece.at[kind],
                    weight.at[pl.ds(row * HALF, HALF), pl.ds(col * SIDE + kind * HALF, HALF)],
                    sem.at[len(copies)],
                )
            )
    return copies


def grid_copies(pieces, weight, sem):
    copies = []
    for number, piece in enumerate(pieces):
        row, col = number % 2, number // 2
        across, down = piece.shape[1], piece.shape[0]
        copies.append(
            pltpu.make_async_copy(
                piece,
                weight.at[pl.ds(col * down, down), pl.ds(row * across, across)],
                sem.at[number],
            )
        )
    return copies


def relay_copies(place, pieces, weight, sem, first_is_row):
    copies = []
    for col in range(2):
        whole, near, far = pieces[3 * col : 3 * col + 3]
        down, across = whole.shape
        size = near.shape[0]
        for piece, row, start in (
            (whole, 0, 0),
            (near, 1, place * size),
            (far, 1, (1 - place) * size),
        ):
            top, left = (row, col) if first_is_row else (col, row)
            rows = pl.ds(pl.multiple_of(top * down + start, 16), piece.shape[0])
            copies.append(
                pltpu.make_async_copy(
                    piece, weight.at[rows, pl.ds(left * across, across)], sem.at[len(copies)]
                )
            )
    return copies


def forward_kernel(
    start, tok_own, tok_oth, mod_own, mod_oth, col_own, col_oth, w0, w1, w2, w3, *others
):
    first_ref, qkv_ref, att_ref, weight, sem = others[-5:]
    rows = functools.partial(spread_rows, (mod_own, mod_oth), per_tile=1, start=start)

    @pl.when(pl.program_id(0) == 0)
    def _():
        copies = attend_copies((w0, w1, w2, w3), weight, sem)
        for copy in copies:
            copy.start()
        for copy in copies:
            copy.wait()

    normal, _ = normalize(both(tok_own, tok_oth))
    first = (normal * (1.0 + rows(1)) + rows(0)).astype(B16)
    first_ref[...] = first
    blank = jnp.zeros((1, HALF), F32)
    last = col_oth.shape[0] - 1
    bias = jnp.concatenate(
        [line(col_own, 0, 0), blank, line(col_own, 0, 1)]
        + [line(col_oth, last, 0), blank, line(col_oth, last, 1)],
        axis=1,
    )
    qkv_ref[...] = (dot(first, weight[...]) + bias).astype(B16)
    low = lax.broadcasted_iota(jnp.int32, (SEQ, PAIR), 1) < HEAD_DIM
    for col in range(2):
        for pair in range(HALF // PAIR):
            base = col * SIDE + pair * PAIR
            q_part = qkv_ref[:, base : base + PAIR] * SCALE
            k_part = qkv_ref[:, base + HALF : base + HALF + PAIR]
            v_part = qkv_ref[:, base + D : base + D + PAIR]
            outs = []
            for keep in (low, jnp.logical_not(low)):
                scores = dot_nt(jnp.where(keep, q_part, 0).astype(B16), k_part)
                exponent = jnp.exp(scores - jnp.max(scores, axis=1, keepdims=True))
                probs = exponent * (1.0 / jnp.sum(exponent, axis=1, keepdims=True))
                outs.append(dot(probs.astype(B16), v_part))
            at = col * HALF + pair * PAIR
            att_ref[:, at : at + PAIR] = jnp.where(low, outs[0], outs[1]).astype(B16)


def middle_kernel(
    place, tok_own, tok_oth, cot_own, cot_oth, att, mod_own, mod_oth, col_own, col_oth, row_own,
    o0, o1, o2, o3, x0, x1, x2, x3, x4, x5, s0, s1, s2, s3, s4, s5,
    res_own, res_oth, second_ref, act_own, act_oth, dh_own, dh_oth, e_one_ref, e_two_ref,
    d_mid_ref, d_att_ref, mod_ref, sum_ref,
    w_out, w_exp, w_shr, sem_out, sem_exp, sem_shr,
):
    @pl.when(pl.program_id(0) == 0)
    def _():
        copies = (
            grid_copies((o0, o1, o2, o3), w_out, sem_out)
            + relay_copies(place[0], (x0, x1, x2, x3, x4, x5), w_exp, sem_exp, True)
            + relay_copies(place[0], (s0, s1, s2, s3, s4, s5), w_shr, sem_shr, False)
        )
        for copy in copies:
            copy.start()
        for copy in copies:
            copy.wait()

    per_tile = mod_ref.shape[0]
    last = mod_oth.shape[0] - 1
    rows = functools.partial(spread_rows, (mod_own, mod_oth), per_tile=per_tile)
    outbias = jnp.concatenate([line(row_own, 0, 0), line(mod_oth, last, 0)], axis=1)
    shrbias = jnp.concatenate([line(row_own, 0, 1), line(mod_oth, last, 1)], axis=1)

    branch_one = dot(att[...], w_out[...]) + outbias
    middle = both(tok_own, tok_oth) + rows(2) * branch_one
    normal, inverse = normalize(middle)
    second = (normal * (1.0 + rows(4)) + rows(3)).astype(B16)
    second_ref[...] = second
    upstream = both(cot_own, cot_oth)
    e_two = (rows(5) * upstream).astype(B16)
    e_two_ref[...] = e_two
    branch_two = shrbias
    d_second = 0.0
    for part in range(FF // D):
        at = part * D
        owner, lead = (col_own, 0) if 2 * at < FF else (col_oth, col_oth.shape[0] - 1)
        number = 2 + 2 * (part % (FF // D // 2))
        expbias = jnp.concatenate(
            [line(owner, lead, number), line(owner, lead, number + 1)], axis=1
        )
        hidden = dot(second, w_exp[:, at : at + D]) + expbias
        square = hidden * hidden
        bend = jnp.tanh(hidden * (ROOT + (ROOT * CUBE) * square))
        share = 0.5 + 0.5 * bend
        active = (hidden * share).astype(B16)
        slope = share + (0.5 * hidden) * (1.0 - bend * bend) * (ROOT + (3.0 * ROOT * CUBE) * square)
        branch_two = branch_two + dot(active, w_shr[at : at + D, :])
        d_hidden = (dot_nt(e_two, w_shr[at : at + D, :]) * slope).astype(B16)
        d_second = d_second + dot_nt(d_hidden, w_exp[:, at : at + D])
        act_ref, dh_ref = (act_own, dh_own) if 2 * at < FF else (act_oth, dh_oth)
        into = at % (FF // 2)
        act_ref[:, into : into + D] = active
        dh_ref[:, into : into + D] = d_hidden
        sum_ref[0, :, 2 * D + at : 2 * D + at + D] = jnp.sum(
            d_hidden.astype(F32), axis=0, keepdims=True
        )
    result = (middle + rows(5) * branch_two).astype(B16)
    res_own[...] = result[:, :HALF]
    res_oth[...] = result[:, HALF:]
    store_sums(mod_ref, 3, upstream * branch_two)
    store_sums(mod_ref, 1, d_second)
    store_sums(mod_ref, 2, d_second * normal)
    d_middle = upstream + norm_grad(d_second * (1.0 + rows(4)), normal, inverse)
    d_mid_ref[...] = d_middle
    store_sums(mod_ref, 0, d_middle * branch_one)
    e_one = (rows(2) * d_middle).astype(B16)
    e_one_ref[...] = e_one
    d_att_ref[...] = dot_nt(e_one, w_out[...]).astype(B16)
    sum_ref[0, :, :D] = jnp.sum(e_one.astype(F32), axis=0, keepdims=True)
    sum_ref[0, :, D : 2 * D] = jnp.sum(e_two.astype(F32), axis=0, keepdims=True)


def backward_kernel(qkv, d_att, dqkv_own, dqkv_oth, sum_ref):
    low = lax.broadcasted_iota(jnp.int32, (SEQ, PAIR), 1) < HEAD_DIM
    for col in range(2):
        out_ref = (dqkv_own, dqkv_oth)[col]
        for pair in range(HALF // PAIR):
            base = col * SIDE + pair * PAIR
            q_part = qkv[:, base : base + PAIR]
            k_part = qkv[:, base + HALF : base + HALF + PAIR]
            v_part = qkv[:, base + D : base + D + PAIR]
            d_part = d_att[:, col * HALF + pair * PAIR : col * HALF + (pair + 1) * PAIR]
            queries, keys, values = [], [], []
            for keep in (low, jnp.logical_not(low)):
                scores = dot_nt(jnp.where(keep, k_part * SCALE, 0).astype(B16), q_part)
                exponent = jnp.exp(scores - jnp.max(scores, axis=0, keepdims=True))
                probs = exponent * (1.0 / jnp.sum(exponent, axis=0, keepdims=True))
                d_probs = dot_nt(jnp.where(keep, v_part, 0).astype(B16), d_part)
                weighted = probs * d_probs
                d_scores = (weighted - probs * jnp.sum(weighted, axis=0, keepdims=True)).astype(B16)
                values.append(dot(probs.astype(B16), d_part))
                keys.append(dot(d_scores, q_part))
                queries.append(dot_tn(d_scores, k_part))
            for kind, (first, then, factor) in enumerate(
                ((*queries, SCALE), (*keys, SCALE), (*values, 1.0))
            ):
                at = kind * HALF + pair * PAIR
                piece = (jnp.where(low, first, then) * factor).astype(B16)
                out_ref[:, at : at + PAIR] = piece
                sum_ref[0, :, col * SIDE + at : col * SIDE + at + PAIR] = jnp.sum(
                    piece.astype(F32), axis=0, keepdims=True
                )


def project_kernel(
    tok_own, tok_oth, mod_own, mod_oth, dqkv_own, dqkv_oth, d_mid, w0, w1, w2, w3,
    grad_own, grad_oth, mod_ref, weight, sem,
):
    @pl.when(pl.program_id(0) == 0)
    def _():
        copies = attend_copies((w0, w1, w2, w3), weight, sem)
        for copy in copies:
            copy.start()
        for copy in copies:
            copy.wait()

    d_first = dot_nt(dqkv_own[...], weight[:, :SIDE]) + dot_nt(dqkv_oth[...], weight[:, SIDE:])
    normal, inverse = normalize(both(tok_own, tok_oth))
    store_sums(mod_ref, 0, d_first)
    store_sums(mod_ref, 1, d_first * normal)
    grad = (
        d_mid[...] + norm_grad(d_first * (1.0 + spread_rows((mod_own, mod_oth), 1, 1)), normal, inverse)
    ).astype(B16)
    grad_own[...] = grad[:, :HALF]
    grad_oth[...] = grad[:, HALF:]


def adaptive_kernel(cond, mods, out_ref):
    out_ref[0] = dot_tn(cond[...], mods[0])


def tiles(rows, width):
    return pl.BlockSpec((rows, width), lambda step: (step, 0))


def stacked(count, rows, width):
    return pl.BlockSpec((count, rows, width), lambda step: (step, 0, 0))


def fixed(values):
    return pl.BlockSpec(values.shape, lambda step: (0,) * values.ndim)


def anywhere(count):
    return [pl.BlockSpec(memory_space=pl.ANY)] * count


def params():
    return pltpu.CompilerParams(
        vmem_limit_bytes=VMEM_BYTES, dimension_semantics=("arbitrary",)
    )


def call_forward(tok_own, tok_oth, vectors, pieces, start, steps, before=()):
    count = tok_own.shape[0]

    def part(width):
        return pl.BlockSpec((SEQ, width), lambda step: (step + start, 0))

    inputs = (tok_own, tok_oth, *vectors, *pieces)
    return pl.pallas_call(
        functools.partial(forward_kernel, start),
        grid=(steps,),
        in_specs=[part(HALF)] * 2
        + [fixed(values) for values in vectors]
        + anywhere(4 + len(before)),
        out_specs=[part(D), part(2 * SIDE), part(D)],
        out_shape=[
            jax.ShapeDtypeStruct((count, D), B16),
            jax.ShapeDtypeStruct((count, 2 * SIDE), B16),
            jax.ShapeDtypeStruct((count, D), B16),
        ],
        input_output_aliases={len(inputs) + number: number for number in range(len(before))},
        scratch_shapes=[pltpu.VMEM((D, 2 * SIDE), B16), pltpu.SemaphoreType.DMA((12,))],
        compiler_params=params(),
        cost_estimate=pl.CostEstimate(
            flops=14 * 10**9 * steps // 4,
            bytes_accessed=16 * 10**6 * steps // 4,
            transcendentals=steps * SEQ * SEQ * 12,
        ),
        name="forward",
    )(*inputs, *before)


def call_middle(place, tok, cot, att, vectors, out_pieces, exp_pieces, shr_pieces):
    count = att.shape[0]
    latents = count // SEQ
    per_tile = PER_TILE if latents % PER_TILE == 0 else 1
    rows = per_tile * SEQ
    steps = latents // per_tile
    halves = [tiles(rows, HALF)] * 2

    def shape(width, kind=B16):
        return jax.ShapeDtypeStruct((count, width), kind)

    return pl.pallas_call(
        middle_kernel,
        grid=(steps,),
        in_specs=[pl.BlockSpec(memory_space=pltpu.SMEM)]
        + halves
        + halves
        + [tiles(rows, D)]
        + [fixed(values) for values in vectors]
        + anywhere(16),
        out_specs=halves
        + [tiles(rows, D)]
        + [tiles(rows, FF // 2)] * 4
        + [tiles(rows, D)] * 4
        + [stacked(per_tile, 4, D), stacked(1, 1, 2 * D + FF)],
        out_shape=[shape(HALF), shape(HALF), shape(D)]
        + [shape(FF // 2)] * 4
        + [shape(D), shape(D), shape(D, F32), shape(D)]
        + [
            jax.ShapeDtypeStruct((latents, 4, D), F32),
            jax.ShapeDtypeStruct((steps, 1, 2 * D + FF), F32),
        ],
        scratch_shapes=[
            pltpu.VMEM((D, D), B16),
            pltpu.VMEM((D, FF), B16),
            pltpu.VMEM((FF, D), B16),
            pltpu.SemaphoreType.DMA((4,)),
            pltpu.SemaphoreType.DMA((6,)),
            pltpu.SemaphoreType.DMA((6,)),
        ],
        compiler_params=params(),
        cost_estimate=pl.CostEstimate(
            flops=30 * 10**9, bytes_accessed=50 * 10**6, transcendentals=count * FF
        ),
        name="middle",
    )(place, *tok, *cot, att, *vectors, *out_pieces, *exp_pieces, *shr_pieces)


def call_backward(qkv, d_att):
    count = d_att.shape[0]
    latents = count // SEQ
    return pl.pallas_call(
        backward_kernel,
        grid=(latents,),
        in_specs=[tiles(SEQ, 2 * SIDE), tiles(SEQ, D)],
        out_specs=[tiles(SEQ, SIDE)] * 2 + [stacked(1, 1, 2 * SIDE)],
        out_shape=[jax.ShapeDtypeStruct((count, SIDE), B16)] * 2
        + [jax.ShapeDtypeStruct((latents, 1, 2 * SIDE), F32)],
        compiler_params=params(),
        cost_estimate=pl.CostEstimate(
            flops=20 * 10**9, bytes_accessed=16 * 10**6, transcendentals=count * SEQ * 12
        ),
        name="backward",
    )(qkv, d_att)


def call_project(tok, vectors, dqkv_own, dqkv_oth, d_mid, pieces):
    count = d_mid.shape[0]
    latents = count // SEQ
    return pl.pallas_call(
        project_kernel,
        grid=(latents,),
        in_specs=[tiles(SEQ, HALF)] * 2
        + [fixed(values) for values in vectors]
        + [tiles(SEQ, SIDE)] * 2
        + [tiles(SEQ, D)]
        + anywhere(4),
        out_specs=[tiles(SEQ, HALF)] * 2 + [stacked(1, 2, D)],
        out_shape=[jax.ShapeDtypeStruct((count, HALF), B16)] * 2
        + [jax.ShapeDtypeStruct((latents, 2, D), F32)],
        scratch_shapes=[pltpu.VMEM((D, 2 * SIDE), B16), pltpu.SemaphoreType.DMA((12,))],
        compiler_params=params(),
        cost_estimate=pl.CostEstimate(
            flops=7 * 10**9, bytes_accessed=16 * 10**6, transcendentals=count
        ),
        name="project",
    )(*tok, *vectors, dqkv_own, dqkv_oth, d_mid, *pieces)


def call_adaptive(cond, mods):
    latents, width = cond.shape
    kinds = mods.shape[0]
    return pl.pallas_call(
        adaptive_kernel,
        grid=(kinds,),
        in_specs=[
            pl.BlockSpec((latents, width), lambda step: (0, 0)),
            stacked(1, latents, HALF),
        ],
        out_specs=stacked(1, width, HALF),
        out_shape=jax.ShapeDtypeStruct((kinds, width, HALF), F32),
        compiler_params=params(),
        name="adaptive",
    )(cond, mods)


def swap_row(values):
    return lax.ppermute(values, "row", SWAP)


def swap_col(values):
    return lax.ppermute(values, "col", SWAP)


def swap_dp(values, distance):
    size = lax.axis_size("dp")
    return lax.ppermute(values, "dp", [(place, place ^ distance) for place in range(size)])


def distances():
    size = lax.axis_size("dp")
    return [1 << bit for bit in range(size.bit_length() - 1)]


def after(values, *earlier):
    return lax.optimization_barrier((values,) + earlier)[0]


def halves(values, dim):
    size = values.shape[dim] // 2
    return lax.slice_in_dim(values, 0, size, axis=dim), lax.slice_in_dim(
        values, size, 2 * size, axis=dim
    )


def pick(values, place, axis=0):
    size = values.shape[axis] // 2
    kept = lax.dynamic_slice_in_dim(values, place * size, size, axis)
    sent = lax.dynamic_slice_in_dim(values, (1 - place) * size, size, axis)
    return kept, sent


def in_order(place, mine, theirs):
    return jnp.concatenate(
        [jnp.where(place == 0, mine, theirs), jnp.where(place == 0, theirs, mine)], axis=0
    )


def x_place():
    return lax.axis_index("dp") % 2


def scatter_stage(values, distance, axis=0):
    place = (lax.axis_index("dp") // distance) % 2
    size = values.shape[axis] // 2
    kept = lax.dynamic_slice_in_dim(values, place * size, size, axis)
    sent = lax.dynamic_slice_in_dim(values, (1 - place) * size, size, axis)
    return kept + swap_dp(sent.astype(B16), distance).astype(F32)


def far_groups():
    far = distances()[1:]
    return [far[at : at + 2] for at in range(0, len(far), 2)]


def around(group):
    if len(group) == 1:
        return [group[0]]
    return [group[1], group[0], group[0] + group[1]]


def scatter_group(values, group):
    me = lax.axis_index("dp")
    place = 0
    for distance in group:
        place = 2 * place + (me // distance) % 2
    size = values.shape[0] >> len(group)
    total = lax.dynamic_slice_in_dim(values, place * size, size, 0)
    for block, distance in enumerate(around(group), 1):
        sent = lax.dynamic_slice_in_dim(values, (place ^ block) * size, size, 0)
        total = total + swap_dp(sent.astype(B16), distance).astype(F32)
    return total


def gather_group(values, group):
    return jnp.concatenate(
        [values] + [swap_dp(values, distance) for distance in around(group)], axis=0
    )


def gather_far(values):
    for group in reversed(far_groups()):
        values = gather_group(values, group)
    return values


def gather_near(values):
    return jnp.concatenate([values, swap_dp(values, 1)], axis=0)


def near_place():
    return jnp.full((1,), x_place(), jnp.int32)


def sum_place():
    me, mine = lax.axis_index("dp"), 0
    for distance in distances():
        mine = mine * 2 + (me // distance) % 2
    return jnp.full((1,), mine, jnp.int32)


def order_grid_kernel(mine, p0, p1, p2, p3, shr_out, out_out, exp_out):
    shr_rows, out_rows, exp_rows = shr_out.shape[1], out_out.shape[1], exp_out.shape[1]
    index = 0
    for values in (p0, p1, p2, p3):
        for block in range(values.shape[0]):
            into = mine[0] ^ index
            index += 1
            shr_out[into] = values[block, :shr_rows].astype(F32)
            out_out[into] = values[block, shr_rows : shr_rows + out_rows].astype(F32)
            for part in range(exp_out.shape[2] // HALF):
                at = shr_rows + out_rows + part * exp_rows
                exp_out[into, :, part * HALF : (part + 1) * HALF] = values[
                    block, at : at + exp_rows
                ].astype(F32)


def order_attend_kernel(mine, near, far, out):
    count = near.shape[0]
    for number, values in enumerate((near, far)):
        for block in range(count):
            place = mine[0] ^ (number * count + block)
            for kind in range(out.shape[0]):
                out[kind, place] = values[block, :, kind * HALF : (kind + 1) * HALF].astype(F32)


def order(kernel, place, values, shapes):
    whole = [pl.BlockSpec(memory_space=pltpu.VMEM)]
    return pl.pallas_call(
        kernel,
        in_specs=[pl.BlockSpec(memory_space=pltpu.SMEM)] + whole * len(values),
        out_specs=whole * len(shapes),
        out_shape=[jax.ShapeDtypeStruct(shape, F32) for shape in shapes],
        compiler_params=pltpu.CompilerParams(vmem_limit_bytes=VMEM_BYTES),
        name="order",
    )(place, *values)


def shards(
    tokens, condition, adaptive, adabias, attend, attbias, outproj, outbias,
    expand, expbias, shrink, shrbias, cotangent,
):
    row = lax.axis_index("row")
    col = lax.axis_index("col")

    tok_own, sent = pick(tokens, row)
    tok_oth = swap_row(sent)
    tok = (tok_own, tok_oth)

    raw_condition = after(condition, sent).astype(F32)
    act_cond = jax.nn.silu(raw_condition).astype(B16)
    mod_terms = jnp.einsum("ld,kde->kle", act_cond, adaptive, preferred_element_type=F32)
    kept, sent = pick(mod_terms, col, 1)
    group = kept.shape[1]
    latents = group // 2
    col_own = jnp.concatenate([attbias, expbias.reshape(-1, HALF)], axis=0).astype(F32)
    col_own = jnp.pad(col_own, ((0, group - col_own.shape[0]), (0, 0)))[None]
    col_oth = swap_col(jnp.concatenate([sent, col_own], axis=0))
    mod_rows = kept + col_oth[:6] + adabias.astype(F32)[:, None]
    mod_own, sent = pick(mod_rows, row, 1)
    row_own = jnp.stack([outbias, shrbias]).astype(F32)
    row_own = jnp.pad(row_own, ((0, latents - 2), (0, 0)))[None]
    mod_oth = swap_row(jnp.concatenate([sent, row_own], axis=0))
    mods = (mod_own, mod_oth)

    def pieces(values, over):
        return values, over, swap_col(values), swap_col(over)

    def near(values):
        return pick(values, x_place())[0]

    cot_own, cot_sent = pick(cotangent, row)
    attend, _, _, exp_near, shr_near, cot_sent, cond_all = lax.optimization_barrier(
        (attend, tok_oth, mod_oth, near(expand), near(shrink), cot_sent, gather_far(act_cond))
    )
    attend_pieces = pieces(attend, swap_row(attend))
    cond_all = gather_near(cond_all)
    *attend_pieces, exp_near, shr_near, cond_all = lax.optimization_barrier(
        (*attend_pieces, exp_near, shr_near, cond_all)
    )
    exp_near = swap_row(exp_near)
    vectors = (*mods, col_own, col_oth)
    half = latents // 2
    *begun, exp_near, shr_near = lax.optimization_barrier(
        (*call_forward(tok_own, tok_oth, vectors, attend_pieces, 0, half), exp_near, shr_near)
    )
    shr_near, exp_far = swap_row(shr_near), swap_dp(exp_near, 1)
    first, qkv, attended = call_forward(
        tok_own, tok_oth, vectors, attend_pieces, half, latents - half, begun
    )
    attended, exp_far, shr_near, outproj, cot_sent = lax.optimization_barrier(
        (attended, exp_far, shr_near, outproj, cot_sent)
    )
    cot_oth, out_over = swap_row(cot_sent), swap_row(outproj)
    shr_far = swap_dp(shr_near, 1)
    early = [swap_col(values) for values in (expand, shrink, exp_near, shr_near)]
    cot_oth, out_over, exp_far, shr_far, *early = lax.optimization_barrier(
        (cot_oth, out_over, exp_far, shr_far, *early)
    )
    exp_pieces = (expand, exp_near, exp_far, early[0], early[2], swap_col(exp_far))
    shr_pieces = (shrink, shr_near, shr_far, early[1], early[3], swap_col(shr_far))
    out_pieces = pieces(outproj, out_over)
    (
        res_own, res_oth, second, act_own, act_oth, dh_own, dh_oth, e_one, e_two,
        d_middle, d_attended, mod_late, sums_late,
    ) = call_middle(
        near_place(), tok, (cot_own, cot_oth), attended, (*mods, col_own, col_oth, row_own),
        out_pieces, exp_pieces, shr_pieces,
    )
    att_own, att_oth = halves(attended, 1)
    depth = act_oth.shape[1]
    shr_got = swap_col(
        jnp.concatenate(
            [dot_tn(act_oth, e_two).astype(B16), dot_tn(att_oth, e_one).astype(B16)], axis=0
        )
    )
    exp_got = swap_col(dot_tn(second, dh_oth).astype(B16))
    shr_total = dot_tn(act_own, e_two) + shr_got[:depth].astype(F32)
    out_total = dot_tn(att_own, e_one) + shr_got[depth:].astype(F32)
    exp_total = dot_tn(second, dh_own) + exp_got.astype(F32)
    near_step, *far_steps = distances()
    size = lax.axis_size("dp")
    shr_mine, shr_theirs = [
        jnp.concatenate([part.reshape(size, -1, HALF) for part in parts], axis=1)
        for parts in zip(halves(shr_total, 1), halves(out_total, 1))
    ]
    d_attended, shr_mine, shr_theirs, exp_total = lax.optimization_barrier(
        (d_attended, shr_mine, shr_theirs.astype(B16), exp_total)
    )
    shr_got = swap_row(shr_theirs)
    exp_kept, exp_sent = pick(exp_total.reshape(2, HALF, -1), x_place(), 1)
    exp_got = swap_dp(exp_sent.astype(B16), near_step)

    dqkv_own, dqkv_oth, sums_early = call_backward(qkv, d_attended)
    dqkv_own, dqkv_oth, shr_got, exp_got = lax.optimization_barrier(
        (dqkv_own, dqkv_oth, shr_got, exp_got)
    )
    att_got = swap_col(dot_tn(first, dqkv_oth).astype(B16)).astype(F32)
    exp_part = exp_kept + exp_got.astype(F32)
    shr_kept, shr_sent = pick(shr_mine + shr_got.astype(F32), x_place())
    exp_got = swap_row(exp_part[1].astype(B16))
    shr_got = swap_dp(shr_sent.astype(B16), near_step)
    att_total = dot_tn(first, dqkv_own) + att_got
    att_total, exp_got, shr_got, d_middle = lax.optimization_barrier(
        (att_total, exp_got, shr_got, d_middle)
    )
    att_mine, att_theirs = halves(att_total, 0)
    att_part = att_mine + swap_row(att_theirs.astype(B16)).astype(F32)
    exp_part = exp_part[0] + exp_got.astype(F32)
    exp_part = exp_part.reshape(size // 2, HALF // size, -1)
    grid_part = jnp.concatenate(
        [shr_kept + shr_got.astype(F32)]
        + [exp_part[:, :, at : at + HALF] for at in range(0, exp_part.shape[2], HALF)],
        axis=1,
    )
    grid_part = scatter_stage(grid_part, far_steps[0])

    grad_own, grad_oth, mod_early = call_project(
        tok, mods, dqkv_own, dqkv_oth, d_middle, attend_pieces
    )
    att_part, grid_part, mod_early, res_oth = lax.optimization_barrier(
        (att_part, grid_part, mod_early, res_oth)
    )

    d_modulation = jnp.concatenate([mod_early, mod_late], axis=1).astype(B16).astype(F32)
    sums_late = jnp.sum(sums_late, axis=(0, 1))
    sums_early = jnp.sum(sums_early, axis=(0, 1)).reshape(6, HALF)
    row_sums = sums_late[: 2 * D].reshape(2, 2, HALF)
    wide = sums_late[2 * D :].reshape(2, -1, HALF)
    col_sums = jnp.concatenate(
        [sums_early[0:3:2], wide[0], sums_early[3:6:2], wide[1]], axis=0
    )
    mine = d_modulation[:, :, :HALF].reshape(-1, HALF)
    theirs = d_modulation[:, :, HALF:].reshape(-1, HALF)
    got = swap_row(jnp.concatenate([theirs, row_sums[:, 1], col_sums], axis=0))
    rows = mine.shape[0]
    block = in_order(row, mine, got[:rows]).astype(B16)
    sums = jnp.concatenate([row_sums[:, 0], col_sums], axis=0) + got[rows:]
    high = sums.astype(B16)
    low = (sums - high.astype(F32)).astype(B16)
    width = block.shape[0] + 2 * sums.shape[0]
    packed = jnp.concatenate([block, high, low], axis=0)[None]

    res_got = swap_row(res_oth)
    att_part = scatter_stage(att_part.reshape(size, HALF // size, -1), near_step)
    for distance in far_steps[1:]:
        grid_part = scatter_stage(grid_part, distance)
    att_part, near_one, packed, grad_oth = lax.optimization_barrier(
        (att_part, grid_part.astype(B16), packed, grad_oth)
    )

    grad_got = swap_row(grad_oth)
    for distance in reversed(far_steps[1:]):
        near_one = jnp.concatenate([near_one, swap_dp(near_one, distance)], axis=0)
    for places in far_groups():
        att_part = scatter_group(att_part, places)
    packed_all = gather_far(packed)
    att_near, near_one, packed_all = lax.optimization_barrier(
        (att_part.astype(B16), near_one, packed_all)
    )

    near_two = swap_dp(near_one, far_steps[0])
    far_one = swap_dp(near_one, near_step)
    att_near = gather_far(att_near)
    packed_all = gather_near(packed_all)
    att_near, near_two, packed_all = lax.optimization_barrier((att_near, near_two, packed_all))

    far_two = swap_dp(near_two, near_step)
    att_far = swap_dp(att_near, near_step)
    result = in_order(row, res_own, res_got)
    input_gradient = in_order(row, grad_own, grad_got)
    exp_width = expand.shape[1]
    shrink_grad, outproj_grad, expand_grad = order(
        order_grid_kernel,
        sum_place(),
        (near_one, near_two, far_one, far_two),
        [(size, depth // size, HALF), (size, HALF // size, HALF), (size, HALF // size, exp_width)],
    )
    shrink_grad, outproj_grad = [part.reshape(-1, HALF) for part in (shrink_grad, outproj_grad)]
    expand_grad = expand_grad.reshape(HALF, exp_width)
    (attend_grad,) = order(
        order_attend_kernel,
        sum_place(),
        (att_near, att_far),
        [(3, size, HALF // size, HALF)],
    )
    attend_grad = attend_grad.reshape(3, HALF, HALF)
    block_all = packed_all[:, : block.shape[0]].reshape(-1, HALF)
    both_sums = jnp.sum(packed_all[:, block.shape[0] :].astype(F32), axis=0)
    sums = both_sums[: sums.shape[0]] + both_sums[sums.shape[0] :]
    count = col_sums.shape[0] // 2
    given = jnp.concatenate([sums[:2], sums[2 + count :]], axis=0)
    high = given.astype(B16)
    low = (given - high.astype(F32)).astype(B16)
    got = swap_col(jnp.concatenate([block_all, high, low], axis=0))
    other_all = got[: block_all.shape[0]]
    got = got[block_all.shape[0] :].astype(F32)
    sums = sums[: 2 + count] + got[: 2 + count] + got[2 + count :]
    outbias_grad, shrbias_grad = sums[0], sums[1]
    attbias_grad = sums[2:4]
    expbias_grad = sums[4:].reshape(-1)

    mod_all = jnp.concatenate([block_all, other_all], axis=0).reshape(-1, 6, HALF)
    cond_mine, cond_theirs = pick(
        cond_all.reshape(-1, 2 * group, HALF).transpose(1, 0, 2), col
    )
    cond_all = jnp.concatenate(
        [part.transpose(1, 0, 2).reshape(-1, HALF) for part in (cond_mine, cond_theirs)], axis=0
    )
    adabias_grad = jnp.sum(mod_all, axis=0, dtype=F32)
    adaptive_grad = call_adaptive(cond_all, mod_all.transpose(1, 0, 2))
    mod_group = in_order(col, block, other_all[: block.shape[0]]).reshape(-1, 6, HALF)
    d_act = jnp.einsum("lke,kde->ld", mod_group, adaptive, preferred_element_type=F32)
    d_act = d_act + swap_row(d_act)
    condition_gradient = jax.vjp(jax.nn.silu, raw_condition)[1](d_act)[0].astype(B16)
    return (
        result, input_gradient, condition_gradient, adaptive_grad, adabias_grad, attend_grad,
        attbias_grad, outproj_grad, outbias_grad, expand_grad, expbias_grad, shrink_grad,
        shrbias_grad,
    )


def solution(mesh):
    placed = (
        P(("dp", "col"), "row"),
        P("dp", "col"),
        P(None, "col", "row"),
        P(None, "row"),
        P(None, "row", "col"),
        P(None, "col"),
        P("col", "row"),
        P("row"),
        P("row", "col"),
        P("col"),
        P("col", "row"),
        P("row"),
        P(("dp", "col"), "row"),
    )
    return jax.shard_map(
        shards,
        mesh=mesh,
        in_specs=placed,
        out_specs=(
            P(("dp", "col"), "row"),
            P(("dp", "col"), "row"),
            P("dp", "col"),
            P(None, "col", "row"),
            P(None, "row"),
            P(None, "row", "col"),
            P(None, "col"),
            P("col", "row"),
            P("row"),
            P("row", "col"),
            P("col"),
            P("col", "row"),
            P("row"),
        ),
        check_vma=False,
    )
```

```python
import functools

import jax
import jax.numpy as jnp
from jax import lax
from jax.experimental import pallas as pl
from jax.experimental.pallas import tpu as pltpu
from jax.sharding import PartitionSpec as P

D = 768
HALF = D // 2
FF = 3072
SEQ = 256
HEAD_DIM = 64
PAIR = 2 * HEAD_DIM
SIDE = 3 * HALF
EPS = 1e-06
F32 = jnp.float32
B16 = jnp.bfloat16
SWAP = ((0, 1), (1, 0))
SCALE = HEAD_DIM ** (-0.5)
ROOT = (2.0 / 3.141592653589793) ** 0.5
CUBE = 0.044715
PER_TILE = 2
VMEM_BYTES = 60 * 1024 * 1024


def dot(left, right):
    return jnp.dot(left, right, preferred_element_type=F32)


def dot_nt(left, right):
    return lax.dot_general(left, right, (((1,), (1,)), ((), ())), preferred_element_type=F32)


def dot_tn(left, right):
    return lax.dot_general(left, right, (((0,), (0,)), ((), ())), preferred_element_type=F32)


def normalize(values):
    center = jnp.mean(values, axis=1, keepdims=True)
    spread = jnp.mean(values * values, axis=1, keepdims=True) - center * center
    inverse = lax.rsqrt(spread + EPS)
    return (values - center) * inverse, inverse


def norm_grad(upstream, normal, inverse):
    first_mean = jnp.mean(upstream, axis=1, keepdims=True)
    second_mean = jnp.mean(upstream * normal, axis=1, keepdims=True)
    return inverse * (upstream - first_mean - normal * second_mean)


def both(own_ref, oth_ref):
    return jnp.concatenate([own_ref[...], oth_ref[...]], axis=1).astype(F32)


def line(ref, lead, number):
    return ref[lead, number : number + 1, :]


def spread_rows(mods, number, per_tile, start=0):
    own, oth = mods
    rows = []
    for latent in range(per_tile):
        at = pl.ds((pl.program_id(0) + start) * per_tile + latent, 1)
        pair = jnp.concatenate([own[number, at, :], oth[number, at, :]], axis=1)
        rows.append(jnp.broadcast_to(pair, (SEQ, D)))
    return rows[0] if per_tile == 1 else jnp.concatenate(rows, axis=0)


def store_sums(out_ref, number, values):
    for latent in range(out_ref.shape[0]):
        out_ref[latent, number : number + 1, :] = jnp.sum(
            values[latent * SEQ : (latent + 1) * SEQ], axis=0, keepdims=True
        )


def attend_copies(pieces, weight, sem):
    copies = []
    for number, piece in enumerate(pieces):
        row, col = number % 2, number // 2
        for kind in range(3):
            copies.append(
                pltpu.make_async_copy(
                    piece.at[kind],
                    weight.at[pl.ds(row * HALF, HALF), pl.ds(col * SIDE + kind * HALF, HALF)],
                    sem.at[len(copies)],
                )
            )
    return copies


def grid_copies(pieces, weight, sem):
    copies = []
    for number, piece in enumerate(pieces):
        row, col = number % 2, number // 2
        across, down = piece.shape[1], piece.shape[0]
        copies.append(
            pltpu.make_async_copy(
                piece,
                weight.at[pl.ds(col * down, down), pl.ds(row * across, across)],
                sem.at[number],
            )
        )
    return copies


def relay_copies(place, pieces, weight, sem, first_is_row):
    copies = []
    for col in range(2):
        whole, near, far = pieces[3 * col : 3 * col + 3]
        down, across = whole.shape
        size = near.shape[0]
        for piece, row, start in (
            (whole, 0, 0),
            (near, 1, place * size),
            (far, 1, (1 - place) * size),
        ):
            top, left = (row, col) if first_is_row else (col, row)
            rows = pl.ds(pl.multiple_of(top * down + start, 16), piece.shape[0])
            copies.append(
                pltpu.make_async_copy(
                    piece, weight.at[rows, pl.ds(left * across, across)], sem.at[len(copies)]
                )
            )
    return copies


def forward_kernel(
    start, tok_own, tok_oth, mod_own, mod_oth, col_own, col_oth, w0, w1, w2, w3, *others
):
    first_ref, qkv_ref, att_ref, weight, sem = others[-5:]
    rows = functools.partial(spread_rows, (mod_own, mod_oth), per_tile=1, start=start)

    @pl.when(pl.program_id(0) == 0)
    def _():
        copies = attend_copies((w0, w1, w2, w3), weight, sem)
        for copy in copies:
            copy.start()
        for copy in copies:
            copy.wait()

    normal, _ = normalize(both(tok_own, tok_oth))
    first = (normal * (1.0 + rows(1)) + rows(0)).astype(B16)
    first_ref[...] = first
    blank = jnp.zeros((1, HALF), F32)
    last = col_oth.shape[0] - 1
    bias = jnp.concatenate(
        [line(col_own, 0, 0), blank, line(col_own, 0, 1)]
        + [line(col_oth, last, 0), blank, line(col_oth, last, 1)],
        axis=1,
    )
    qkv_ref[...] = (dot(first, weight[...]) + bias).astype(B16)
    low = lax.broadcasted_iota(jnp.int32, (SEQ, PAIR), 1) < HEAD_DIM
    for col in range(2):
        for pair in range(HALF // PAIR):
            base = col * SIDE + pair * PAIR
            q_part = qkv_ref[:, base : base + PAIR] * SCALE
            k_part = qkv_ref[:, base + HALF : base + HALF + PAIR]
            v_part = qkv_ref[:, base + D : base + D + PAIR]
            outs = []
            for keep in (low, jnp.logical_not(low)):
                scores = dot_nt(jnp.where(keep, q_part, 0).astype(B16), k_part)
                exponent = jnp.exp(scores - jnp.max(scores, axis=1, keepdims=True))
                probs = exponent * (1.0 / jnp.sum(exponent, axis=1, keepdims=True))
                outs.append(dot(probs.astype(B16), v_part))
            at = col * HALF + pair * PAIR
            att_ref[:, at : at + PAIR] = jnp.where(low, outs[0], outs[1]).astype(B16)


def middle_kernel(
    place, tok_own, tok_oth, cot_own, cot_oth, att, mod_own, mod_oth, col_own, col_oth, row_own,
    o0, o1, o2, o3, x0, x1, x2, x3, x4, x5, s0, s1, s2, s3, s4, s5,
    res_own, res_oth, second_ref, act_own, act_oth, dh_own, dh_oth, e_one_ref, e_two_ref,
    d_mid_ref, d_att_ref, mod_ref, sum_ref,
    w_out, w_exp, w_shr, sem_out, sem_exp, sem_shr,
):
    @pl.when(pl.program_id(0) == 0)
    def _():
        copies = (
            grid_copies((o0, o1, o2, o3), w_out, sem_out)
            + relay_copies(place[0], (x0, x1, x2, x3, x4, x5), w_exp, sem_exp, True)
            + relay_copies(place[0], (s0, s1, s2, s3, s4, s5), w_shr, sem_shr, False)
        )
        for copy in copies:
            copy.start()
        for copy in copies:
            copy.wait()

    per_tile = mod_ref.shape[0]
    last = mod_oth.shape[0] - 1
    rows = functools.partial(spread_rows, (mod_own, mod_oth), per_tile=per_tile)
    outbias = jnp.concatenate([line(row_own, 0, 0), line(mod_oth, last, 0)], axis=1)
    shrbias = jnp.concatenate([line(row_own, 0, 1), line(mod_oth, last, 1)], axis=1)

    branch_one = dot(att[...], w_out[...]) + outbias
    middle = both(tok_own, tok_oth) + rows(2) * branch_one
    normal, inverse = normalize(middle)
    second = (normal * (1.0 + rows(4)) + rows(3)).astype(B16)
    second_ref[...] = second
    upstream = both(cot_own, cot_oth)
    e_two = (rows(5) * upstream).astype(B16)
    e_two_ref[...] = e_two
    branch_two = shrbias
    d_second = 0.0
    for part in range(FF // D):
        at = part * D
        owner, lead = (col_own, 0) if 2 * at < FF else (col_oth, col_oth.shape[0] - 1)
        number = 2 + 2 * (part % (FF // D // 2))
        expbias = jnp.concatenate(
            [line(owner, lead, number), line(owner, lead, number + 1)], axis=1
        )
        hidden = dot(second, w_exp[:, at : at + D]) + expbias
        square = hidden * hidden
        bend = jnp.tanh(hidden * (ROOT + (ROOT * CUBE) * square))
        share = 0.5 + 0.5 * bend
        active = (hidden * share).astype(B16)
        slope = share + (0.5 * hidden) * (1.0 - bend * bend) * (ROOT + (3.0 * ROOT * CUBE) * square)
        branch_two = branch_two + dot(active, w_shr[at : at + D, :])
        d_hidden = (dot_nt(e_two, w_shr[at : at + D, :]) * slope).astype(B16)
        d_second = d_second + dot_nt(d_hidden, w_exp[:, at : at + D])
        act_ref, dh_ref = (act_own, dh_own) if 2 * at < FF else (act_oth, dh_oth)
        into = at % (FF // 2)
        act_ref[:, into : into + D] = active
        dh_ref[:, into : into + D] = d_hidden
        sum_ref[0, :, 2 * D + at : 2 * D + at + D] = jnp.sum(
            d_hidden.astype(F32), axis=0, keepdims=True
        )
    result = (middle + rows(5) * branch_two).astype(B16)
    res_own[...] = result[:, :HALF]
    res_oth[...] = result[:, HALF:]
    store_sums(mod_ref, 3, upstream * branch_two)
    store_sums(mod_ref, 1, d_second)
    store_sums(mod_ref, 2, d_second * normal)
    d_middle = upstream + norm_grad(d_second * (1.0 + rows(4)), normal, inverse)
    d_mid_ref[...] = d_middle
    store_sums(mod_ref, 0, d_middle * branch_one)
    e_one = (rows(2) * d_middle).astype(B16)
    e_one_ref[...] = e_one
    d_att_ref[...] = dot_nt(e_one, w_out[...]).astype(B16)
    sum_ref[0, :, :D] = jnp.sum(e_one.astype(F32), axis=0, keepdims=True)
    sum_ref[0, :, D : 2 * D] = jnp.sum(e_two.astype(F32), axis=0, keepdims=True)


def backward_kernel(qkv, d_att, dqkv_own, dqkv_oth, sum_ref):
    low = lax.broadcasted_iota(jnp.int32, (SEQ, PAIR), 1) < HEAD_DIM
    for col in range(2):
        out_ref = (dqkv_own, dqkv_oth)[col]
        for pair in range(HALF // PAIR):
            base = col * SIDE + pair * PAIR
            q_part = qkv[:, base : base + PAIR]
            k_part = qkv[:, base + HALF : base + HALF + PAIR]
            v_part = qkv[:, base + D : base + D + PAIR]
            d_part = d_att[:, col * HALF + pair * PAIR : col * HALF + (pair + 1) * PAIR]
            queries, keys, values = [], [], []
            for keep in (low, jnp.logical_not(low)):
                scores = dot_nt(jnp.where(keep, k_part * SCALE, 0).astype(B16), q_part)
                exponent = jnp.exp(scores - jnp.max(scores, axis=0, keepdims=True))
                probs = exponent * (1.0 / jnp.sum(exponent, axis=0, keepdims=True))
                d_probs = dot_nt(jnp.where(keep, v_part, 0).astype(B16), d_part)
                weighted = probs * d_probs
                d_scores = (weighted - probs * jnp.sum(weighted, axis=0, keepdims=True)).astype(B16)
                values.append(dot(probs.astype(B16), d_part))
                keys.append(dot(d_scores, q_part))
                queries.append(dot_tn(d_scores, k_part))
            for kind, (first, then, factor) in enumerate(
                ((*queries, SCALE), (*keys, SCALE), (*values, 1.0))
            ):
                at = kind * HALF + pair * PAIR
                piece = (jnp.where(low, first, then) * factor).astype(B16)
                out_ref[:, at : at + PAIR] = piece
                sum_ref[0, :, col * SIDE + at : col * SIDE + at + PAIR] = jnp.sum(
                    piece.astype(F32), axis=0, keepdims=True
                )


def project_kernel(
    tok_own, tok_oth, mod_own, mod_oth, dqkv_own, dqkv_oth, d_mid, w0, w1, w2, w3,
    grad_own, grad_oth, mod_ref, weight, sem,
):
    @pl.when(pl.program_id(0) == 0)
    def _():
        copies = attend_copies((w0, w1, w2, w3), weight, sem)
        for copy in copies:
            copy.start()
        for copy in copies:
            copy.wait()

    d_first = dot_nt(dqkv_own[...], weight[:, :SIDE]) + dot_nt(dqkv_oth[...], weight[:, SIDE:])
    normal, inverse = normalize(both(tok_own, tok_oth))
    store_sums(mod_ref, 0, d_first)
    store_sums(mod_ref, 1, d_first * normal)
    grad = (
        d_mid[...] + norm_grad(d_first * (1.0 + spread_rows((mod_own, mod_oth), 1, 1)), normal, inverse)
    ).astype(B16)
    grad_own[...] = grad[:, :HALF]
    grad_oth[...] = grad[:, HALF:]


def adaptive_kernel(cond, mods, out_ref):
    out_ref[0] = dot_tn(cond[...], mods[0])


def tiles(rows, width):
    return pl.BlockSpec((rows, width), lambda step: (step, 0))


def stacked(count, rows, width):
    return pl.BlockSpec((count, rows, width), lambda step: (step, 0, 0))


def fixed(values):
    return pl.BlockSpec(values.shape, lambda step: (0,) * values.ndim)


def anywhere(count):
    return [pl.BlockSpec(memory_space=pl.ANY)] * count


def params():
    return pltpu.CompilerParams(
        vmem_limit_bytes=VMEM_BYTES, dimension_semantics=("arbitrary",)
    )


def call_forward(tok_own, tok_oth, vectors, pieces, start, steps, before=()):
    count = tok_own.shape[0]

    def part(width):
        return pl.BlockSpec((SEQ, width), lambda step: (step + start, 0))

    inputs = (tok_own, tok_oth, *vectors, *pieces)
    return pl.pallas_call(
        functools.partial(forward_kernel, start),
        grid=(steps,),
        in_specs=[part(HALF)] * 2
        + [fixed(values) for values in vectors]
        + anywhere(4 + len(before)),
        out_specs=[part(D), part(2 * SIDE), part(D)],
        out_shape=[
            jax.ShapeDtypeStruct((count, D), B16),
            jax.ShapeDtypeStruct((count, 2 * SIDE), B16),
            jax.ShapeDtypeStruct((count, D), B16),
        ],
        input_output_aliases={len(inputs) + number: number for number in range(len(before))},
        scratch_shapes=[pltpu.VMEM((D, 2 * SIDE), B16), pltpu.SemaphoreType.DMA((12,))],
        compiler_params=params(),
        cost_estimate=pl.CostEstimate(
            flops=14 * 10**9 * steps // 4,
            bytes_accessed=16 * 10**6 * steps // 4,
            transcendentals=steps * SEQ * SEQ * 12,
        ),
        name="forward",
    )(*inputs, *before)


def call_middle(place, tok, cot, att, vectors, out_pieces, exp_pieces, shr_pieces):
    count = att.shape[0]
    latents = count // SEQ
    per_tile = PER_TILE if latents % PER_TILE == 0 else 1
    rows = per_tile * SEQ
    steps = latents // per_tile
    halves = [tiles(rows, HALF)] * 2

    def shape(width, kind=B16):
        return jax.ShapeDtypeStruct((count, width), kind)

    return pl.pallas_call(
        middle_kernel,
        grid=(steps,),
        in_specs=[pl.BlockSpec(memory_space=pltpu.SMEM)]
        + halves
        + halves
        + [tiles(rows, D)]
        + [fixed(values) for values in vectors]
        + anywhere(16),
        out_specs=halves
        + [tiles(rows, D)]
        + [tiles(rows, FF // 2)] * 4
        + [tiles(rows, D)] * 4
        + [stacked(per_tile, 4, D), stacked(1, 1, 2 * D + FF)],
        out_shape=[shape(HALF), shape(HALF), shape(D)]
        + [shape(FF // 2)] * 4
        + [shape(D), shape(D), shape(D, F32), shape(D)]
        + [
            jax.ShapeDtypeStruct((latents, 4, D), F32),
            jax.ShapeDtypeStruct((steps, 1, 2 * D + FF), F32),
        ],
        scratch_shapes=[
            pltpu.VMEM((D, D), B16),
            pltpu.VMEM((D, FF), B16),
            pltpu.VMEM((FF, D), B16),
            pltpu.SemaphoreType.DMA((4,)),
            pltpu.SemaphoreType.DMA((6,)),
            pltpu.SemaphoreType.DMA((6,)),
        ],
        compiler_params=params(),
        cost_estimate=pl.CostEstimate(
            flops=30 * 10**9, bytes_accessed=50 * 10**6, transcendentals=count * FF
        ),
        name="middle",
    )(place, *tok, *cot, att, *vectors, *out_pieces, *exp_pieces, *shr_pieces)


def call_backward(qkv, d_att):
    count = d_att.shape[0]
    latents = count // SEQ
    return pl.pallas_call(
        backward_kernel,
        grid=(latents,),
        in_specs=[tiles(SEQ, 2 * SIDE), tiles(SEQ, D)],
        out_specs=[tiles(SEQ, SIDE)] * 2 + [stacked(1, 1, 2 * SIDE)],
        out_shape=[jax.ShapeDtypeStruct((count, SIDE), B16)] * 2
        + [jax.ShapeDtypeStruct((latents, 1, 2 * SIDE), F32)],
        compiler_params=params(),
        cost_estimate=pl.CostEstimate(
            flops=10**9, bytes_accessed=10**6, transcendentals=0
        ),
        name="backward",
    )(qkv, d_att)


def call_project(tok, vectors, dqkv_own, dqkv_oth, d_mid, pieces):
    count = d_mid.shape[0]
    latents = count // SEQ
    return pl.pallas_call(
        project_kernel,
        grid=(latents,),
        in_specs=[tiles(SEQ, HALF)] * 2
        + [fixed(values) for values in vectors]
        + [tiles(SEQ, SIDE)] * 2
        + [tiles(SEQ, D)]
        + anywhere(4),
        out_specs=[tiles(SEQ, HALF)] * 2 + [stacked(1, 2, D)],
        out_shape=[jax.ShapeDtypeStruct((count, HALF), B16)] * 2
        + [jax.ShapeDtypeStruct((latents, 2, D), F32)],
        scratch_shapes=[pltpu.VMEM((D, 2 * SIDE), B16), pltpu.SemaphoreType.DMA((12,))],
        compiler_params=params(),
        cost_estimate=pl.CostEstimate(
            flops=7 * 10**9, bytes_accessed=16 * 10**6, transcendentals=count
        ),
        name="project",
    )(*tok, *vectors, dqkv_own, dqkv_oth, d_mid, *pieces)


def call_adaptive(cond, mods):
    latents, width = cond.shape
    kinds = mods.shape[0]
    return pl.pallas_call(
        adaptive_kernel,
        grid=(kinds,),
        in_specs=[
            pl.BlockSpec((latents, width), lambda step: (0, 0)),
            stacked(1, latents, HALF),
        ],
        out_specs=stacked(1, width, HALF),
        out_shape=jax.ShapeDtypeStruct((kinds, width, HALF), F32),
        compiler_params=params(),
        name="adaptive",
    )(cond, mods)


def swap_row(values):
    return lax.ppermute(values, "row", SWAP)


def swap_col(values):
    return lax.ppermute(values, "col", SWAP)


def swap_dp(values, distance):
    size = lax.axis_size("dp")
    return lax.ppermute(values, "dp", [(place, place ^ distance) for place in range(size)])


def distances():
    size = lax.axis_size("dp")
    return [1 << bit for bit in range(size.bit_length() - 1)]


def after(values, *earlier):
    return lax.optimization_barrier((values,) + earlier)[0]


def halves(values, dim):
    size = values.shape[dim] // 2
    return lax.slice_in_dim(values, 0, size, axis=dim), lax.slice_in_dim(
        values, size, 2 * size, axis=dim
    )


def pick(values, place, axis=0):
    size = values.shape[axis] // 2
    kept = lax.dynamic_slice_in_dim(values, place * size, size, axis)
    sent = lax.dynamic_slice_in_dim(values, (1 - place) * size, size, axis)
    return kept, sent


def in_order(place, mine, theirs):
    return jnp.concatenate(
        [jnp.where(place == 0, mine, theirs), jnp.where(place == 0, theirs, mine)], axis=0
    )


def x_place():
    return lax.axis_index("dp") % 2


def scatter_stage(values, distance, axis=0):
    place = (lax.axis_index("dp") // distance) % 2
    size = values.shape[axis] // 2
    kept = lax.dynamic_slice_in_dim(values, place * size, size, axis)
    sent = lax.dynamic_slice_in_dim(values, (1 - place) * size, size, axis)
    return kept + swap_dp(sent.astype(B16), distance).astype(F32)


def far_groups():
    far = distances()[1:]
    return [far[at : at + 2] for at in range(0, len(far), 2)]


def around(group):
    if len(group) == 1:
        return [group[0]]
    return [group[1], group[0], group[0] + group[1]]


def scatter_group(values, group):
    me = lax.axis_index("dp")
    place = 0
    for distance in group:
        place = 2 * place + (me // distance) % 2
    size = values.shape[0] >> len(group)
    total = lax.dynamic_slice_in_dim(values, place * size, size, 0)
    for block, distance in enumerate(around(group), 1):
        sent = lax.dynamic_slice_in_dim(values, (place ^ block) * size, size, 0)
        total = total + swap_dp(sent.astype(B16), distance).astype(F32)
    return total


def gather_group(values, group):
    return jnp.concatenate(
        [values] + [swap_dp(values, distance) for distance in around(group)], axis=0
    )


def gather_far(values):
    for group in reversed(far_groups()):
        values = gather_group(values, group)
    return values


def gather_near(values):
    return jnp.concatenate([values, swap_dp(values, 1)], axis=0)


def near_place():
    return jnp.full((1,), x_place(), jnp.int32)


def sum_place():
    me, mine = lax.axis_index("dp"), 0
    for distance in distances():
        mine = mine * 2 + (me // distance) % 2
    return jnp.full((1,), mine, jnp.int32)


def order_grid_kernel(mine, p0, p1, p2, p3, shr_out, out_out, exp_out):
    shr_rows, out_rows, exp_rows = shr_out.shape[1], out_out.shape[1], exp_out.shape[1]
    index = 0
    for values in (p0, p1, p2, p3):
        for block in range(values.shape[0]):
            into = mine[0] ^ index
            index += 1
            shr_out[into] = values[block, :shr_rows].astype(F32)
            out_out[into] = values[block, shr_rows : shr_rows + out_rows].astype(F32)
            for part in range(exp_out.shape[2] // HALF):
                at = shr_rows + out_rows + part * exp_rows
                exp_out[into, :, part * HALF : (part + 1) * HALF] = values[
                    block, at : at + exp_rows
                ].astype(F32)


def order_attend_kernel(mine, near, far, out):
    count = near.shape[0]
    for number, values in enumerate((near, far)):
        for block in range(count):
            place = mine[0] ^ (number * count + block)
            for kind in range(out.shape[0]):
                out[kind, place] = values[block, :, kind * HALF : (kind + 1) * HALF].astype(F32)


def order(kernel, place, values, shapes):
    whole = [pl.BlockSpec(memory_space=pltpu.VMEM)]
    return pl.pallas_call(
        kernel,
        in_specs=[pl.BlockSpec(memory_space=pltpu.SMEM)] + whole * len(values),
        out_specs=whole * len(shapes),
        out_shape=[jax.ShapeDtypeStruct(shape, F32) for shape in shapes],
        compiler_params=pltpu.CompilerParams(vmem_limit_bytes=VMEM_BYTES),
        name="order",
    )(place, *values)


def shards(
    tokens, condition, adaptive, adabias, attend, attbias, outproj, outbias,
    expand, expbias, shrink, shrbias, cotangent,
):
    row = lax.axis_index("row")
    col = lax.axis_index("col")

    tok_own, sent = pick(tokens, row)
    tok_oth = swap_row(sent)
    tok = (tok_own, tok_oth)

    raw_condition = after(condition, sent).astype(F32)
    act_cond = jax.nn.silu(raw_condition).astype(B16)
    mod_terms = jnp.einsum("ld,kde->kle", act_cond, adaptive, preferred_element_type=F32)
    kept, sent = pick(mod_terms, col, 1)
    group = kept.shape[1]
    latents = group // 2
    col_own = jnp.concatenate([attbias, expbias.reshape(-1, HALF)], axis=0).astype(F32)
    col_own = jnp.pad(col_own, ((0, group - col_own.shape[0]), (0, 0)))[None]
    col_oth = swap_col(jnp.concatenate([sent, col_own], axis=0))
    mod_rows = kept + col_oth[:6] + adabias.astype(F32)[:, None]
    mod_own, sent = pick(mod_rows, row, 1)
    row_own = jnp.stack([outbias, shrbias]).astype(F32)
    row_own = jnp.pad(row_own, ((0, latents - 2), (0, 0)))[None]
    mod_oth = swap_row(jnp.concatenate([sent, row_own], axis=0))
    mods = (mod_own, mod_oth)

    def pieces(values, over):
        return values, over, swap_col(values), swap_col(over)

    def near(values):
        return pick(values, x_place())[0]

    cot_own, cot_sent = pick(cotangent, row)
    attend, _, _, exp_near, shr_near, cot_sent, act_cond = lax.optimization_barrier(
        (attend, tok_oth, mod_oth, near(expand), near(shrink), cot_sent, act_cond)
    )
    attend_over, cond_all = lax.optimization_barrier((swap_row(attend), gather_far(act_cond)))
    attend_pieces = pieces(attend, attend_over)
    *attend_pieces, exp_near, shr_near = lax.optimization_barrier(
        (*attend_pieces, exp_near, shr_near)
    )
    exp_near = swap_row(exp_near)
    vectors = (*mods, col_own, col_oth)
    half = latents // 2
    *begun, exp_near, shr_near, cot_sent = lax.optimization_barrier(
        (
            *call_forward(tok_own, tok_oth, vectors, attend_pieces, 0, half),
            exp_near, shr_near, cot_sent,
        )
    )
    shr_near, exp_far, cot_oth = swap_row(shr_near), swap_dp(exp_near, 1), swap_row(cot_sent)
    first, qkv, attended = call_forward(
        tok_own, tok_oth, vectors, attend_pieces, half, latents - half, begun
    )
    attended, exp_far, shr_near, outproj, cond_all = lax.optimization_barrier(
        (attended, exp_far, shr_near, outproj, cond_all)
    )
    out_over = swap_row(outproj)
    shr_far = swap_dp(shr_near, 1)
    cond_all = gather_near(cond_all)
    early = [swap_col(values) for values in (expand, shrink, exp_near, shr_near)]
    cot_oth, out_over, exp_far, shr_far, cond_all, *early = lax.optimization_barrier(
        (cot_oth, out_over, exp_far, shr_far, cond_all, *early)
    )
    exp_pieces = (expand, exp_near, exp_far, early[0], early[2], swap_col(exp_far))
    shr_pieces = (shrink, shr_near, shr_far, early[1], early[3], swap_col(shr_far))
    out_pieces = pieces(outproj, out_over)
    (
        res_own, res_oth, second, act_own, act_oth, dh_own, dh_oth, e_one, e_two,
        d_middle, d_attended, mod_late, sums_late,
    ) = call_middle(
        near_place(), tok, (cot_own, cot_oth), attended, (*mods, col_own, col_oth, row_own),
        out_pieces, exp_pieces, shr_pieces,
    )
    att_own, att_oth = halves(attended, 1)
    depth = act_oth.shape[1]
    shr_sent = jnp.concatenate(
        [dot_tn(act_oth, e_two).astype(B16), dot_tn(att_oth, e_one).astype(B16)], axis=0
    )
    shr_sent, dh_oth = lax.optimization_barrier((shr_sent, dh_oth))
    shr_got = swap_col(shr_sent)
    exp_sent = dot_tn(second, dh_oth).astype(B16)
    exp_sent, act_own = lax.optimization_barrier((exp_sent, act_own))
    exp_got = swap_col(exp_sent)
    shr_total = dot_tn(act_own, e_two) + shr_got[:depth].astype(F32)
    out_total = dot_tn(att_own, e_one) + shr_got[depth:].astype(F32)
    near_step, *far_steps = distances()
    size = lax.axis_size("dp")
    shr_mine, shr_theirs = [
        jnp.concatenate([part.reshape(size, -1, HALF) for part in parts], axis=1)
        for parts in zip(halves(shr_total, 1), halves(out_total, 1))
    ]
    shr_mine, shr_theirs, dh_own = lax.optimization_barrier(
        (shr_mine, shr_theirs.astype(B16), dh_own)
    )
    shr_got = swap_row(shr_theirs)
    exp_total = dot_tn(second, dh_own) + exp_got.astype(F32)
    d_attended, exp_total = lax.optimization_barrier((d_attended, exp_total))
    exp_kept, exp_sent = pick(exp_total.reshape(2, HALF, -1), x_place(), 1)
    exp_got = swap_dp(exp_sent.astype(B16), near_step)

    dqkv_own, dqkv_oth, sums_early = call_backward(qkv, d_attended)
    dqkv_own, dqkv_oth, shr_got, exp_got = lax.optimization_barrier(
        (dqkv_own, dqkv_oth, shr_got, exp_got)
    )
    att_got = swap_col(dot_tn(first, dqkv_oth).astype(B16)).astype(F32)
    exp_part = exp_kept + exp_got.astype(F32)
    shr_kept, shr_sent = pick(shr_mine + shr_got.astype(F32), x_place())
    exp_got = swap_row(exp_part[1].astype(B16))
    shr_got = swap_dp(shr_sent.astype(B16), near_step)
    att_total = dot_tn(first, dqkv_own) + att_got
    att_total, exp_got, shr_got, d_middle = lax.optimization_barrier(
        (att_total, exp_got, shr_got, d_middle)
    )
    att_mine, att_theirs = halves(att_total, 0)
    att_part = att_mine + swap_row(att_theirs.astype(B16)).astype(F32)
    exp_part = exp_part[0] + exp_got.astype(F32)
    exp_part = exp_part.reshape(size // 2, HALF // size, -1)
    grid_part = jnp.concatenate(
        [shr_kept + shr_got.astype(F32)]
        + [exp_part[:, :, at : at + HALF] for at in range(0, exp_part.shape[2], HALF)],
        axis=1,
    )
    grid_part = scatter_stage(grid_part, far_steps[0])

    grad_own, grad_oth, mod_early = call_project(
        tok, mods, dqkv_own, dqkv_oth, d_middle, attend_pieces
    )
    sums_late = jnp.sum(sums_late, axis=(0, 1))
    sums_early = jnp.sum(sums_early, axis=(0, 1)).reshape(6, HALF)
    row_sums = sums_late[: 2 * D].reshape(2, 2, HALF)
    wide = sums_late[2 * D :].reshape(2, -1, HALF)
    col_sums = jnp.concatenate(
        [sums_early[0:3:2], wide[0], sums_early[3:6:2], wide[1]], axis=0
    )
    sums_sent = jnp.concatenate([row_sums[:, 1], col_sums], axis=0)
    sums_kept = jnp.concatenate([row_sums[:, 0], col_sums], axis=0)
    att_part, grid_part, mod_early, res_oth, sums_sent, sums_kept = lax.optimization_barrier(
        (att_part, grid_part, mod_early, res_oth, sums_sent, sums_kept)
    )

    d_modulation = jnp.concatenate([mod_early, mod_late], axis=1).astype(B16).astype(F32)
    mine = d_modulation[:, :, :HALF].reshape(-1, HALF)
    theirs = d_modulation[:, :, HALF:].reshape(-1, HALF)
    got = swap_row(jnp.concatenate([theirs, sums_sent], axis=0))
    rows = mine.shape[0]
    block = in_order(row, mine, got[:rows]).astype(B16)
    sums = sums_kept + got[rows:]
    high = sums.astype(B16)
    low = (sums - high.astype(F32)).astype(B16)
    width = block.shape[0] + 2 * sums.shape[0]
    packed = jnp.concatenate([block, high, low], axis=0)[None]

    res_got = swap_row(res_oth)
    att_part = scatter_stage(att_part.reshape(size, HALF // size, -1), near_step)
    for distance in far_steps[1:]:
        grid_part = scatter_stage(grid_part, distance)
    att_part, near_one, packed, grad_oth = lax.optimization_barrier(
        (att_part, grid_part.astype(B16), packed, grad_oth)
    )

    grad_got = swap_row(grad_oth)
    for distance in reversed(far_steps[1:]):
        near_one = jnp.concatenate([near_one, swap_dp(near_one, distance)], axis=0)
    for places in far_groups():
        att_part = scatter_group(att_part, places)
    packed_all = gather_far(packed)
    att_near, near_one, packed_all = lax.optimization_barrier(
        (att_part.astype(B16), near_one, packed_all)
    )

    near_two = swap_dp(near_one, far_steps[0])
    far_one = swap_dp(near_one, near_step)
    att_near = gather_far(att_near)
    packed_all = gather_near(packed_all)
    att_near, near_two, packed_all = lax.optimization_barrier((att_near, near_two, packed_all))

    far_two = swap_dp(near_two, near_step)
    att_far = swap_dp(att_near, near_step)
    result = in_order(row, res_own, res_got)
    input_gradient = in_order(row, grad_own, grad_got)
    exp_width = expand.shape[1]
    shrink_grad, outproj_grad, expand_grad = order(
        order_grid_kernel,
        sum_place(),
        (near_one, near_two, far_one, far_two),
        [(size, depth // size, HALF), (size, HALF // size, HALF), (size, HALF // size, exp_width)],
    )
    shrink_grad, outproj_grad = [part.reshape(-1, HALF) for part in (shrink_grad, outproj_grad)]
    expand_grad = expand_grad.reshape(HALF, exp_width)
    (attend_grad,) = order(
        order_attend_kernel,
        sum_place(),
        (att_near, att_far),
        [(3, size, HALF // size, HALF)],
    )
    attend_grad = attend_grad.reshape(3, HALF, HALF)
    block_all = packed_all[:, : block.shape[0]].reshape(-1, HALF)
    both_sums = jnp.sum(packed_all[:, block.shape[0] :].astype(F32), axis=0)
    sums = both_sums[: sums.shape[0]] + both_sums[sums.shape[0] :]
    count = col_sums.shape[0] // 2
    given = jnp.concatenate([sums[:2], sums[2 + count :]], axis=0)
    high = given.astype(B16)
    low = (given - high.astype(F32)).astype(B16)
    got = swap_col(jnp.concatenate([block_all, high, low], axis=0))
    other_all = got[: block_all.shape[0]]
    got = got[block_all.shape[0] :].astype(F32)
    sums = sums[: 2 + count] + got[: 2 + count] + got[2 + count :]
    outbias_grad, shrbias_grad = sums[0], sums[1]
    attbias_grad = sums[2:4]
    expbias_grad = sums[4:].reshape(-1)

    mod_all = jnp.concatenate([block_all, other_all], axis=0).reshape(-1, 6, HALF)
    cond_mine, cond_theirs = pick(
        cond_all.reshape(-1, 2 * group, HALF).transpose(1, 0, 2), col
    )
    cond_all = jnp.concatenate(
        [part.transpose(1, 0, 2).reshape(-1, HALF) for part in (cond_mine, cond_theirs)], axis=0
    )
    adabias_grad = jnp.sum(mod_all, axis=0, dtype=F32)
    adaptive_grad = call_adaptive(cond_all, mod_all.transpose(1, 0, 2))
    mod_group = in_order(col, block, other_all[: block.shape[0]]).reshape(-1, 6, HALF)
    d_act = jnp.einsum("lke,kde->ld", mod_group, adaptive, preferred_element_type=F32)
    d_act = d_act + swap_row(d_act)
    condition_gradient = jax.vjp(jax.nn.silu, raw_condition)[1](d_act)[0].astype(B16)
    return (
        result, input_gradient, condition_gradient, adaptive_grad, adabias_grad, attend_grad,
        attbias_grad, outproj_grad, outbias_grad, expand_grad, expbias_grad, shrink_grad,
        shrbias_grad,
    )


def solution(mesh):
    placed = (
        P(("dp", "col"), "row"),
        P("dp", "col"),
        P(None, "col", "row"),
        P(None, "row"),
        P(None, "row", "col"),
        P(None, "col"),
        P("col", "row"),
        P("row"),
        P("row", "col"),
        P("col"),
        P("col", "row"),
        P("row"),
        P(("dp", "col"), "row"),
    )
    return jax.shard_map(
        shards,
        mesh=mesh,
        in_specs=placed,
        out_specs=(
            P(("dp", "col"), "row"),
            P(("dp", "col"), "row"),
            P("dp", "col"),
            P(None, "col", "row"),
            P(None, "row"),
            P(None, "row", "col"),
            P(None, "col"),
            P("col", "row"),
            P("row"),
            P("row", "col"),
            P("col"),
            P("col", "row"),
            P("row"),
        ),
        check_vma=False,
    )
```

```python
import functools

import jax
import jax.numpy as jnp
from jax import lax
from jax.experimental import pallas as pl
from jax.experimental.pallas import tpu as pltpu
from jax.sharding import PartitionSpec as P

D = 768
HALF = D // 2
FF = 3072
SEQ = 256
HEAD_DIM = 64
PAIR = 2 * HEAD_DIM
SIDE = 3 * HALF
EPS = 1e-06
F32 = jnp.float32
B16 = jnp.bfloat16
SWAP = ((0, 1), (1, 0))
SCALE = HEAD_DIM ** (-0.5)
ROOT = (2.0 / 3.141592653589793) ** 0.5
CUBE = 0.044715
PER_TILE = 2
VMEM_BYTES = 60 * 1024 * 1024


def dot(left, right):
    return jnp.dot(left, right, preferred_element_type=F32)


def dot_nt(left, right):
    return lax.dot_general(left, right, (((1,), (1,)), ((), ())), preferred_element_type=F32)


def dot_tn(left, right):
    return lax.dot_general(left, right, (((0,), (0,)), ((), ())), preferred_element_type=F32)


def normalize(values):
    center = jnp.mean(values, axis=1, keepdims=True)
    spread = jnp.mean(values * values, axis=1, keepdims=True) - center * center
    inverse = lax.rsqrt(spread + EPS)
    return (values - center) * inverse, inverse


def norm_grad(upstream, normal, inverse):
    first_mean = jnp.mean(upstream, axis=1, keepdims=True)
    second_mean = jnp.mean(upstream * normal, axis=1, keepdims=True)
    return inverse * (upstream - first_mean - normal * second_mean)


def both(own_ref, oth_ref):
    return jnp.concatenate([own_ref[...], oth_ref[...]], axis=1).astype(F32)


def line(ref, lead, number):
    return ref[lead, number : number + 1, :]


def spread_rows(mods, number, per_tile, start=0):
    own, oth = mods
    rows = []
    for latent in range(per_tile):
        at = pl.ds((pl.program_id(0) + start) * per_tile + latent, 1)
        pair = jnp.concatenate([own[number, at, :], oth[number, at, :]], axis=1)
        rows.append(jnp.broadcast_to(pair, (SEQ, D)))
    return rows[0] if per_tile == 1 else jnp.concatenate(rows, axis=0)


def store_sums(out_ref, number, values):
    for latent in range(out_ref.shape[0]):
        out_ref[latent, number : number + 1, :] = jnp.sum(
            values[latent * SEQ : (latent + 1) * SEQ], axis=0, keepdims=True
        )


def attend_copies(pieces, weight, sem):
    copies = []
    for number, piece in enumerate(pieces):
        row, col = number % 2, number // 2
        for kind in range(3):
            copies.append(
                pltpu.make_async_copy(
                    piece.at[kind],
                    weight.at[pl.ds(row * HALF, HALF), pl.ds(col * SIDE + kind * HALF, HALF)],
                    sem.at[len(copies)],
                )
            )
    return copies


def grid_copies(pieces, weight, sem):
    copies = []
    for number, piece in enumerate(pieces):
        row, col = number % 2, number // 2
        across, down = piece.shape[1], piece.shape[0]
        copies.append(
            pltpu.make_async_copy(
                piece,
                weight.at[pl.ds(col * down, down), pl.ds(row * across, across)],
                sem.at[number],
            )
        )
    return copies


def relay_copies(place, pieces, weight, sem, first_is_row):
    copies = []
    for col in range(2):
        whole, near, far = pieces[3 * col : 3 * col + 3]
        down, across = whole.shape
        size = near.shape[0]
        for piece, row, start in (
            (whole, 0, 0),
            (near, 1, place * size),
            (far, 1, (1 - place) * size),
        ):
            top, left = (row, col) if first_is_row else (col, row)
            rows = pl.ds(pl.multiple_of(top * down + start, 16), piece.shape[0])
            copies.append(
                pltpu.make_async_copy(
                    piece, weight.at[rows, pl.ds(left * across, across)], sem.at[len(copies)]
                )
            )
    return copies


def forward_kernel(
    start, tok_own, tok_oth, mod_own, mod_oth, col_own, col_oth, w0, w1, w2, w3, *others
):
    first_ref, qkv_ref, att_ref, weight, sem = others[-5:]
    rows = functools.partial(spread_rows, (mod_own, mod_oth), per_tile=1, start=start)

    @pl.when(pl.program_id(0) == 0)
    def _():
        copies = attend_copies((w0, w1, w2, w3), weight, sem)
        for copy in copies:
            copy.start()
        for copy in copies:
            copy.wait()

    normal, _ = normalize(both(tok_own, tok_oth))
    first = (normal * (1.0 + rows(1)) + rows(0)).astype(B16)
    first_ref[...] = first
    blank = jnp.zeros((1, HALF), F32)
    last = col_oth.shape[0] - 1
    bias = jnp.concatenate(
        [line(col_own, 0, 0), blank, line(col_own, 0, 1)]
        + [line(col_oth, last, 0), blank, line(col_oth, last, 1)],
        axis=1,
    )
    qkv_ref[...] = (dot(first, weight[...]) + bias).astype(B16)
    low = lax.broadcasted_iota(jnp.int32, (SEQ, PAIR), 1) < HEAD_DIM
    for col in range(2):
        for pair in range(HALF // PAIR):
            base = col * SIDE + pair * PAIR
            q_part = qkv_ref[:, base : base + PAIR] * SCALE
            k_part = qkv_ref[:, base + HALF : base + HALF + PAIR]
            v_part = qkv_ref[:, base + D : base + D + PAIR]
            outs = []
            for keep in (low, jnp.logical_not(low)):
                scores = dot_nt(jnp.where(keep, q_part, 0).astype(B16), k_part)
                exponent = jnp.exp(scores - jnp.max(scores, axis=1, keepdims=True))
                probs = exponent * (1.0 / jnp.sum(exponent, axis=1, keepdims=True))
                outs.append(dot(probs.astype(B16), v_part))
            at = col * HALF + pair * PAIR
            att_ref[:, at : at + PAIR] = jnp.where(low, outs[0], outs[1]).astype(B16)


def middle_kernel(
    place, tok_own, tok_oth, cot_own, cot_oth, att, mod_own, mod_oth, col_own, col_oth, row_own,
    o0, o1, o2, o3, x0, x1, x2, x3, x4, x5, s0, s1, s2, s3, s4, s5,
    res_own, res_oth, second_ref, act_own, act_oth, dh_own, dh_oth, e_one_ref, e_two_ref,
    d_mid_ref, d_att_ref, mod_ref, sum_ref,
    w_out, w_exp, w_shr, sem_out, sem_exp, sem_shr,
):
    @pl.when(pl.program_id(0) == 0)
    def _():
        copies = (
            grid_copies((o0, o1, o2, o3), w_out, sem_out)
            + relay_copies(place[0], (x0, x1, x2, x3, x4, x5), w_exp, sem_exp, True)
            + relay_copies(place[0], (s0, s1, s2, s3, s4, s5), w_shr, sem_shr, False)
        )
        for copy in copies:
            copy.start()
        for copy in copies:
            copy.wait()

    per_tile = mod_ref.shape[0]
    last = mod_oth.shape[0] - 1
    rows = functools.partial(spread_rows, (mod_own, mod_oth), per_tile=per_tile)
    outbias = jnp.concatenate([line(row_own, 0, 0), line(mod_oth, last, 0)], axis=1)
    shrbias = jnp.concatenate([line(row_own, 0, 1), line(mod_oth, last, 1)], axis=1)

    branch_one = dot(att[...], w_out[...]) + outbias
    middle = both(tok_own, tok_oth) + rows(2) * branch_one
    normal, inverse = normalize(middle)
    second = (normal * (1.0 + rows(4)) + rows(3)).astype(B16)
    second_ref[...] = second
    upstream = both(cot_own, cot_oth)
    e_two = (rows(5) * upstream).astype(B16)
    e_two_ref[...] = e_two
    branch_two = shrbias
    d_second = 0.0
    for part in range(FF // D):
        at = part * D
        owner, lead = (col_own, 0) if 2 * at < FF else (col_oth, col_oth.shape[0] - 1)
        number = 2 + 2 * (part % (FF // D // 2))
        expbias = jnp.concatenate(
            [line(owner, lead, number), line(owner, lead, number + 1)], axis=1
        )
        hidden = dot(second, w_exp[:, at : at + D]) + expbias
        square = hidden * hidden
        bend = jnp.tanh(hidden * (ROOT + (ROOT * CUBE) * square))
        share = 0.5 + 0.5 * bend
        active = (hidden * share).astype(B16)
        slope = share + (0.5 * hidden) * (1.0 - bend * bend) * (ROOT + (3.0 * ROOT * CUBE) * square)
        branch_two = branch_two + dot(active, w_shr[at : at + D, :])
        d_hidden = (dot_nt(e_two, w_shr[at : at + D, :]) * slope).astype(B16)
        d_second = d_second + dot_nt(d_hidden, w_exp[:, at : at + D])
        act_ref, dh_ref = (act_own, dh_own) if 2 * at < FF else (act_oth, dh_oth)
        into = at % (FF // 2)
        act_ref[:, into : into + D] = active
        dh_ref[:, into : into + D] = d_hidden
        sum_ref[0, :, 2 * D + at : 2 * D + at + D] = jnp.sum(
            d_hidden.astype(F32), axis=0, keepdims=True
        )
    result = (middle + rows(5) * branch_two).astype(B16)
    res_own[...] = result[:, :HALF]
    res_oth[...] = result[:, HALF:]
    store_sums(mod_ref, 3, upstream * branch_two)
    store_sums(mod_ref, 1, d_second)
    store_sums(mod_ref, 2, d_second * normal)
    d_middle = upstream + norm_grad(d_second * (1.0 + rows(4)), normal, inverse)
    d_mid_ref[...] = d_middle
    store_sums(mod_ref, 0, d_middle * branch_one)
    e_one = (rows(2) * d_middle).astype(B16)
    e_one_ref[...] = e_one
    d_att_ref[...] = dot_nt(e_one, w_out[...]).astype(B16)
    sum_ref[0, :, :D] = jnp.sum(e_one.astype(F32), axis=0, keepdims=True)
    sum_ref[0, :, D : 2 * D] = jnp.sum(e_two.astype(F32), axis=0, keepdims=True)


def backward_kernel(qkv, d_att, dqkv_own, dqkv_oth, sum_ref):
    low = lax.broadcasted_iota(jnp.int32, (SEQ, PAIR), 1) < HEAD_DIM
    for col in range(2):
        out_ref = (dqkv_own, dqkv_oth)[col]
        for pair in range(HALF // PAIR):
            base = col * SIDE + pair * PAIR
            q_part = qkv[:, base : base + PAIR]
            k_part = qkv[:, base + HALF : base + HALF + PAIR]
            v_part = qkv[:, base + D : base + D + PAIR]
            d_part = d_att[:, col * HALF + pair * PAIR : col * HALF + (pair + 1) * PAIR]
            queries, keys, values = [], [], []
            for keep in (low, jnp.logical_not(low)):
                scores = dot_nt(jnp.where(keep, k_part * SCALE, 0).astype(B16), q_part)
                exponent = jnp.exp(scores - jnp.max(scores, axis=0, keepdims=True))
                probs = exponent * (1.0 / jnp.sum(exponent, axis=0, keepdims=True))
                d_probs = dot_nt(jnp.where(keep, v_part, 0).astype(B16), d_part)
                weighted = probs * d_probs
                d_scores = (weighted - probs * jnp.sum(weighted, axis=0, keepdims=True)).astype(B16)
                values.append(dot(probs.astype(B16), d_part))
                keys.append(dot(d_scores, q_part))
                queries.append(dot_tn(d_scores, k_part))
            for kind, (first, then, factor) in enumerate(
                ((*queries, SCALE), (*keys, SCALE), (*values, 1.0))
            ):
                at = kind * HALF + pair * PAIR
                piece = (jnp.where(low, first, then) * factor).astype(B16)
                out_ref[:, at : at + PAIR] = piece
                sum_ref[0, :, col * SIDE + at : col * SIDE + at + PAIR] = jnp.sum(
                    piece.astype(F32), axis=0, keepdims=True
                )


def project_kernel(
    tok_own, tok_oth, mod_own, mod_oth, dqkv_own, dqkv_oth, d_mid, w0, w1, w2, w3,
    grad_own, grad_oth, mod_ref, weight, sem,
):
    @pl.when(pl.program_id(0) == 0)
    def _():
        copies = attend_copies((w0, w1, w2, w3), weight, sem)
        for copy in copies:
            copy.start()
        for copy in copies:
            copy.wait()

    d_first = dot_nt(dqkv_own[...], weight[:, :SIDE]) + dot_nt(dqkv_oth[...], weight[:, SIDE:])
    normal, inverse = normalize(both(tok_own, tok_oth))
    store_sums(mod_ref, 0, d_first)
    store_sums(mod_ref, 1, d_first * normal)
    grad = (
        d_mid[...] + norm_grad(d_first * (1.0 + spread_rows((mod_own, mod_oth), 1, 1)), normal, inverse)
    ).astype(B16)
    grad_own[...] = grad[:, :HALF]
    grad_oth[...] = grad[:, HALF:]


def adaptive_kernel(cond, mods, out_ref):
    out_ref[0] = dot_tn(cond[...], mods[0])


def tiles(rows, width):
    return pl.BlockSpec((rows, width), lambda step: (step, 0))


def stacked(count, rows, width):
    return pl.BlockSpec((count, rows, width), lambda step: (step, 0, 0))


def fixed(values):
    return pl.BlockSpec(values.shape, lambda step: (0,) * values.ndim)


def anywhere(count):
    return [pl.BlockSpec(memory_space=pl.ANY)] * count


def params():
    return pltpu.CompilerParams(
        vmem_limit_bytes=VMEM_BYTES, dimension_semantics=("arbitrary",)
    )


def call_forward(tok_own, tok_oth, vectors, pieces, start, steps, before=()):
    count = tok_own.shape[0]

    def part(width):
        return pl.BlockSpec((SEQ, width), lambda step: (step + start, 0))

    inputs = (tok_own, tok_oth, *vectors, *pieces)
    return pl.pallas_call(
        functools.partial(forward_kernel, start),
        grid=(steps,),
        in_specs=[part(HALF)] * 2
        + [fixed(values) for values in vectors]
        + anywhere(4 + len(before)),
        out_specs=[part(D), part(2 * SIDE), part(D)],
        out_shape=[
            jax.ShapeDtypeStruct((count, D), B16),
            jax.ShapeDtypeStruct((count, 2 * SIDE), B16),
            jax.ShapeDtypeStruct((count, D), B16),
        ],
        input_output_aliases={len(inputs) + number: number for number in range(len(before))},
        scratch_shapes=[pltpu.VMEM((D, 2 * SIDE), B16), pltpu.SemaphoreType.DMA((12,))],
        compiler_params=params(),
        cost_estimate=pl.CostEstimate(
            flops=14 * 10**9 * steps // 4,
            bytes_accessed=16 * 10**6 * steps // 4,
            transcendentals=steps * SEQ * SEQ * 12,
        ),
        name="forward",
    )(*inputs, *before)


def call_middle(place, tok, cot, att, vectors, out_pieces, exp_pieces, shr_pieces):
    count = att.shape[0]
    latents = count // SEQ
    per_tile = PER_TILE if latents % PER_TILE == 0 else 1
    rows = per_tile * SEQ
    steps = latents // per_tile
    halves = [tiles(rows, HALF)] * 2

    def shape(width, kind=B16):
        return jax.ShapeDtypeStruct((count, width), kind)

    return pl.pallas_call(
        middle_kernel,
        grid=(steps,),
        in_specs=[pl.BlockSpec(memory_space=pltpu.SMEM)]
        + halves
        + halves
        + [tiles(rows, D)]
        + [fixed(values) for values in vectors]
        + anywhere(16),
        out_specs=halves
        + [tiles(rows, D)]
        + [tiles(rows, FF // 2)] * 4
        + [tiles(rows, D)] * 4
        + [stacked(per_tile, 4, D), stacked(1, 1, 2 * D + FF)],
        out_shape=[shape(HALF), shape(HALF), shape(D)]
        + [shape(FF // 2)] * 4
        + [shape(D), shape(D), shape(D, F32), shape(D)]
        + [
            jax.ShapeDtypeStruct((latents, 4, D), F32),
            jax.ShapeDtypeStruct((steps, 1, 2 * D + FF), F32),
        ],
        scratch_shapes=[
            pltpu.VMEM((D, D), B16),
            pltpu.VMEM((D, FF), B16),
            pltpu.VMEM((FF, D), B16),
            pltpu.SemaphoreType.DMA((4,)),
            pltpu.SemaphoreType.DMA((6,)),
            pltpu.SemaphoreType.DMA((6,)),
        ],
        compiler_params=params(),
        cost_estimate=pl.CostEstimate(
            flops=30 * 10**9, bytes_accessed=50 * 10**6, transcendentals=count * FF
        ),
        name="middle",
    )(place, *tok, *cot, att, *vectors, *out_pieces, *exp_pieces, *shr_pieces)


def call_backward(qkv, d_att):
    count = d_att.shape[0]
    latents = count // SEQ
    return pl.pallas_call(
        backward_kernel,
        grid=(latents,),
        in_specs=[tiles(SEQ, 2 * SIDE), tiles(SEQ, D)],
        out_specs=[tiles(SEQ, SIDE)] * 2 + [stacked(1, 1, 2 * SIDE)],
        out_shape=[jax.ShapeDtypeStruct((count, SIDE), B16)] * 2
        + [jax.ShapeDtypeStruct((latents, 1, 2 * SIDE), F32)],
        compiler_params=params(),
        cost_estimate=pl.CostEstimate(
            flops=10**9, bytes_accessed=10**6, transcendentals=0
        ),
        name="backward",
    )(qkv, d_att)


def call_project(tok, vectors, dqkv_own, dqkv_oth, d_mid, pieces):
    count = d_mid.shape[0]
    latents = count // SEQ
    return pl.pallas_call(
        project_kernel,
        grid=(latents,),
        in_specs=[tiles(SEQ, HALF)] * 2
        + [fixed(values) for values in vectors]
        + [tiles(SEQ, SIDE)] * 2
        + [tiles(SEQ, D)]
        + anywhere(4),
        out_specs=[tiles(SEQ, HALF)] * 2 + [stacked(1, 2, D)],
        out_shape=[jax.ShapeDtypeStruct((count, HALF), B16)] * 2
        + [jax.ShapeDtypeStruct((latents, 2, D), F32)],
        scratch_shapes=[pltpu.VMEM((D, 2 * SIDE), B16), pltpu.SemaphoreType.DMA((12,))],
        compiler_params=params(),
        cost_estimate=pl.CostEstimate(
            flops=7 * 10**9, bytes_accessed=16 * 10**6, transcendentals=count
        ),
        name="project",
    )(*tok, *vectors, dqkv_own, dqkv_oth, d_mid, *pieces)


def call_adaptive(cond, mods):
    latents, width = cond.shape
    kinds = mods.shape[0]
    return pl.pallas_call(
        adaptive_kernel,
        grid=(kinds,),
        in_specs=[
            pl.BlockSpec((latents, width), lambda step: (0, 0)),
            stacked(1, latents, HALF),
        ],
        out_specs=stacked(1, width, HALF),
        out_shape=jax.ShapeDtypeStruct((kinds, width, HALF), F32),
        compiler_params=params(),
        name="adaptive",
    )(cond, mods)


def swap_row(values):
    return lax.ppermute(values, "row", SWAP)


def swap_col(values):
    return lax.ppermute(values, "col", SWAP)


def swap_dp(values, distance):
    size = lax.axis_size("dp")
    return lax.ppermute(values, "dp", [(place, place ^ distance) for place in range(size)])


def distances():
    size = lax.axis_size("dp")
    return [1 << bit for bit in range(size.bit_length() - 1)]


def after(values, *earlier):
    return lax.optimization_barrier((values,) + earlier)[0]


def halves(values, dim):
    size = values.shape[dim] // 2
    return lax.slice_in_dim(values, 0, size, axis=dim), lax.slice_in_dim(
        values, size, 2 * size, axis=dim
    )


def pick(values, place, axis=0):
    size = values.shape[axis] // 2
    kept = lax.dynamic_slice_in_dim(values, place * size, size, axis)
    sent = lax.dynamic_slice_in_dim(values, (1 - place) * size, size, axis)
    return kept, sent


def in_order(place, mine, theirs):
    return jnp.concatenate(
        [jnp.where(place == 0, mine, theirs), jnp.where(place == 0, theirs, mine)], axis=0
    )


def x_place():
    return lax.axis_index("dp") % 2


def scatter_stage(values, distance, axis=0):
    place = (lax.axis_index("dp") // distance) % 2
    size = values.shape[axis] // 2
    kept = lax.dynamic_slice_in_dim(values, place * size, size, axis)
    sent = lax.dynamic_slice_in_dim(values, (1 - place) * size, size, axis)
    return kept + swap_dp(sent.astype(B16), distance).astype(F32)


def far_groups():
    far = distances()[1:]
    return [far[at : at + 2] for at in range(0, len(far), 2)]


def around(group):
    if len(group) == 1:
        return [group[0]]
    return [group[1], group[0], group[0] + group[1]]


def scatter_group(values, group):
    me = lax.axis_index("dp")
    place = 0
    for distance in group:
        place = 2 * place + (me // distance) % 2
    size = values.shape[0] >> len(group)
    total = lax.dynamic_slice_in_dim(values, place * size, size, 0)
    for block, distance in enumerate(around(group), 1):
        sent = lax.dynamic_slice_in_dim(values, (place ^ block) * size, size, 0)
        total = total + swap_dp(sent.astype(B16), distance).astype(F32)
    return total


def gather_group(values, group):
    return jnp.concatenate(
        [values] + [swap_dp(values, distance) for distance in around(group)], axis=0
    )


def gather_far(values):
    for group in reversed(far_groups()):
        values = gather_group(values, group)
    return values


def gather_near(values):
    return jnp.concatenate([values, swap_dp(values, 1)], axis=0)


def near_place():
    return jnp.full((1,), x_place(), jnp.int32)


def sum_place():
    me, mine = lax.axis_index("dp"), 0
    for distance in distances():
        mine = mine * 2 + (me // distance) % 2
    return jnp.full((1,), mine, jnp.int32)


def order_grid_kernel(mine, p0, p1, p2, p3, shr_out, out_out, exp_out):
    shr_rows, out_rows, exp_rows = shr_out.shape[1], out_out.shape[1], exp_out.shape[1]
    index = 0
    for values in (p0, p1, p2, p3):
        for block in range(values.shape[0]):
            into = mine[0] ^ index
            index += 1
            shr_out[into] = values[block, :shr_rows].astype(F32)
            out_out[into] = values[block, shr_rows : shr_rows + out_rows].astype(F32)
            for part in range(exp_out.shape[2] // HALF):
                at = shr_rows + out_rows + part * exp_rows
                exp_out[into, :, part * HALF : (part + 1) * HALF] = values[
                    block, at : at + exp_rows
                ].astype(F32)


def order_attend_kernel(mine, near, far, out):
    count = near.shape[0]
    for number, values in enumerate((near, far)):
        for block in range(count):
            place = mine[0] ^ (number * count + block)
            for kind in range(out.shape[0]):
                out[kind, place] = values[block, :, kind * HALF : (kind + 1) * HALF].astype(F32)


def order(kernel, place, values, shapes):
    whole = [pl.BlockSpec(memory_space=pltpu.VMEM)]
    return pl.pallas_call(
        kernel,
        in_specs=[pl.BlockSpec(memory_space=pltpu.SMEM)] + whole * len(values),
        out_specs=whole * len(shapes),
        out_shape=[jax.ShapeDtypeStruct(shape, F32) for shape in shapes],
        compiler_params=pltpu.CompilerParams(vmem_limit_bytes=VMEM_BYTES),
        name="order",
    )(place, *values)


def shards(
    tokens, condition, adaptive, adabias, attend, attbias, outproj, outbias,
    expand, expbias, shrink, shrbias, cotangent,
):
    row = lax.axis_index("row")
    col = lax.axis_index("col")

    tok_own, sent = pick(tokens, row)
    tok_oth = swap_row(sent)
    tok = (tok_own, tok_oth)

    raw_condition = after(condition, sent).astype(F32)
    act_cond = jax.nn.silu(raw_condition).astype(B16)
    mod_terms = jnp.einsum("ld,kde->kle", act_cond, adaptive, preferred_element_type=F32)
    kept, sent = pick(mod_terms, col, 1)
    group = kept.shape[1]
    latents = group // 2
    col_own = jnp.concatenate([attbias, expbias.reshape(-1, HALF)], axis=0).astype(F32)
    col_own = jnp.pad(col_own, ((0, group - col_own.shape[0]), (0, 0)))[None]
    col_oth = swap_col(jnp.concatenate([sent, col_own], axis=0))
    mod_rows = kept + col_oth[:6] + adabias.astype(F32)[:, None]
    mod_own, sent = pick(mod_rows, row, 1)
    row_own = jnp.stack([outbias, shrbias]).astype(F32)
    row_own = jnp.pad(row_own, ((0, latents - 2), (0, 0)))[None]
    mod_oth = swap_row(jnp.concatenate([sent, row_own], axis=0))
    mods = (mod_own, mod_oth)

    def pieces(values, over):
        return values, over, swap_col(values), swap_col(over)

    def near(values):
        return pick(values, x_place())[0]

    cot_own, cot_sent = pick(cotangent, row)
    attend, _, _, exp_near, shr_near, cot_sent, act_cond = lax.optimization_barrier(
        (attend, tok_oth, mod_oth, near(expand), near(shrink), cot_sent, act_cond)
    )
    attend_over, cond_all = lax.optimization_barrier((swap_row(attend), gather_far(act_cond)))
    attend_pieces = pieces(attend, attend_over)
    *attend_pieces, exp_near, shr_near = lax.optimization_barrier(
        (*attend_pieces, exp_near, shr_near)
    )
    exp_near = swap_row(exp_near)
    vectors = (*mods, col_own, col_oth)
    half = latents // 2
    *begun, exp_near, shr_near, cot_sent, outproj = lax.optimization_barrier(
        (
            *call_forward(tok_own, tok_oth, vectors, attend_pieces, 0, half),
            exp_near, shr_near, cot_sent, outproj,
        )
    )
    shr_near, exp_far = swap_row(shr_near), swap_dp(exp_near, 1)
    cot_oth, out_over = swap_row(cot_sent), swap_row(outproj)
    first, qkv, attended = call_forward(
        tok_own, tok_oth, vectors, attend_pieces, half, latents - half, begun
    )
    attended, exp_far, shr_near = lax.optimization_barrier((attended, exp_far, shr_near))
    shr_far = swap_dp(shr_near, 1)
    early = [swap_col(values) for values in (expand, shrink, exp_near, shr_near)]
    cot_oth, out_over, exp_far, shr_far, *early = lax.optimization_barrier(
        (cot_oth, out_over, exp_far, shr_far, *early)
    )
    exp_pieces = (expand, exp_near, exp_far, early[0], early[2], swap_col(exp_far))
    shr_pieces = (shrink, shr_near, shr_far, early[1], early[3], swap_col(shr_far))
    out_pieces = pieces(outproj, out_over)
    (
        res_own, res_oth, second, act_own, act_oth, dh_own, dh_oth, e_one, e_two,
        d_middle, d_attended, mod_late, sums_late,
    ) = call_middle(
        near_place(), tok, (cot_own, cot_oth), attended, (*mods, col_own, col_oth, row_own),
        out_pieces, exp_pieces, shr_pieces,
    )
    att_own, att_oth = halves(attended, 1)
    depth = act_oth.shape[1]
    shr_sent = jnp.concatenate(
        [dot_tn(act_oth, e_two).astype(B16), dot_tn(att_oth, e_one).astype(B16)], axis=0
    )
    shr_sent, dh_oth = lax.optimization_barrier((shr_sent, dh_oth))
    shr_got = swap_col(shr_sent)
    exp_sent = dot_tn(second, dh_oth).astype(B16)
    exp_sent, act_own = lax.optimization_barrier((exp_sent, act_own))
    exp_got = swap_col(exp_sent)
    shr_total = dot_tn(act_own, e_two) + shr_got[:depth].astype(F32)
    out_total = dot_tn(att_own, e_one) + shr_got[depth:].astype(F32)
    near_step, *far_steps = distances()
    size = lax.axis_size("dp")
    shr_mine, shr_theirs = [
        jnp.concatenate([part.reshape(size, -1, HALF) for part in parts], axis=1)
        for parts in zip(halves(shr_total, 1), halves(out_total, 1))
    ]
    shr_mine, shr_theirs, dh_own = lax.optimization_barrier(
        (shr_mine, shr_theirs.astype(B16), dh_own)
    )
    shr_got = swap_row(shr_theirs)
    exp_total = dot_tn(second, dh_own) + exp_got.astype(F32)
    d_attended, exp_total = lax.optimization_barrier((d_attended, exp_total))
    exp_kept, exp_sent = pick(exp_total.reshape(2, HALF, -1), x_place(), 1)
    exp_got = swap_dp(exp_sent.astype(B16), near_step)

    dqkv_own, dqkv_oth, sums_early = call_backward(qkv, d_attended)
    dqkv_own, dqkv_oth, shr_got, exp_got = lax.optimization_barrier(
        (dqkv_own, dqkv_oth, shr_got, exp_got)
    )
    att_got = swap_col(dot_tn(first, dqkv_oth).astype(B16)).astype(F32)
    exp_part = exp_kept + exp_got.astype(F32)
    shr_kept, shr_sent = pick(shr_mine + shr_got.astype(F32), x_place())
    exp_got = swap_row(exp_part[1].astype(B16))
    shr_got = swap_dp(shr_sent.astype(B16), near_step)
    att_total = dot_tn(first, dqkv_own) + att_got
    grad_own, grad_oth, mod_early = call_project(
        tok, mods, dqkv_own, dqkv_oth, d_middle, attend_pieces
    )
    att_total, exp_got, shr_got, mod_early, cond_all = lax.optimization_barrier(
        (att_total, exp_got, shr_got, mod_early, cond_all)
    )
    cond_all = gather_near(cond_all)
    att_mine, att_theirs = halves(att_total, 0)
    att_part = att_mine + swap_row(att_theirs.astype(B16)).astype(F32)
    exp_part = exp_part[0] + exp_got.astype(F32)
    exp_part = exp_part.reshape(size // 2, HALF // size, -1)
    grid_part = jnp.concatenate(
        [shr_kept + shr_got.astype(F32)]
        + [exp_part[:, :, at : at + HALF] for at in range(0, exp_part.shape[2], HALF)],
        axis=1,
    )
    grid_part = scatter_stage(grid_part, far_steps[0])

    sums_late = jnp.sum(sums_late, axis=(0, 1))
    sums_early = jnp.sum(sums_early, axis=(0, 1)).reshape(6, HALF)
    row_sums = sums_late[: 2 * D].reshape(2, 2, HALF)
    wide = sums_late[2 * D :].reshape(2, -1, HALF)
    col_sums = jnp.concatenate(
        [sums_early[0:3:2], wide[0], sums_early[3:6:2], wide[1]], axis=0
    )
    sums_sent = jnp.concatenate([row_sums[:, 1], col_sums], axis=0)
    sums_kept = jnp.concatenate([row_sums[:, 0], col_sums], axis=0)
    d_modulation = jnp.concatenate([mod_early, mod_late], axis=1).astype(B16).astype(F32)
    mine = d_modulation[:, :, :HALF].reshape(-1, HALF)
    theirs = d_modulation[:, :, HALF:].reshape(-1, HALF)
    got = swap_row(jnp.concatenate([theirs, sums_sent], axis=0))
    rows = mine.shape[0]
    block = in_order(row, mine, got[:rows]).astype(B16)
    sums = sums_kept + got[rows:]
    high = sums.astype(B16)
    low = (sums - high.astype(F32)).astype(B16)
    width = block.shape[0] + 2 * sums.shape[0]
    packed = jnp.concatenate([block, high, low], axis=0)[None]
    att_part, grid_part, packed, res_oth, cond_all = lax.optimization_barrier(
        (att_part, grid_part, packed, res_oth, cond_all)
    )


    res_got = swap_row(res_oth)
    att_part = scatter_stage(att_part.reshape(size, HALF // size, -1), near_step)
    for distance in far_steps[1:]:
        grid_part = scatter_stage(grid_part, distance)
    packed_all = gather_far(packed)
    att_part, near_one, packed_all, grad_oth = lax.optimization_barrier(
        (att_part, grid_part.astype(B16), packed_all, grad_oth)
    )

    grad_got = swap_row(grad_oth)
    for distance in reversed(far_steps[1:]):
        near_one = jnp.concatenate([near_one, swap_dp(near_one, distance)], axis=0)
    for places in far_groups():
        att_part = scatter_group(att_part, places)
    packed_all = gather_near(packed_all)
    att_near, near_one, packed_all = lax.optimization_barrier(
        (att_part.astype(B16), near_one, packed_all)
    )

    near_two = swap_dp(near_one, far_steps[0])
    far_one = swap_dp(near_one, near_step)
    att_near = gather_far(att_near)
    att_near, near_two = lax.optimization_barrier((att_near, near_two))

    far_two = swap_dp(near_two, near_step)
    att_far = swap_dp(att_near, near_step)
    result = in_order(row, res_own, res_got)
    input_gradient = in_order(row, grad_own, grad_got)
    exp_width = expand.shape[1]
    shrink_grad, outproj_grad, expand_grad = order(
        order_grid_kernel,
        sum_place(),
        (near_one, near_two, far_one, far_two),
        [(size, depth // size, HALF), (size, HALF // size, HALF), (size, HALF // size, exp_width)],
    )
    shrink_grad, outproj_grad = [part.reshape(-1, HALF) for part in (shrink_grad, outproj_grad)]
    expand_grad = expand_grad.reshape(HALF, exp_width)
    att_far, shrink_grad = lax.optimization_barrier((att_far, shrink_grad))
    (attend_grad,) = order(
        order_attend_kernel,
        sum_place(),
        (att_near, att_far),
        [(3, size, HALF // size, HALF)],
    )
    attend_grad = attend_grad.reshape(3, HALF, HALF)
    block_all = packed_all[:, : block.shape[0]].reshape(-1, HALF)
    both_sums = jnp.sum(packed_all[:, block.shape[0] :].astype(F32), axis=0)
    sums = both_sums[: sums.shape[0]] + both_sums[sums.shape[0] :]
    count = col_sums.shape[0] // 2
    given = jnp.concatenate([sums[:2], sums[2 + count :]], axis=0)
    high = given.astype(B16)
    low = (given - high.astype(F32)).astype(B16)
    got = swap_col(jnp.concatenate([block_all, high, low], axis=0))
    other_all = got[: block_all.shape[0]]
    got = got[block_all.shape[0] :].astype(F32)
    sums = sums[: 2 + count] + got[: 2 + count] + got[2 + count :]
    outbias_grad, shrbias_grad = sums[0], sums[1]
    attbias_grad = sums[2:4]
    expbias_grad = sums[4:].reshape(-1)

    mod_all = jnp.concatenate([block_all, other_all], axis=0).reshape(-1, 6, HALF)
    cond_mine, cond_theirs = pick(
        cond_all.reshape(-1, 2 * group, HALF).transpose(1, 0, 2), col
    )
    cond_all = jnp.concatenate(
        [part.transpose(1, 0, 2).reshape(-1, HALF) for part in (cond_mine, cond_theirs)], axis=0
    )
    adabias_grad = jnp.sum(mod_all, axis=0, dtype=F32)
    adaptive_grad = call_adaptive(cond_all, mod_all.transpose(1, 0, 2))
    mod_group = in_order(col, block, other_all[: block.shape[0]]).reshape(-1, 6, HALF)
    d_act = jnp.einsum("lke,kde->ld", mod_group, adaptive, preferred_element_type=F32)
    d_act = d_act + swap_row(d_act)
    condition_gradient = jax.vjp(jax.nn.silu, raw_condition)[1](d_act)[0].astype(B16)
    return (
        result, input_gradient, condition_gradient, adaptive_grad, adabias_grad, attend_grad,
        attbias_grad, outproj_grad, outbias_grad, expand_grad, expbias_grad, shrink_grad,
        shrbias_grad,
    )


def solution(mesh):
    placed = (
        P(("dp", "col"), "row"),
        P("dp", "col"),
        P(None, "col", "row"),
        P(None, "row"),
        P(None, "row", "col"),
        P(None, "col"),
        P("col", "row"),
        P("row"),
        P("row", "col"),
        P("col"),
        P("col", "row"),
        P("row"),
        P(("dp", "col"), "row"),
    )
    return jax.shard_map(
        shards,
        mesh=mesh,
        in_specs=placed,
        out_specs=(
            P(("dp", "col"), "row"),
            P(("dp", "col"), "row"),
            P("dp", "col"),
            P(None, "col", "row"),
            P(None, "row"),
            P(None, "row", "col"),
            P(None, "col"),
            P("col", "row"),
            P("row"),
            P("row", "col"),
            P("col"),
            P("col", "row"),
            P("row"),
        ),
        check_vma=False,
    )
```

```python
import functools

import jax
import jax.numpy as jnp
from jax import lax
from jax.experimental import pallas as pl
from jax.experimental.pallas import tpu as pltpu
from jax.sharding import PartitionSpec as P

D = 768
HALF = D // 2
FF = 3072
SEQ = 256
HEAD_DIM = 64
PAIR = 2 * HEAD_DIM
SIDE = 3 * HALF
EPS = 1e-06
F32 = jnp.float32
B16 = jnp.bfloat16
SWAP = ((0, 1), (1, 0))
SCALE = HEAD_DIM ** (-0.5)
ROOT = (2.0 / 3.141592653589793) ** 0.5
CUBE = 0.044715
PER_TILE = 2
VMEM_BYTES = 60 * 1024 * 1024


def dot(left, right):
    return jnp.dot(left, right, preferred_element_type=F32)


def dot_nt(left, right):
    return lax.dot_general(left, right, (((1,), (1,)), ((), ())), preferred_element_type=F32)


def dot_tn(left, right):
    return lax.dot_general(left, right, (((0,), (0,)), ((), ())), preferred_element_type=F32)


def normalize(values):
    center = jnp.mean(values, axis=1, keepdims=True)
    spread = jnp.mean(values * values, axis=1, keepdims=True) - center * center
    inverse = lax.rsqrt(spread + EPS)
    return (values - center) * inverse, inverse


def norm_grad(upstream, normal, inverse):
    first_mean = jnp.mean(upstream, axis=1, keepdims=True)
    second_mean = jnp.mean(upstream * normal, axis=1, keepdims=True)
    return inverse * (upstream - first_mean - normal * second_mean)


def both(own_ref, oth_ref):
    return jnp.concatenate([own_ref[...], oth_ref[...]], axis=1).astype(F32)


def line(ref, lead, number):
    return ref[lead, number : number + 1, :]


def spread_rows(mods, number, per_tile, start=0):
    own, oth = mods
    rows = []
    for latent in range(per_tile):
        at = pl.ds((pl.program_id(0) + start) * per_tile + latent, 1)
        pair = jnp.concatenate([own[number, at, :], oth[number, at, :]], axis=1)
        rows.append(jnp.broadcast_to(pair, (SEQ, D)))
    return rows[0] if per_tile == 1 else jnp.concatenate(rows, axis=0)


def store_sums(out_ref, number, values):
    for latent in range(out_ref.shape[0]):
        out_ref[latent, number : number + 1, :] = jnp.sum(
            values[latent * SEQ : (latent + 1) * SEQ], axis=0, keepdims=True
        )


def attend_copies(pieces, weight, sem):
    copies = []
    for number, piece in enumerate(pieces):
        row, col = number % 2, number // 2
        for kind in range(3):
            copies.append(
                pltpu.make_async_copy(
                    piece.at[kind],
                    weight.at[pl.ds(row * HALF, HALF), pl.ds(col * SIDE + kind * HALF, HALF)],
                    sem.at[len(copies)],
                )
            )
    return copies


def grid_copies(pieces, weight, sem):
    copies = []
    for number, piece in enumerate(pieces):
        row, col = number % 2, number // 2
        across, down = piece.shape[1], piece.shape[0]
        copies.append(
            pltpu.make_async_copy(
                piece,
                weight.at[pl.ds(col * down, down), pl.ds(row * across, across)],
                sem.at[number],
            )
        )
    return copies


def relay_copies(place, pieces, weight, sem, first_is_row):
    copies = []
    for col in range(2):
        whole, near, far = pieces[3 * col : 3 * col + 3]
        down, across = whole.shape
        size = near.shape[0]
        for piece, row, start in (
            (whole, 0, 0),
            (near, 1, place * size),
            (far, 1, (1 - place) * size),
        ):
            top, left = (row, col) if first_is_row else (col, row)
            rows = pl.ds(pl.multiple_of(top * down + start, 16), piece.shape[0])
            copies.append(
                pltpu.make_async_copy(
                    piece, weight.at[rows, pl.ds(left * across, across)], sem.at[len(copies)]
                )
            )
    return copies


def forward_kernel(
    start, tok_own, tok_oth, mod_own, mod_oth, col_own, col_oth, w0, w1, w2, w3, *others
):
    first_ref, qkv_ref, att_ref, weight, sem = others[-5:]
    rows = functools.partial(spread_rows, (mod_own, mod_oth), per_tile=1, start=start)

    @pl.when(pl.program_id(0) == 0)
    def _():
        copies = attend_copies((w0, w1, w2, w3), weight, sem)
        for copy in copies:
            copy.start()
        for copy in copies:
            copy.wait()

    normal, _ = normalize(both(tok_own, tok_oth))
    first = (normal * (1.0 + rows(1)) + rows(0)).astype(B16)
    first_ref[...] = first
    blank = jnp.zeros((1, HALF), F32)
    last = col_oth.shape[0] - 1
    bias = jnp.concatenate(
        [line(col_own, 0, 0), blank, line(col_own, 0, 1)]
        + [line(col_oth, last, 0), blank, line(col_oth, last, 1)],
        axis=1,
    )
    qkv_ref[...] = (dot(first, weight[...]) + bias).astype(B16)
    low = lax.broadcasted_iota(jnp.int32, (SEQ, PAIR), 1) < HEAD_DIM
    for col in range(2):
        for pair in range(HALF // PAIR):
            base = col * SIDE + pair * PAIR
            q_part = qkv_ref[:, base : base + PAIR] * SCALE
            k_part = qkv_ref[:, base + HALF : base + HALF + PAIR]
            v_part = qkv_ref[:, base + D : base + D + PAIR]
            outs = []
            for keep in (low, jnp.logical_not(low)):
                scores = dot_nt(jnp.where(keep, q_part, 0).astype(B16), k_part)
                exponent = jnp.exp(scores - jnp.max(scores, axis=1, keepdims=True))
                probs = exponent * (1.0 / jnp.sum(exponent, axis=1, keepdims=True))
                outs.append(dot(probs.astype(B16), v_part))
            at = col * HALF + pair * PAIR
            att_ref[:, at : at + PAIR] = jnp.where(low, outs[0], outs[1]).astype(B16)


def middle_kernel(
    place, tok_own, tok_oth, cot_own, cot_oth, att, mod_own, mod_oth, col_own, col_oth, row_own,
    o0, o1, o2, o3, x0, x1, x2, x3, x4, x5, s0, s1, s2, s3, s4, s5,
    res_own, res_oth, second_ref, act_own, act_oth, dh_own, dh_oth, e_one_ref, e_two_ref,
    d_mid_ref, d_att_ref, mod_ref, sum_ref,
    w_out, w_exp, w_shr, sem_out, sem_exp, sem_shr,
):
    @pl.when(pl.program_id(0) == 0)
    def _():
        copies = (
            grid_copies((o0, o1, o2, o3), w_out, sem_out)
            + relay_copies(place[0], (x0, x1, x2, x3, x4, x5), w_exp, sem_exp, True)
            + relay_copies(place[0], (s0, s1, s2, s3, s4, s5), w_shr, sem_shr, False)
        )
        for copy in copies:
            copy.start()
        for copy in copies:
            copy.wait()

    per_tile = mod_ref.shape[0]
    last = mod_oth.shape[0] - 1
    rows = functools.partial(spread_rows, (mod_own, mod_oth), per_tile=per_tile)
    outbias = jnp.concatenate([line(row_own, 0, 0), line(mod_oth, last, 0)], axis=1)
    shrbias = jnp.concatenate([line(row_own, 0, 1), line(mod_oth, last, 1)], axis=1)

    branch_one = dot(att[...], w_out[...]) + outbias
    middle = both(tok_own, tok_oth) + rows(2) * branch_one
    normal, inverse = normalize(middle)
    second = (normal * (1.0 + rows(4)) + rows(3)).astype(B16)
    second_ref[...] = second
    upstream = both(cot_own, cot_oth)
    e_two = (rows(5) * upstream).astype(B16)
    e_two_ref[...] = e_two
    branch_two = shrbias
    d_second = 0.0
    for part in range(FF // D):
        at = part * D
        owner, lead = (col_own, 0) if 2 * at < FF else (col_oth, col_oth.shape[0] - 1)
        number = 2 + 2 * (part % (FF // D // 2))
        expbias = jnp.concatenate(
            [line(owner, lead, number), line(owner, lead, number + 1)], axis=1
        )
        hidden = dot(second, w_exp[:, at : at + D]) + expbias
        square = hidden * hidden
        bend = jnp.tanh(hidden * (ROOT + (ROOT * CUBE) * square))
        share = 0.5 + 0.5 * bend
        active = (hidden * share).astype(B16)
        slope = share + (0.5 * hidden) * (1.0 - bend * bend) * (ROOT + (3.0 * ROOT * CUBE) * square)
        branch_two = branch_two + dot(active, w_shr[at : at + D, :])
        d_hidden = (dot_nt(e_two, w_shr[at : at + D, :]) * slope).astype(B16)
        d_second = d_second + dot_nt(d_hidden, w_exp[:, at : at + D])
        act_ref, dh_ref = (act_own, dh_own) if 2 * at < FF else (act_oth, dh_oth)
        into = at % (FF // 2)
        act_ref[:, into : into + D] = active
        dh_ref[:, into : into + D] = d_hidden
        sum_ref[0, :, 2 * D + at : 2 * D + at + D] = jnp.sum(
            d_hidden.astype(F32), axis=0, keepdims=True
        )
    result = (middle + rows(5) * branch_two).astype(B16)
    res_own[...] = result[:, :HALF]
    res_oth[...] = result[:, HALF:]
    store_sums(mod_ref, 3, upstream * branch_two)
    store_sums(mod_ref, 1, d_second)
    store_sums(mod_ref, 2, d_second * normal)
    d_middle = upstream + norm_grad(d_second * (1.0 + rows(4)), normal, inverse)
    d_mid_ref[...] = d_middle
    store_sums(mod_ref, 0, d_middle * branch_one)
    e_one = (rows(2) * d_middle).astype(B16)
    e_one_ref[...] = e_one
    d_att_ref[...] = dot_nt(e_one, w_out[...]).astype(B16)
    sum_ref[0, :, :D] = jnp.sum(e_one.astype(F32), axis=0, keepdims=True)
    sum_ref[0, :, D : 2 * D] = jnp.sum(e_two.astype(F32), axis=0, keepdims=True)


def backward_kernel(qkv, d_att, dqkv_own, dqkv_oth, sum_ref):
    low = lax.broadcasted_iota(jnp.int32, (SEQ, PAIR), 1) < HEAD_DIM
    for col in range(2):
        out_ref = (dqkv_own, dqkv_oth)[col]
        for pair in range(HALF // PAIR):
            base = col * SIDE + pair * PAIR
            q_part = qkv[:, base : base + PAIR]
            k_part = qkv[:, base + HALF : base + HALF + PAIR]
            v_part = qkv[:, base + D : base + D + PAIR]
            d_part = d_att[:, col * HALF + pair * PAIR : col * HALF + (pair + 1) * PAIR]
            queries, keys, values = [], [], []
            for keep in (low, jnp.logical_not(low)):
                scores = dot_nt(jnp.where(keep, k_part * SCALE, 0).astype(B16), q_part)
                exponent = jnp.exp(scores - jnp.max(scores, axis=0, keepdims=True))
                probs = exponent * (1.0 / jnp.sum(exponent, axis=0, keepdims=True))
                d_probs = dot_nt(jnp.where(keep, v_part, 0).astype(B16), d_part)
                weighted = probs * d_probs
                d_scores = (weighted - probs * jnp.sum(weighted, axis=0, keepdims=True)).astype(B16)
                values.append(dot(probs.astype(B16), d_part))
                keys.append(dot(d_scores, q_part))
                queries.append(dot_tn(d_scores, k_part))
            for kind, (first, then, factor) in enumerate(
                ((*queries, SCALE), (*keys, SCALE), (*values, 1.0))
            ):
                at = kind * HALF + pair * PAIR
                piece = (jnp.where(low, first, then) * factor).astype(B16)
                out_ref[:, at : at + PAIR] = piece
                sum_ref[0, :, col * SIDE + at : col * SIDE + at + PAIR] = jnp.sum(
                    piece.astype(F32), axis=0, keepdims=True
                )


def project_kernel(
    tok_own, tok_oth, mod_own, mod_oth, dqkv_own, dqkv_oth, d_mid, w0, w1, w2, w3,
    grad_own, grad_oth, mod_ref, weight, sem,
):
    @pl.when(pl.program_id(0) == 0)
    def _():
        copies = attend_copies((w0, w1, w2, w3), weight, sem)
        for copy in copies:
            copy.start()
        for copy in copies:
            copy.wait()

    d_first = dot_nt(dqkv_own[...], weight[:, :SIDE]) + dot_nt(dqkv_oth[...], weight[:, SIDE:])
    normal, inverse = normalize(both(tok_own, tok_oth))
    store_sums(mod_ref, 0, d_first)
    store_sums(mod_ref, 1, d_first * normal)
    grad = (
        d_mid[...] + norm_grad(d_first * (1.0 + spread_rows((mod_own, mod_oth), 1, 1)), normal, inverse)
    ).astype(B16)
    grad_own[...] = grad[:, :HALF]
    grad_oth[...] = grad[:, HALF:]


def adaptive_kernel(cond, mods, out_ref):
    out_ref[0] = dot_tn(cond[...], mods[0])


def tiles(rows, width):
    return pl.BlockSpec((rows, width), lambda step: (step, 0))


def stacked(count, rows, width):
    return pl.BlockSpec((count, rows, width), lambda step: (step, 0, 0))


def fixed(values):
    return pl.BlockSpec(values.shape, lambda step: (0,) * values.ndim)


def anywhere(count):
    return [pl.BlockSpec(memory_space=pl.ANY)] * count


def params():
    return pltpu.CompilerParams(
        vmem_limit_bytes=VMEM_BYTES, dimension_semantics=("arbitrary",)
    )


def call_forward(tok_own, tok_oth, vectors, pieces, start, steps, before=()):
    count = tok_own.shape[0]

    def part(width):
        return pl.BlockSpec((SEQ, width), lambda step: (step + start, 0))

    inputs = (tok_own, tok_oth, *vectors, *pieces)
    return pl.pallas_call(
        functools.partial(forward_kernel, start),
        grid=(steps,),
        in_specs=[part(HALF)] * 2
        + [fixed(values) for values in vectors]
        + anywhere(4 + len(before)),
        out_specs=[part(D), part(2 * SIDE), part(D)],
        out_shape=[
            jax.ShapeDtypeStruct((count, D), B16),
            jax.ShapeDtypeStruct((count, 2 * SIDE), B16),
            jax.ShapeDtypeStruct((count, D), B16),
        ],
        input_output_aliases={len(inputs) + number: number for number in range(len(before))},
        scratch_shapes=[pltpu.VMEM((D, 2 * SIDE), B16), pltpu.SemaphoreType.DMA((12,))],
        compiler_params=params(),
        cost_estimate=pl.CostEstimate(
            flops=14 * 10**9 * steps // 4,
            bytes_accessed=16 * 10**6 * steps // 4,
            transcendentals=steps * SEQ * SEQ * 12,
        ),
        name="forward",
    )(*inputs, *before)


def call_middle(place, tok, cot, att, vectors, out_pieces, exp_pieces, shr_pieces):
    count = att.shape[0]
    latents = count // SEQ
    per_tile = PER_TILE if latents % PER_TILE == 0 else 1
    rows = per_tile * SEQ
    steps = latents // per_tile
    halves = [tiles(rows, HALF)] * 2

    def shape(width, kind=B16):
        return jax.ShapeDtypeStruct((count, width), kind)

    return pl.pallas_call(
        middle_kernel,
        grid=(steps,),
        in_specs=[pl.BlockSpec(memory_space=pltpu.SMEM)]
        + halves
        + halves
        + [tiles(rows, D)]
        + [fixed(values) for values in vectors]
        + anywhere(16),
        out_specs=halves
        + [tiles(rows, D)]
        + [tiles(rows, FF // 2)] * 4
        + [tiles(rows, D)] * 4
        + [stacked(per_tile, 4, D), stacked(1, 1, 2 * D + FF)],
        out_shape=[shape(HALF), shape(HALF), shape(D)]
        + [shape(FF // 2)] * 4
        + [shape(D), shape(D), shape(D, F32), shape(D)]
        + [
            jax.ShapeDtypeStruct((latents, 4, D), F32),
            jax.ShapeDtypeStruct((steps, 1, 2 * D + FF), F32),
        ],
        scratch_shapes=[
            pltpu.VMEM((D, D), B16),
            pltpu.VMEM((D, FF), B16),
            pltpu.VMEM((FF, D), B16),
            pltpu.SemaphoreType.DMA((4,)),
            pltpu.SemaphoreType.DMA((6,)),
            pltpu.SemaphoreType.DMA((6,)),
        ],
        compiler_params=params(),
        cost_estimate=pl.CostEstimate(
            flops=30 * 10**9, bytes_accessed=50 * 10**6, transcendentals=count * FF
        ),
        name="middle",
    )(place, *tok, *cot, att, *vectors, *out_pieces, *exp_pieces, *shr_pieces)


def call_backward(qkv, d_att):
    count = d_att.shape[0]
    latents = count // SEQ
    return pl.pallas_call(
        backward_kernel,
        grid=(latents,),
        in_specs=[tiles(SEQ, 2 * SIDE), tiles(SEQ, D)],
        out_specs=[tiles(SEQ, SIDE)] * 2 + [stacked(1, 1, 2 * SIDE)],
        out_shape=[jax.ShapeDtypeStruct((count, SIDE), B16)] * 2
        + [jax.ShapeDtypeStruct((latents, 1, 2 * SIDE), F32)],
        compiler_params=params(),
        cost_estimate=pl.CostEstimate(
            flops=10**9, bytes_accessed=10**6, transcendentals=0
        ),
        name="backward",
    )(qkv, d_att)


def call_project(tok, vectors, dqkv_own, dqkv_oth, d_mid, pieces):
    count = d_mid.shape[0]
    latents = count // SEQ
    return pl.pallas_call(
        project_kernel,
        grid=(latents,),
        in_specs=[tiles(SEQ, HALF)] * 2
        + [fixed(values) for values in vectors]
        + [tiles(SEQ, SIDE)] * 2
        + [tiles(SEQ, D)]
        + anywhere(4),
        out_specs=[tiles(SEQ, HALF)] * 2 + [stacked(1, 2, D)],
        out_shape=[jax.ShapeDtypeStruct((count, HALF), B16)] * 2
        + [jax.ShapeDtypeStruct((latents, 2, D), F32)],
        scratch_shapes=[pltpu.VMEM((D, 2 * SIDE), B16), pltpu.SemaphoreType.DMA((12,))],
        compiler_params=params(),
        cost_estimate=pl.CostEstimate(
            flops=7 * 10**9, bytes_accessed=16 * 10**6, transcendentals=count
        ),
        name="project",
    )(*tok, *vectors, dqkv_own, dqkv_oth, d_mid, *pieces)


def call_adaptive(cond, mods):
    latents, width = cond.shape
    kinds = mods.shape[0]
    return pl.pallas_call(
        adaptive_kernel,
        grid=(kinds,),
        in_specs=[
            pl.BlockSpec((latents, width), lambda step: (0, 0)),
            stacked(1, latents, HALF),
        ],
        out_specs=stacked(1, width, HALF),
        out_shape=jax.ShapeDtypeStruct((kinds, width, HALF), F32),
        compiler_params=params(),
        name="adaptive",
    )(cond, mods)


def swap_row(values):
    return lax.ppermute(values, "row", SWAP)


def swap_col(values):
    return lax.ppermute(values, "col", SWAP)


def swap_dp(values, distance):
    size = lax.axis_size("dp")
    return lax.ppermute(values, "dp", [(place, place ^ distance) for place in range(size)])


def distances():
    size = lax.axis_size("dp")
    return [1 << bit for bit in range(size.bit_length() - 1)]


def after(values, *earlier):
    return lax.optimization_barrier((values,) + earlier)[0]


def halves(values, dim):
    size = values.shape[dim] // 2
    return lax.slice_in_dim(values, 0, size, axis=dim), lax.slice_in_dim(
        values, size, 2 * size, axis=dim
    )


def pick(values, place, axis=0):
    size = values.shape[axis] // 2
    kept = lax.dynamic_slice_in_dim(values, place * size, size, axis)
    sent = lax.dynamic_slice_in_dim(values, (1 - place) * size, size, axis)
    return kept, sent


def in_order(place, mine, theirs):
    return jnp.concatenate(
        [jnp.where(place == 0, mine, theirs), jnp.where(place == 0, theirs, mine)], axis=0
    )


def x_place():
    return lax.axis_index("dp") % 2


def scatter_stage(values, distance, axis=0):
    place = (lax.axis_index("dp") // distance) % 2
    size = values.shape[axis] // 2
    kept = lax.dynamic_slice_in_dim(values, place * size, size, axis)
    sent = lax.dynamic_slice_in_dim(values, (1 - place) * size, size, axis)
    return kept + swap_dp(sent.astype(B16), distance).astype(F32)


def far_groups():
    far = distances()[1:]
    return [far[at : at + 2] for at in range(0, len(far), 2)]


def around(group):
    if len(group) == 1:
        return [group[0]]
    return [group[1], group[0], group[0] + group[1]]


def scatter_group(values, group):
    me = lax.axis_index("dp")
    place = 0
    for distance in group:
        place = 2 * place + (me // distance) % 2
    size = values.shape[0] >> len(group)
    total = lax.dynamic_slice_in_dim(values, place * size, size, 0)
    for block, distance in enumerate(around(group), 1):
        sent = lax.dynamic_slice_in_dim(values, (place ^ block) * size, size, 0)
        total = total + swap_dp(sent.astype(B16), distance).astype(F32)
    return total


def gather_group(values, group):
    return jnp.concatenate(
        [values] + [swap_dp(values, distance) for distance in around(group)], axis=0
    )


def gather_far(values):
    for group in reversed(far_groups()):
        values = gather_group(values, group)
    return values


def gather_near(values):
    return jnp.concatenate([values, swap_dp(values, 1)], axis=0)


def near_place():
    return jnp.full((1,), x_place(), jnp.int32)


def sum_place():
    me, mine = lax.axis_index("dp"), 0
    for distance in distances():
        mine = mine * 2 + (me // distance) % 2
    return jnp.full((1,), mine, jnp.int32)


def order_grid_kernel(mine, p0, p1, p2, p3, shr_out, out_out, exp_out):
    shr_rows, out_rows, exp_rows = shr_out.shape[1], out_out.shape[1], exp_out.shape[1]
    index = 0
    for values in (p0, p1, p2, p3):
        for block in range(values.shape[0]):
            into = mine[0] ^ index
            index += 1
            shr_out[into] = values[block, :shr_rows].astype(F32)
            out_out[into] = values[block, shr_rows : shr_rows + out_rows].astype(F32)
            for part in range(exp_out.shape[2] // HALF):
                at = shr_rows + out_rows + part * exp_rows
                exp_out[into, :, part * HALF : (part + 1) * HALF] = values[
                    block, at : at + exp_rows
                ].astype(F32)


def order_attend_kernel(mine, near, far, out):
    count = near.shape[0]
    for number, values in enumerate((near, far)):
        for block in range(count):
            place = mine[0] ^ (number * count + block)
            for kind in range(out.shape[0]):
                out[kind, place] = values[block, :, kind * HALF : (kind + 1) * HALF].astype(F32)


def order(kernel, place, values, shapes):
    whole = [pl.BlockSpec(memory_space=pltpu.VMEM)]
    return pl.pallas_call(
        kernel,
        in_specs=[pl.BlockSpec(memory_space=pltpu.SMEM)] + whole * len(values),
        out_specs=whole * len(shapes),
        out_shape=[jax.ShapeDtypeStruct(shape, F32) for shape in shapes],
        compiler_params=pltpu.CompilerParams(vmem_limit_bytes=VMEM_BYTES),
        name="order",
    )(place, *values)


def shards(
    tokens, condition, adaptive, adabias, attend, attbias, outproj, outbias,
    expand, expbias, shrink, shrbias, cotangent,
):
    row = lax.axis_index("row")
    col = lax.axis_index("col")

    tok_own, sent = pick(tokens, row)
    tok_oth = swap_row(sent)
    tok = (tok_own, tok_oth)

    raw_condition = after(condition, sent).astype(F32)
    act_cond = jax.nn.silu(raw_condition).astype(B16)
    mod_terms = jnp.einsum("ld,kde->kle", act_cond, adaptive, preferred_element_type=F32)
    kept, sent = pick(mod_terms, col, 1)
    group = kept.shape[1]
    latents = group // 2
    col_own = jnp.concatenate([attbias, expbias.reshape(-1, HALF)], axis=0).astype(F32)
    col_own = jnp.pad(col_own, ((0, group - col_own.shape[0]), (0, 0)))[None]
    col_oth = swap_col(jnp.concatenate([sent, col_own], axis=0))
    mod_rows = kept + col_oth[:6] + adabias.astype(F32)[:, None]
    mod_own, sent = pick(mod_rows, row, 1)
    row_own = jnp.stack([outbias, shrbias]).astype(F32)
    row_own = jnp.pad(row_own, ((0, latents - 2), (0, 0)))[None]
    mod_oth = swap_row(jnp.concatenate([sent, row_own], axis=0))
    mods = (mod_own, mod_oth)

    def pieces(values, over):
        return values, over, swap_col(values), swap_col(over)

    def near(values):
        return pick(values, x_place())[0]

    cot_own, cot_sent = pick(cotangent, row)
    attend, _, _, exp_near, shr_near, cot_sent, act_cond = lax.optimization_barrier(
        (attend, tok_oth, mod_oth, near(expand), near(shrink), cot_sent, act_cond)
    )
    attend_over, cond_all = lax.optimization_barrier((swap_row(attend), gather_far(act_cond)))
    attend_pieces = pieces(attend, attend_over)
    *attend_pieces, exp_near, shr_near, outproj = lax.optimization_barrier(
        (*attend_pieces, exp_near, shr_near, outproj)
    )
    exp_near, out_over = swap_row(exp_near), swap_row(outproj)
    vectors = (*mods, col_own, col_oth)
    half = latents // 2
    *begun, exp_near, shr_near, cot_sent, out_over = lax.optimization_barrier(
        (
            *call_forward(tok_own, tok_oth, vectors, attend_pieces, 0, half),
            exp_near, shr_near, cot_sent, out_over,
        )
    )
    shr_near, exp_far = swap_row(shr_near), swap_dp(exp_near, 1)
    cot_oth = swap_row(cot_sent)
    first, qkv, attended = call_forward(
        tok_own, tok_oth, vectors, attend_pieces, half, latents - half, begun
    )
    attended, exp_far, shr_near = lax.optimization_barrier((attended, exp_far, shr_near))
    shr_far = swap_dp(shr_near, 1)
    early = [swap_col(values) for values in (expand, shrink, exp_near, shr_near)]
    cot_oth, out_over, exp_far, shr_far, *early = lax.optimization_barrier(
        (cot_oth, out_over, exp_far, shr_far, *early)
    )
    exp_pieces = (expand, exp_near, exp_far, early[0], early[2], swap_col(exp_far))
    shr_pieces = (shrink, shr_near, shr_far, early[1], early[3], swap_col(shr_far))
    out_pieces = pieces(outproj, out_over)
    (
        res_own, res_oth, second, act_own, act_oth, dh_own, dh_oth, e_one, e_two,
        d_middle, d_attended, mod_late, sums_late,
    ) = call_middle(
        near_place(), tok, (cot_own, cot_oth), attended, (*mods, col_own, col_oth, row_own),
        out_pieces, exp_pieces, shr_pieces,
    )
    att_own, att_oth = halves(attended, 1)
    depth = act_oth.shape[1]
    shr_sent = jnp.concatenate(
        [dot_tn(act_oth, e_two).astype(B16), dot_tn(att_oth, e_one).astype(B16)], axis=0
    )
    shr_sent, dh_oth = lax.optimization_barrier((shr_sent, dh_oth))
    shr_got = swap_col(shr_sent)
    exp_sent = dot_tn(second, dh_oth).astype(B16)
    exp_sent, act_own = lax.optimization_barrier((exp_sent, act_own))
    exp_got = swap_col(exp_sent)
    shr_total = dot_tn(act_own, e_two) + shr_got[:depth].astype(F32)
    out_total = dot_tn(att_own, e_one) + shr_got[depth:].astype(F32)
    near_step, *far_steps = distances()
    size = lax.axis_size("dp")
    shr_mine, shr_theirs = [
        jnp.concatenate([part.reshape(size, -1, HALF) for part in parts], axis=1)
        for parts in zip(halves(shr_total, 1), halves(out_total, 1))
    ]
    shr_mine, shr_theirs, dh_own = lax.optimization_barrier(
        (shr_mine, shr_theirs.astype(B16), dh_own)
    )
    shr_got = swap_row(shr_theirs)
    exp_total = dot_tn(second, dh_own) + exp_got.astype(F32)
    d_attended, exp_total = lax.optimization_barrier((d_attended, exp_total))
    exp_kept, exp_sent = pick(exp_total.reshape(2, HALF, -1), x_place(), 1)
    exp_got = swap_dp(exp_sent.astype(B16), near_step)

    dqkv_own, dqkv_oth, sums_early = call_backward(qkv, d_attended)
    dqkv_own, dqkv_oth, shr_got, exp_got = lax.optimization_barrier(
        (dqkv_own, dqkv_oth, shr_got, exp_got)
    )
    att_got = swap_col(dot_tn(first, dqkv_oth).astype(B16)).astype(F32)
    exp_part = exp_kept + exp_got.astype(F32)
    shr_kept, shr_sent = pick(shr_mine + shr_got.astype(F32), x_place())
    exp_got = swap_row(exp_part[1].astype(B16))
    shr_got = swap_dp(shr_sent.astype(B16), near_step)
    att_total = dot_tn(first, dqkv_own) + att_got
    grad_own, grad_oth, mod_early = call_project(
        tok, mods, dqkv_own, dqkv_oth, d_middle, attend_pieces
    )
    att_total, exp_got, shr_got, mod_early, cond_all = lax.optimization_barrier(
        (att_total, exp_got, shr_got, mod_early, cond_all)
    )
    cond_all = gather_near(cond_all)
    att_mine, att_theirs = halves(att_total, 0)
    att_part = att_mine + swap_row(att_theirs.astype(B16)).astype(F32)
    exp_part = exp_part[0] + exp_got.astype(F32)
    exp_part = exp_part.reshape(size // 2, HALF // size, -1)
    grid_part = jnp.concatenate(
        [shr_kept + shr_got.astype(F32)]
        + [exp_part[:, :, at : at + HALF] for at in range(0, exp_part.shape[2], HALF)],
        axis=1,
    )
    grid_part = scatter_stage(grid_part, far_steps[0])

    sums_late = jnp.sum(sums_late, axis=(0, 1))
    sums_early = jnp.sum(sums_early, axis=(0, 1)).reshape(6, HALF)
    row_sums = sums_late[: 2 * D].reshape(2, 2, HALF)
    wide = sums_late[2 * D :].reshape(2, -1, HALF)
    col_sums = jnp.concatenate(
        [sums_early[0:3:2], wide[0], sums_early[3:6:2], wide[1]], axis=0
    )
    sums_sent = jnp.concatenate([row_sums[:, 1], col_sums], axis=0)
    sums_kept = jnp.concatenate([row_sums[:, 0], col_sums], axis=0)
    d_modulation = jnp.concatenate([mod_early, mod_late], axis=1).astype(B16).astype(F32)
    mine = d_modulation[:, :, :HALF].reshape(-1, HALF)
    theirs = d_modulation[:, :, HALF:].reshape(-1, HALF)
    got = swap_row(jnp.concatenate([theirs, sums_sent], axis=0))
    rows = mine.shape[0]
    block = in_order(row, mine, got[:rows]).astype(B16)
    sums = sums_kept + got[rows:]
    high = sums.astype(B16)
    low = (sums - high.astype(F32)).astype(B16)
    width = block.shape[0] + 2 * sums.shape[0]
    packed = jnp.concatenate([block, high, low], axis=0)[None]
    att_part, grid_part, packed, res_oth, cond_all = lax.optimization_barrier(
        (att_part, grid_part, packed, res_oth, cond_all)
    )


    res_got = swap_row(res_oth)
    att_part = scatter_stage(att_part.reshape(size, HALF // size, -1), near_step)
    for distance in far_steps[1:]:
        grid_part = scatter_stage(grid_part, distance)
    packed_all = gather_far(packed)
    att_part, near_one, packed_all, grad_oth = lax.optimization_barrier(
        (att_part, grid_part.astype(B16), packed_all, grad_oth)
    )

    grad_got = swap_row(grad_oth)
    for distance in reversed(far_steps[1:]):
        near_one = jnp.concatenate([near_one, swap_dp(near_one, distance)], axis=0)
    for places in far_groups():
        att_part = scatter_group(att_part, places)
    packed_all = gather_near(packed_all)
    att_near, near_one, packed_all = lax.optimization_barrier(
        (att_part.astype(B16), near_one, packed_all)
    )

    near_two = swap_dp(near_one, far_steps[0])
    far_one = swap_dp(near_one, near_step)
    att_near = gather_far(att_near)
    att_near, near_two, packed_all = lax.optimization_barrier((att_near, near_two, packed_all))

    far_two = swap_dp(near_two, near_step)
    att_far = swap_dp(att_near, near_step)
    result = in_order(row, res_own, res_got)
    input_gradient = in_order(row, grad_own, grad_got)
    exp_width = expand.shape[1]
    shrink_grad, outproj_grad, expand_grad = order(
        order_grid_kernel,
        sum_place(),
        (near_one, near_two, far_one, far_two),
        [(size, depth // size, HALF), (size, HALF // size, HALF), (size, HALF // size, exp_width)],
    )
    shrink_grad, outproj_grad = [part.reshape(-1, HALF) for part in (shrink_grad, outproj_grad)]
    expand_grad = expand_grad.reshape(HALF, exp_width)
    att_far, shrink_grad = lax.optimization_barrier((att_far, shrink_grad))
    (attend_grad,) = order(
        order_attend_kernel,
        sum_place(),
        (att_near, att_far),
        [(3, size, HALF // size, HALF)],
    )
    attend_grad = attend_grad.reshape(3, HALF, HALF)
    block_all = packed_all[:, : block.shape[0]].reshape(-1, HALF)
    both_sums = jnp.sum(packed_all[:, block.shape[0] :].astype(F32), axis=0)
    sums = both_sums[: sums.shape[0]] + both_sums[sums.shape[0] :]
    count = col_sums.shape[0] // 2
    given = jnp.concatenate([sums[:2], sums[2 + count :]], axis=0)
    high = given.astype(B16)
    low = (given - high.astype(F32)).astype(B16)
    got = swap_col(jnp.concatenate([block_all, high, low], axis=0))
    other_all = got[: block_all.shape[0]]
    got = got[block_all.shape[0] :].astype(F32)
    sums = sums[: 2 + count] + got[: 2 + count] + got[2 + count :]
    outbias_grad, shrbias_grad = sums[0], sums[1]
    attbias_grad = sums[2:4]
    expbias_grad = sums[4:].reshape(-1)

    mod_all = jnp.concatenate([block_all, other_all], axis=0).reshape(-1, 6, HALF)
    cond_mine, cond_theirs = pick(
        cond_all.reshape(-1, 2 * group, HALF).transpose(1, 0, 2), col
    )
    cond_all = jnp.concatenate(
        [part.transpose(1, 0, 2).reshape(-1, HALF) for part in (cond_mine, cond_theirs)], axis=0
    )
    adabias_grad = jnp.sum(mod_all, axis=0, dtype=F32)
    adaptive_grad = call_adaptive(cond_all, mod_all.transpose(1, 0, 2))
    mod_group = in_order(col, block, other_all[: block.shape[0]]).reshape(-1, 6, HALF)
    d_act = jnp.einsum("lke,kde->ld", mod_group, adaptive, preferred_element_type=F32)
    d_act = d_act + swap_row(d_act)
    condition_gradient = jax.vjp(jax.nn.silu, raw_condition)[1](d_act)[0].astype(B16)
    return (
        result, input_gradient, condition_gradient, adaptive_grad, adabias_grad, attend_grad,
        attbias_grad, outproj_grad, outbias_grad, expand_grad, expbias_grad, shrink_grad,
        shrbias_grad,
    )


def solution(mesh):
    placed = (
        P(("dp", "col"), "row"),
        P("dp", "col"),
        P(None, "col", "row"),
        P(None, "row"),
        P(None, "row", "col"),
        P(None, "col"),
        P("col", "row"),
        P("row"),
        P("row", "col"),
        P("col"),
        P("col", "row"),
        P("row"),
        P(("dp", "col"), "row"),
    )
    return jax.shard_map(
        shards,
        mesh=mesh,
        in_specs=placed,
        out_specs=(
            P(("dp", "col"), "row"),
            P(("dp", "col"), "row"),
            P("dp", "col"),
            P(None, "col", "row"),
            P(None, "row"),
            P(None, "row", "col"),
            P(None, "col"),
            P("col", "row"),
            P("row"),
            P("row", "col"),
            P("col"),
            P("col", "row"),
            P("row"),
        ),
        check_vma=False,
    )
```
